512 devices in a mesh: node: 16 (over z), ingroup: 32 (over y, x, core).
Axes of the slice: x: 4, y: 4, z: 16, core: 2. Of those that a mesh axis runs over, the one named last changes fastest.
Arguments:
- tokens: bfloat16 [2048, 7168], P(('node', 'ingroup')), may hold values from -6 to 6
- cotangent: bfloat16 [2048, 7168], P(('node', 'ingroup')), may hold values from -6 to 6
- groups: int32 [2048, 2], P(('node', 'ingroup')), may hold values from 0 to 15, as said below
- choices: int32 [2048, 2, 2], P(('node', 'ingroup')), may hold values from 0 to 3, as said below
- gates: bfloat16 [2048, 2, 2], P(('node', 'ingroup')), may hold values from 0.049804688 to 1
- up_weight: bfloat16 [7168, 65536], P(None, ('node', 'ingroup')), may hold values from -0.0625 to 0.0625
- down_weight: bfloat16 [65536, 7168], P(('node', 'ingroup')), may hold values from -0.1875 to 0.1875
Outputs:
- mixed: bfloat16 [2048, 7168], P(('node', 'ingroup'))
- grad_tokens: bfloat16 [2048, 7168], P(('node', 'ingroup'))
- grad_gates: bfloat16 [2048, 2, 2], P(('node', 'ingroup'))
The draws below stay inside these ranges and needn't reach their ends.
Inputs may be any that keep to these rules, and one draw needn't show every extreme that they name: The two groups of a token differ. The tokens of one device name one group at most 1 times, and some device reaches that. Over all devices of one ingroup index, exactly 8 token-group pairs name each group; in some groups, at every ingroup index, all 8 of them name one common expert. `choices`: the two experts named within one group differ.
All inputs are finite; a program needn't handle non-finite values.
Results may differ from the reference program's by a relative error of at most 0.02.
Values may be sent and summed in bfloat16 or wider, within the bound.
No kernel may reach another device: no remote copies, remote signals or barrier semaphores. Data moves between devices by JAX's collectives and lax.ppermute only.
A program may use at most 64 MiB of HBM per device.

```python
import math
import jax
import jax.numpy as jnp
from jax import lax

D = 7168
H = 1024
EXP_NODE = 4
TOK_DEV = 4
TOKENS = 2048
EXPERTS = 64
N_NODE = 16
N_INGROUP = 32


def route_tables(key):
    key_tau, key_pi, key_rank, key_hot, key_shift = jax.random.split(key, 5)
    pair_rows = 2 * TOK_DEV
    tau = jax.vmap(lambda sub: jax.random.permutation(sub, TOK_DEV))(jax.random.split(key_tau, N_NODE * N_INGROUP)).reshape(N_NODE, N_INGROUP, TOK_DEV)
    offsets = jax.vmap(lambda sub: jax.random.permutation(sub, N_NODE))(jax.random.split(key_pi, N_INGROUP))
    ranking = jax.vmap(lambda sub: jax.random.permutation(sub, pair_rows))(jax.random.split(key_rank, N_NODE * N_INGROUP)).reshape(N_NODE, N_INGROUP, pair_rows)
    hot = jax.random.randint(key_hot, (N_NODE,), 0, EXP_NODE)
    shift = jax.random.randint(key_shift, (), 0, 2)
    shape = (N_NODE, N_INGROUP, TOK_DEV, 2)
    source = jnp.broadcast_to(jnp.arange(N_NODE, dtype=jnp.int32)[:, None, None, None], shape)
    member = jnp.broadcast_to(jnp.arange(N_INGROUP, dtype=jnp.int32)[None, :, None, None], shape)
    which = jnp.broadcast_to(jnp.arange(2, dtype=jnp.int32)[None, None, None, :], shape)
    pair_index = 2 * jnp.broadcast_to(tau[:, :, :, None], shape) + which
    target = (source + offsets[member, pair_index % N_NODE]) % N_NODE
    place = ranking[target, member, pair_index]
    hot_count = jnp.where((target + shift) % 2 == 0, pair_rows, pair_rows - 2)
    leader = hot[target]
    first = jnp.where(place < hot_count, leader, leader + 1) % EXP_NODE
    second = jnp.where(place < hot_count, leader + 1 + place % 3, leader + 2 + place % 2) % EXP_NODE
    groups = target.reshape(TOKENS, 2).astype(jnp.int32)
    choices = jnp.stack([first, second], -1).reshape(TOKENS, 2, 2).astype(jnp.int32)
    return (groups, choices)


def draw_groups(key, part):
    return route_tables(key)[0]


def draw_choices(key, part):
    return route_tables(key)[1]


def block_scale(rng, dims, cuts, smallest, high):
    def one(axis_at, shards_of):
        draws = jax.random.uniform(jax.random.fold_in(jax.random.fold_in(rng, 6), axis_at), (shards_of,), jnp.float32, smallest / len(cuts), high / len(cuts))
        return jnp.repeat(jnp.exp(draws), dims[axis_at] // shards_of).reshape((-1,) + (1,) * (len(dims) - axis_at - 1))

    factor_of = one(*cuts[0])
    for cut in cuts[1:]:
        factor_of = factor_of * one(*cut)
    return factor_of


def noise(rng, extent, deviation, most, cuts=(), kind=jnp.bfloat16):
    array = deviation * jax.random.normal(rng, extent, jnp.float32)
    if cuts:
        array = array * block_scale(rng, extent, cuts, -0.22, 0.18)
    return jnp.clip(array, -most, most).astype(kind)


def setup_inputs(seed: int = 0) -> dict:
    key_list = jax.random.split(jax.random.key(seed), 8)
    tokens = noise(key_list[0], (TOKENS, D), 1.0, 6.0, ((0, 512),))
    cotangent = noise(key_list[1], (TOKENS, D), 1.0, 6.0, ((0, 512),))
    groups = draw_groups(jax.random.fold_in(key_list[7], 71), 0)
    choices = draw_choices(jax.random.fold_in(key_list[7], 71), 0)
    gates = jnp.clip(jnp.exp(math.log(1.0) - 2.9996462 * jax.random.uniform(key_list[4], (TOKENS, 2, 2), jnp.float32) ** block_scale(key_list[4], (TOKENS, 2, 2), ((0, 512),), -0.2, 0.2)), 0.049804688, 1.0).astype(jnp.bfloat16)
    up_weight = noise(key_list[5], (D, EXPERTS * H), D ** -0.5, 0.0625, ((1, 512),))
    down_weight = noise(key_list[6], (EXPERTS * H, D), H ** -0.5, 0.1875, ((0, 512),))
    return dict(tokens=tokens, cotangent=cotangent, groups=groups, choices=choices, gates=gates, up_weight=up_weight, down_weight=down_weight)


def reference(tokens, cotangent, groups, choices, gates, up_weight, down_weight):
    slices = N_INGROUP // EXP_NODE
    part = H // slices
    width = tokens.shape[1]
    total = tokens.shape[0]
    count = total * 4
    cape = N_INGROUP * 2 * TOK_DEV
    owner = (groups[:, :, None] * EXP_NODE + choices).reshape(count).astype(jnp.int32)
    holder = (jnp.arange(count, dtype=jnp.int32) // 4).astype(jnp.int32)
    weight_all = gates.reshape(count).astype(jnp.float32)
    order = jnp.argsort(owner, stable=True).astype(jnp.int32)
    ids = jnp.arange(EXPERTS, dtype=jnp.int32)
    starts = jnp.sum((owner[None, :] < ids[:, None]).astype(jnp.int32), 1).astype(jnp.int32)
    totals = jnp.sum((owner[None, :] == ids[:, None]).astype(jnp.int32), 1).astype(jnp.int32)
    padded = jnp.concatenate([order, jnp.zeros((cape,), jnp.int32)])

    def visit(expert, carry):
        out_acc, dx_acc = carry
        index = lax.dynamic_slice_in_dim(padded, starts[expert].astype(jnp.int32), cape).astype(jnp.int32)
        live = jnp.arange(cape, dtype=jnp.int32) < totals[expert]
        rows_x = tokens[holder[index]]
        rows_dy = cotangent[holder[index]]
        gate_col = jnp.where(live, weight_all[index], jnp.float32(0.0))[:, None]
        start = (expert * H).astype(jnp.int32)
        up = lax.dynamic_slice_in_dim(up_weight, start, H, 1)
        down = lax.dynamic_slice_in_dim(down_weight, start, H, 0)
        pre = jnp.dot(rows_x, up, preferred_element_type=jnp.float32)
        active = jax.nn.silu(pre).astype(jnp.bfloat16)
        pieces = jnp.einsum("rsk,skd->rsd", active.reshape(cape, slices, part).astype(jnp.float32),
                            down.reshape(slices, part, width).astype(jnp.float32),
                            precision=lax.Precision.HIGHEST).astype(jnp.bfloat16)
        output = jnp.sum(pieces.astype(jnp.float32), 1).astype(jnp.bfloat16)
        back_hidden = jnp.dot(rows_dy, down.T, preferred_element_type=jnp.float32)
        sig = jax.nn.sigmoid(pre)
        grad_pre = (gate_col * back_hidden * sig * (1.0 + pre * (1.0 - sig))).astype(jnp.bfloat16)
        dx_pieces = jnp.einsum("rsk,skd->rsd", grad_pre.reshape(cape, slices, part).astype(jnp.float32),
                               up.T.reshape(slices, part, width).astype(jnp.float32),
                               precision=lax.Precision.HIGHEST).astype(jnp.bfloat16)
        dx_rows = jnp.sum(dx_pieces.astype(jnp.float32), 1)
        mask = live[:, None]
        out_acc = out_acc.at[index].add(jnp.where(mask, output.astype(jnp.float32), jnp.float32(0.0)))
        dx_acc = dx_acc.at[index].add(jnp.where(mask, dx_rows, jnp.float32(0.0)))
        return out_acc, dx_acc

    zeros = jnp.zeros((count, width), jnp.float32)
    out_all, dx_all = lax.fori_loop(0, EXPERTS, visit, (zeros, zeros))
    out_four = out_all.reshape(total, 2, 2, width)
    gate_four = gates.astype(jnp.float32)
    group_out = jnp.sum(gate_four[..., None] * out_four, 2).astype(jnp.bfloat16)
    mixed = jnp.sum(group_out.astype(jnp.float32), 1).astype(jnp.bfloat16)
    group_dx = jnp.sum(dx_all.reshape(total, 2, 2, width), 2).astype(jnp.bfloat16)
    grad_tokens = jnp.sum(group_dx.astype(jnp.float32), 1).astype(jnp.bfloat16)
    grad_gates = jnp.einsum("td,tckd->tck", cotangent.astype(jnp.float32), out_four,
                            precision=lax.Precision.HIGHEST).astype(jnp.bfloat16)
    return mixed, grad_tokens, grad_gates
```

```python
import jax
import jax.numpy as jnp
from jax import lax
from jax.sharding import Mesh, PartitionSpec as P

EXP_NODE = 4
LANES = 128


def dot(a, b, dims):
    return lax.dot_general(a, b, (dims, ((), ())), preferred_element_type=jnp.float32)


def per_device(tokens, cotangent, groups, choices, gates, up_weight, down_weight):
    f32, bf16 = jnp.float32, jnp.bfloat16
    tok_count, width = tokens.shape
    nodes = lax.axis_size("node")
    experts = lax.axis_size("expert")
    slices = lax.axis_size("slice")
    hidden = up_weight.shape[1]
    pairs = 2 * tok_count
    part = width // slices
    expert = lax.axis_index("expert")
    me = lax.axis_index("slice")
    lane = jnp.arange(LANES, dtype=jnp.int32)
    node_ids = jnp.arange(nodes, dtype=jnp.int32)

    place = node_ids[:, None, None] == groups[None]
    token_at = jnp.any(place, 2).astype(bf16)
    dense = jnp.sum(
        jnp.where(choices[..., None] == lane, gates[..., None].astype(f32), 0.0), 2
    )
    table = jnp.sum(jnp.where(place[..., None], dense[None], 0.0), (1, 2)).astype(bf16)
    packed = jnp.concatenate([tokens, cotangent], 1)
    sent = jnp.concatenate(
        [
            dot(token_at, packed, ((1,), (0,))).astype(bf16).reshape(nodes, -1, LANES),
            jnp.pad(table[:, None, :], ((0, 0), (0, 7), (0, 0))),
        ],
        1,
    )

    both_weights = jnp.concatenate(
        [
            up_weight.reshape(slices, part, hidden),
            down_weight.T.reshape(slices, part, hidden),
        ],
        1,
    )
    sent, both_weights = lax.optimization_barrier((sent, both_weights))
    recv = lax.all_to_all(sent, "node", split_axis=0, concat_axis=0, tiled=True)

    shifts = [(0, 0), (2, 0), (2, 1), (1, 0), (3, 0), (1, 1), (3, 1), (0, 1)]
    chips = slices // 2

    def moved(index, shift, sign):
        return ((index // 2 + sign * shift[0]) % chips) * 2 + (index % 2 + shift[1]) % 2

    held = []
    for shift in shifts:
        block = lax.dynamic_index_in_dim(both_weights, moved(me, shift, 1), 0, False)
        if shift != (0, 0):
            block = lax.ppermute(
                block, "slice", [(i, moved(i, shift, 1)) for i in range(slices)]
            )
        held.append(block)

    used = jnp.any(recv[:, 2 * width // LANES, :] > 0, 1)
    rank = jnp.cumsum(used.astype(jnp.int32)) - 1
    slot = jnp.arange(pairs, dtype=jnp.int32)
    pick = ((rank[None, :] == slot[:, None]) & used[None, :]).astype(bf16)
    mine = dot(pick, recv.reshape(nodes, -1), ((1,), (0,))).astype(bf16)
    blocks = jnp.stack(
        [
            jnp.concatenate(
                [
                    mine[:, m * part : (m + 1) * part],
                    mine[:, width + m * part : width + (m + 1) * part],
                    mine[:, 2 * width : 2 * width + LANES],
                ],
                1,
            )
            for m in range(slices)
        ]
    )
    spread = jnp.broadcast_to(blocks[None], (experts,) + blocks.shape).reshape(
        experts * slices, pairs, -1
    )
    rows = lax.all_to_all(
        spread, ("expert", "slice"), split_axis=0, concat_axis=0, tiled=True
    ).reshape(experts * slices * pairs, -1)
    x = rows[:, :part]
    dy = rows[:, part : 2 * part]
    gate = jnp.sum(
        jnp.where(lane[None, :] == expert, rows[:, 2 * part :].astype(f32), 0.0), 1, keepdims=True
    )

    partial = jnp.stack(
        [
            jnp.concatenate(
                [dot(x, w[:part], ((1,), (0,))), dot(dy, w[part:], ((1,), (0,)))], 1
            ).astype(bf16)
            for w in held
        ]
    )
    order = jnp.stack([jnp.asarray(moved(me, s, -1)) for s in shifts])
    where_is = jnp.sum(
        jnp.where(
            order[None, :] == jnp.arange(slices)[:, None], jnp.arange(slices)[None, :], 0
        ),
        1,
    )
    outgoing = jnp.stack(
        [lax.dynamic_index_in_dim(partial, where_is[m], 0, False) for m in range(slices)]
    )
    incoming = lax.all_to_all(outgoing, "slice", split_axis=0, concat_axis=0, tiled=True)
    both = jnp.sum(incoming.astype(f32), 0)
    pre = both[:, :hidden]
    back = both[:, hidden:]
    sig = jax.nn.sigmoid(pre)
    active = (pre * sig).astype(bf16)
    grad_pre = (gate * back * sig * (1.0 + pre * (1.0 - sig))).astype(bf16)
    own = jnp.concatenate([active, grad_pre], 1)
    every = lax.all_to_all(
        jnp.broadcast_to(own[None], (slices,) + own.shape),
        "slice",
        split_axis=0,
        concat_axis=0,
        tiled=True,
    )

    out = jnp.zeros((x.shape[0], part), f32)
    dx = jnp.zeros((x.shape[0], part), f32)
    for i, w in enumerate(held):
        units = lax.dynamic_index_in_dim(every, order[i], 0, False)
        out = out + dot(units[:, :hidden], w[part:], ((1,), (1,)))
        dx = dx + dot(units[:, hidden:], w[:part], ((1,), (1,)))
    inner = jnp.where(gate > 0, jnp.sum(out * dy.astype(f32), 1, keepdims=True), 0.0)
    result = jnp.concatenate(
        [gate * out, dx, jnp.where(lane[None, :] == expert, inner, 0.0)], 1
    ).astype(bf16)

    parts_back = lax.all_to_all(
        result.reshape(experts * slices, pairs, -1),
        ("expert", "slice"),
        split_axis=0,
        concat_axis=0,
        tiled=True,
    ).reshape(experts, slices, pairs, -1)
    summed = jnp.sum(parts_back.astype(f32), 0)
    inner_all = jnp.sum(summed[:, :, 2 * part :], 0)
    full = jnp.concatenate(
        [summed[m, :, :part] for m in range(slices)]
        + [summed[m, :, part : 2 * part] for m in range(slices)]
        + [inner_all],
        1,
    ).astype(bf16)
    expanded = dot(pick, full, ((0,), (0,))).astype(bf16)
    expanded = jnp.pad(expanded, ((0, 0), (0, 7 * LANES))).reshape(nodes, -1, LANES)
    home = lax.all_to_all(expanded, "node", split_axis=0, concat_axis=0, tiled=True)

    home_rows = home[:, : 2 * width // LANES].reshape(nodes, -1)
    total = dot(token_at, home_rows, ((0,), (0,))).astype(bf16)
    inner_rows = home[:, 2 * width // LANES].astype(f32)
    pair_inner = jnp.sum(jnp.where(place[..., None], inner_rows[:, None, None, :], 0.0), 0)
    grad_gates = jnp.sum(
        jnp.where(choices[..., None] == lane, pair_inner[:, :, None, :], 0.0), -1
    ).astype(bf16)
    return (total[:, :width], total[:, width:], grad_gates)


def solution(mesh):
    nodes, members = mesh.devices.shape
    fine = Mesh(
        mesh.devices.reshape(nodes, EXP_NODE, members // EXP_NODE), ("node", "expert", "slice")
    )
    both = ("node", "expert", "slice")
    placed = (
        P(both, None),
        P(both, None),
        P(both, None),
        P(both, None, None),
        P(both, None, None),
        P(None, both),
        P(both, None),
    )
    return jax.shard_map(
        per_device,
        mesh=fine,
        in_specs=placed,
        out_specs=(P(both, None), P(both, None), P(both, None, None)),
        check_vma=False,
    )
```

```python
import jax
import jax.numpy as jnp
from jax import lax
from jax.experimental import pallas as pl
from jax.experimental.pallas import tpu as pltpu
from jax.sharding import Mesh, PartitionSpec as P

EXP_NODE = 4
LANES = 128


def dot(a, b, dims):
    return lax.dot_general(a, b, (dims, ((), ())), preferred_element_type=jnp.float32)


def columns(own, other, core):
    part = other.shape[0] // (2 * len(own))
    for ref in own:
        start = pl.multiple_of(core * part, part)
        yield ref, start, 2 * part + start
    for i in range(len(own)):
        yield other, 2 * i * part, (2 * i + 1) * part


def pack_kernel(chips, up, down, *refs):
    outs, sems = refs[:-1], refs[-1]
    wide = up.shape[0] // len(outs)
    tiles = wide // LANES
    copies = []
    for i, out in enumerate(outs):
        start = pl.multiple_of(chips[i] * wide, wide)
        copies.append(
            pltpu.make_async_copy(up.at[pl.ds(start, wide)], out.at[pl.ds(0, wide)], sems.at[i, tiles])
        )
        for j in range(tiles):
            copies.append(
                pltpu.make_async_copy(
                    down.at[:, pl.ds(start + j * LANES, LANES)],
                    out.at[pl.ds(wide + j * LANES, LANES)],
                    sems.at[i, j],
                )
            )
    for copy in copies:
        copy.start()
    for copy in copies:
        copy.wait()


def other_kernel(scalars, *refs):
    blocks, out, sems = refs[:-2], refs[-2], refs[-1]
    part = blocks[0].shape[0] // 4
    start = pl.multiple_of((1 - scalars[0]) * part, part)
    copies = [
        pltpu.make_async_copy(
            block.at[pl.ds(2 * u * part + start, part)],
            out.at[pl.ds((2 * i + u) * part, part)],
            sems.at[2 * i + u],
        )
        for i, block in enumerate(blocks)
        for u in range(2)
    ]
    for copy in copies:
        copy.start()
    for copy in copies:
        copy.wait()


def partial_kernel(scalars, rows, *refs):
    own, other, out = refs[:-2], refs[-2], refs[-1]
    hidden = other.shape[1]
    part = other.shape[0] // (2 * len(own))
    x, dy = rows[:, :part], rows[:, part : 2 * part]
    for i, (ref, up, down) in enumerate(columns(own, other, scalars[0])):
        at = scalars[2 + i]
        out[at, :, :hidden] = dot(x, ref[pl.ds(up, part), :], ((1,), (0,))).astype(out.dtype)
        tiles = [ref[pl.ds(down + j, LANES), :] for j in range(0, part, LANES)]
        out[at, :, hidden:] = dot(dy, jnp.concatenate(tiles, 1), ((1,), (1,))).astype(out.dtype)


def output_kernel(scalars, rows, every, *refs):
    own, other, result = refs[:-2], refs[-2], refs[-1]
    hidden = other.shape[1]
    part = other.shape[0] // (2 * len(own))
    count = 2 * len(own)
    lane = lax.broadcasted_iota(jnp.int32, (rows.shape[0], LANES), 1)
    mine = lane == scalars[1]
    gate = jnp.sum(
        jnp.where(mine, rows[:, 2 * part :].astype(jnp.float32), 0.0), 1, keepdims=True
    )
    active = jnp.concatenate([every[scalars[2 + i], :, :hidden] for i in range(count)], 1)
    grad_pre = jnp.concatenate([every[scalars[2 + i], :, hidden:] for i in range(count)], 1)
    pieces = list(columns(own, other, scalars[0]))
    inner = jnp.zeros((rows.shape[0], 1), jnp.float32)
    for j in range(0, part, LANES):
        down = jnp.concatenate([ref[pl.ds(d + j, LANES), :] for ref, _, d in pieces], 0)
        up = jnp.concatenate([ref[pl.ds(u + j, LANES), :] for ref, u, _ in pieces], 1)
        out = dot(active, down, ((1,), (0,)))
        inner += jnp.sum(
            out * rows[:, part + j : part + j + LANES].astype(jnp.float32), 1, keepdims=True
        )
        result[:, j : j + LANES] = (gate * out).astype(result.dtype)
        result[:, part + j : part + j + LANES] = dot(grad_pre, up, ((1,), (1,))).astype(
            result.dtype
        )
    inner = jnp.where(gate > 0, inner, 0.0)
    result[:, 2 * part :] = jnp.where(mine, inner, 0.0).astype(result.dtype)


def call(kernel, shape, scalars, *operands, space=pltpu.VMEM, scratch=()):
    spec = pl.BlockSpec(memory_space=space)
    one = jax.ShapeDtypeStruct(shape, jnp.bfloat16) if isinstance(shape, tuple) else shape
    return pl.pallas_call(
        kernel,
        out_shape=one,
        in_specs=[pl.BlockSpec(memory_space=pltpu.SMEM)] + [spec] * len(operands),
        out_specs=jax.tree.map(lambda _: spec, one),
        scratch_shapes=scratch,
        compiler_params=pltpu.CompilerParams(vmem_limit_bytes=32 * 2**20),
    )(scalars, *operands)


def per_device(tokens, cotangent, groups, choices, gates, up_weight, down_weight):
    f32, bf16 = jnp.float32, jnp.bfloat16
    tok_count, width = tokens.shape
    nodes = lax.axis_size("node")
    experts = lax.axis_size("expert")
    slices = lax.axis_size("slice")
    hidden = up_weight.shape[1]
    pairs = 2 * tok_count
    part = width // slices
    expert = lax.axis_index("expert")
    me = lax.axis_index("slice")
    lane = jnp.arange(LANES, dtype=jnp.int32)
    node_ids = jnp.arange(nodes, dtype=jnp.int32)

    place = node_ids[:, None, None] == groups[None]
    token_at = jnp.any(place, 2).astype(bf16)
    dense = jnp.sum(
        jnp.where(choices[..., None] == lane, gates[..., None].astype(f32), 0.0), 2
    )
    table = jnp.sum(jnp.where(place[..., None], dense[None], 0.0), (1, 2)).astype(bf16)
    packed = jnp.concatenate([tokens, cotangent], 1)
    sent = jnp.concatenate(
        [
            dot(token_at, packed, ((1,), (0,))).astype(bf16).reshape(nodes, -1, LANES),
            jnp.pad(table[:, None, :], ((0, 0), (0, 7), (0, 0))),
        ],
        1,
    )

    chip, core = me // 2, me % 2
    chips = slices // 2
    block = jax.ShapeDtypeStruct((4 * part, hidden), bf16)
    targets = jnp.stack([(chip + s) % chips for s in range(chips)]).astype(jnp.int32)
    targets, sent = lax.optimization_barrier((targets, sent))
    own = call(
        pack_kernel,
        [block] * chips,
        targets,
        up_weight,
        down_weight,
        space=pl.ANY,
        scratch=[pltpu.SemaphoreType.DMA((chips, 2 * part // LANES + 1))],
    )
    own = [own[0]] + [
        lax.ppermute(
            own[s], "slice", [(i, ((i // 2 + s) % chips) * 2 + i % 2) for i in range(slices)]
        )
        for s in range(1, chips)
    ]
    recv = lax.all_to_all(sent, "node", split_axis=0, concat_axis=0, tiled=True)
    recv, own = lax.optimization_barrier((recv, own))

    sources = [(chip + chips - s) % chips for s in range(chips)]
    scalars = jnp.stack(
        [core, expert] + [2 * s + core for s in sources] + [2 * s + 1 - core for s in sources]
    ).astype(jnp.int32)
    other = call(
        other_kernel,
        (2 * chips * part, hidden),
        scalars,
        *own,
        space=pl.ANY,
        scratch=[pltpu.SemaphoreType.DMA((2 * chips,))],
    )
    other = lax.ppermute(other, "slice", [(i, i + 1 - 2 * (i % 2)) for i in range(slices)])

    used = jnp.any(recv[:, 2 * width // LANES, :] > 0, 1)
    rank = jnp.cumsum(used.astype(jnp.int32)) - 1
    slot = jnp.arange(pairs, dtype=jnp.int32)
    pick = ((rank[None, :] == slot[:, None]) & used[None, :]).astype(bf16)
    mine = dot(pick, recv.reshape(nodes, -1), ((1,), (0,))).astype(bf16)
    blocks = jnp.stack(
        [
            jnp.concatenate(
                [
                    mine[:, m * part : (m + 1) * part],
                    mine[:, width + m * part : width + (m + 1) * part],
                    mine[:, 2 * width : 2 * width + LANES],
                ],
                1,
            )
            for m in range(slices)
        ]
    )
    spread = jnp.broadcast_to(blocks[None], (experts,) + blocks.shape).reshape(
        experts * slices, pairs, -1
    )
    rows = lax.all_to_all(
        spread, ("expert", "slice"), split_axis=0, concat_axis=0, tiled=True
    ).reshape(experts * slices * pairs, -1)
    gate = jnp.sum(
        jnp.where(lane[None, :] == expert, rows[:, 2 * part :].astype(f32), 0.0), 1, keepdims=True
    )

    outgoing = call(
        partial_kernel, (slices, rows.shape[0], 2 * hidden), scalars, rows, *own, other
    )
    incoming = lax.all_to_all(outgoing, "slice", split_axis=0, concat_axis=0, tiled=True)
    both = jnp.sum(incoming.astype(f32), 0)
    pre = both[:, :hidden]
    back = both[:, hidden:]
    sig = jax.nn.sigmoid(pre)
    active = (pre * sig).astype(bf16)
    grad_pre = (gate * back * sig * (1.0 + pre * (1.0 - sig))).astype(bf16)
    units = jnp.concatenate([active, grad_pre], 1)
    every = lax.all_to_all(
        jnp.broadcast_to(units[None], (slices,) + units.shape),
        "slice",
        split_axis=0,
        concat_axis=0,
        tiled=True,
    )

    result = call(output_kernel, rows.shape, scalars, rows, every, *own, other)

    parts_back = lax.all_to_all(
        result.reshape(experts * slices, pairs, -1),
        ("expert", "slice"),
        split_axis=0,
        concat_axis=0,
        tiled=True,
    ).reshape(experts, slices, pairs, -1)
    summed = jnp.sum(parts_back.astype(f32), 0)
    inner_all = jnp.sum(summed[:, :, 2 * part :], 0)
    full = jnp.concatenate(
        [summed[m, :, :part] for m in range(slices)]
        + [summed[m, :, part : 2 * part] for m in range(slices)]
        + [inner_all],
        1,
    ).astype(bf16)
    expanded = dot(pick, full, ((0,), (0,))).astype(bf16)
    expanded = jnp.pad(expanded, ((0, 0), (0, 7 * LANES))).reshape(nodes, -1, LANES)
    home = lax.all_to_all(expanded, "node", split_axis=0, concat_axis=0, tiled=True)

    home_rows = home[:, : 2 * width // LANES].reshape(nodes, -1)
    total = dot(token_at, home_rows, ((0,), (0,))).astype(bf16)
    inner_rows = home[:, 2 * width // LANES].astype(f32)
    pair_inner = jnp.sum(jnp.where(place[..., None], inner_rows[:, None, None, :], 0.0), 0)
    grad_gates = jnp.sum(
        jnp.where(choices[..., None] == lane, pair_inner[:, :, None, :], 0.0), -1
    ).astype(bf16)
    return (total[:, :width], total[:, width:], grad_gates)


def solution(mesh):
    nodes, members = mesh.devices.shape
    fine = Mesh(
        mesh.devices.reshape(nodes, EXP_NODE, members // EXP_NODE), ("node", "expert", "slice")
    )
    both = ("node", "expert", "slice")
    placed = (
        P(both, None),
        P(both, None),
        P(both, None),
        P(both, None, None),
        P(both, None, None),
        P(None, both),
        P(both, None),
    )
    return jax.shard_map(
        per_device,
        mesh=fine,
        in_specs=placed,
        out_specs=(P(both, None), P(both, None), P(both, None, None)),
        check_vma=False,
    )
```

```python
import jax
import jax.numpy as jnp
from jax import lax
from jax.experimental import pallas as pl
from jax.experimental.pallas import tpu as pltpu
from jax.sharding import Mesh, PartitionSpec as P

EXPERTS = 4
CORES = 2
LANES = 128


def dot(a, b, dims):
    return lax.dot_general(a, b, (dims, ((), ())), preferred_element_type=jnp.float32)


def pack_kernel(chips, up, down, here, ahead, behind, sems):
    wide = here.shape[0] // 2
    tiles = wide // LANES
    copies = []

    def rows(chip, out, at):
        start = pl.multiple_of(chips[chip] * wide, wide)
        copies.append(
            pltpu.make_async_copy(
                up.at[pl.ds(start, wide)], out.at[pl.ds(at, wide)], sems.at[len(copies)]
            )
        )

    def columns(chip, out, at):
        start = pl.multiple_of(chips[chip] * wide, wide)
        for j in range(0, wide, LANES):
            copies.append(
                pltpu.make_async_copy(
                    down.at[:, pl.ds(start + j, LANES)],
                    out.at[pl.ds(at + j, LANES)],
                    sems.at[len(copies)],
                )
            )

    for chip, out in ((1, ahead), (3, behind), (0, here)):
        rows(chip, out, 0)
        columns(chip, out, wide)
    rows(2, ahead, 2 * wide)
    columns(2, behind, 2 * wide)
    for copy in copies:
        copy.start()
    for copy in copies:
        copy.wait()


def partial_kernel(scalars, rows, *refs):
    blocks, out = refs[:-1], refs[-1]
    hidden = blocks[0].shape[1]
    wide = (rows.shape[1] - LANES) // 2
    x, dy = rows[:, :wide], rows[:, wide : 2 * wide]
    for i in range(len(blocks) // CORES):
        pair = blocks[CORES * i : CORES * (i + 1)]
        at = scalars[1 + i]
        up = jnp.concatenate([ref[:wide, :] for ref in pair], 1)
        out[at, :, : CORES * hidden] = dot(x, up, ((1,), (0,))).astype(out.dtype)
        down = jnp.concatenate(
            [
                jnp.concatenate([ref[wide + j : wide + j + LANES, :] for ref in pair], 0)
                for j in range(0, wide, LANES)
            ],
            1,
        )
        out[at, :, CORES * hidden :] = dot(dy, down, ((1,), (1,))).astype(out.dtype)


def output_kernel(scalars, rows, every, *refs):
    blocks, result = refs[:-1], refs[-1]
    hidden = blocks[0].shape[1]
    wide = (rows.shape[1] - LANES) // 2
    chips = len(blocks) // CORES
    count = rows.shape[0]
    lane = lax.broadcasted_iota(jnp.int32, (count, LANES), 1)
    mine = lane == scalars[0]
    gate = jnp.sum(
        jnp.where(mine, rows[:, 2 * wide :].astype(jnp.float32), 0.0), 1, keepdims=True
    )
    active = jnp.concatenate(
        [every[scalars[1 + i], :, : CORES * hidden] for i in range(chips)], 1
    )
    grad_pre = jnp.concatenate(
        [every[scalars[1 + i], :, CORES * hidden :] for i in range(chips)], 1
    )
    inner = jnp.zeros((count, 1), jnp.float32)
    step = 2 * LANES
    for j in range(0, wide, step):
        down = jnp.concatenate(
            [
                jnp.concatenate([ref[wide + j + k : wide + j + k + LANES, :] for ref in blocks], 0)
                for k in range(0, step, LANES)
            ],
            1,
        )
        up = jnp.concatenate([ref[j : j + step, :] for ref in blocks], 1)
        out = dot(active, down, ((1,), (0,)))
        inner += jnp.sum(
            out * rows[:, wide + j : wide + j + step].astype(jnp.float32), 1, keepdims=True
        )
        result[:, j : j + step] = (gate * out).astype(result.dtype)
        result[:, wide + j : wide + j + step] = dot(grad_pre, up, ((1,), (1,))).astype(
            result.dtype
        )
    inner = jnp.where(gate > 0, inner, 0.0)
    result[:, 2 * wide :] = jnp.where(mine, inner, 0.0).astype(result.dtype)


def call(kernel, shapes, scalars, *operands, space=pltpu.VMEM, scratch=()):
    spec = pl.BlockSpec(memory_space=space)
    out = [jax.ShapeDtypeStruct(shape, jnp.bfloat16) for shape in shapes]
    return pl.pallas_call(
        kernel,
        out_shape=out,
        in_specs=[pl.BlockSpec(memory_space=pltpu.SMEM)] + [spec] * len(operands),
        out_specs=[spec] * len(out),
        scratch_shapes=scratch,
        compiler_params=pltpu.CompilerParams(vmem_limit_bytes=40 * 2**20),
    )(scalars, *operands)


def per_device(tokens, cotangent, groups, choices, gates, up_weight, down_weight):
    f32, bf16 = jnp.float32, jnp.bfloat16
    tok_count, width = tokens.shape
    nodes = lax.axis_size("node")
    experts = lax.axis_size("expert")
    chips = lax.axis_size("chip")
    hidden = up_weight.shape[1]
    pairs = 2 * tok_count
    wide = width // chips
    expert = lax.axis_index("expert")
    chip = lax.axis_index("chip")
    lane = jnp.arange(LANES, dtype=jnp.int32)
    node_ids = jnp.arange(nodes, dtype=jnp.int32)

    place = node_ids[:, None, None] == groups[None]
    token_at = jnp.any(place, 2).astype(bf16)
    dense = jnp.sum(
        jnp.where(choices[..., None] == lane, gates[..., None].astype(f32), 0.0), 2
    )
    table = jnp.sum(jnp.where(place[..., None], dense[None], 0.0), (1, 2)).astype(bf16)
    packed = jnp.concatenate([tokens, cotangent], 1)
    sent = jnp.concatenate(
        [
            dot(token_at, packed, ((1,), (0,))).astype(bf16).reshape(nodes, -1, LANES),
            jnp.pad(table[:, None, :], ((0, 0), (0, 7), (0, 0))),
        ],
        1,
    )

    ahead_of = [(i, (i + 1) % chips) for i in range(chips)]
    behind_of = [(i, (i - 1) % chips) for i in range(chips)]
    targets = jnp.stack([(chip + s) % chips for s in range(chips)]).astype(jnp.int32)
    targets, sent = lax.optimization_barrier((targets, sent))
    here, ahead, behind = call(
        pack_kernel,
        [(2 * wide, hidden), (3 * wide, hidden), (3 * wide, hidden)],
        targets,
        up_weight,
        down_weight,
        space=pl.ANY,
        scratch=[pltpu.SemaphoreType.DMA((chips * (wide // LANES + 1),))],
    )
    ahead = lax.ppermute(ahead, "chip", ahead_of)
    behind = lax.ppermute(behind, "chip", behind_of)
    recv = lax.all_to_all(sent, "node", split_axis=0, concat_axis=0, tiled=True)
    recv, ahead, behind = lax.optimization_barrier((recv, ahead, behind))
    swap = [(0, 1), (1, 0)]
    blocks = []
    for block in (here, ahead, behind):
        blocks += [block, lax.ppermute(block, "core", swap)]
    far_up = lax.ppermute(ahead[2 * wide :], "chip", ahead_of)
    far_down = lax.ppermute(behind[2 * wide :], "chip", behind_of)
    scalars = jnp.stack(
        [expert, chip, (chip + chips - 1) % chips, (chip + 1) % chips, (chip + 2) % chips]
    ).astype(jnp.int32)

    used = jnp.any(recv[:, 2 * width // LANES, :] > 0, 1)
    rank = jnp.cumsum(used.astype(jnp.int32)) - 1
    slot = jnp.arange(pairs, dtype=jnp.int32)
    pick = ((rank[None, :] == slot[:, None]) & used[None, :]).astype(bf16)
    mine = dot(pick, recv.reshape(nodes, -1), ((1,), (0,))).astype(bf16)
    parts = jnp.stack(
        [
            jnp.concatenate(
                [
                    mine[:, m * wide : (m + 1) * wide],
                    mine[:, width + m * wide : width + (m + 1) * wide],
                    mine[:, 2 * width : 2 * width + LANES],
                ],
                1,
            )
            for m in range(chips)
        ]
    )
    spread = jnp.broadcast_to(parts[None], (experts,) + parts.shape).reshape(
        experts * chips, pairs, -1
    )
    rows = lax.all_to_all(
        spread, ("expert", "chip"), split_axis=0, concat_axis=0, tiled=True
    ).reshape(experts * chips * pairs, -1)
    rows, far_up, far_down = lax.optimization_barrier((rows, far_up, far_down))
    far = jnp.concatenate([far_up, far_down], 0)
    blocks += [far, lax.ppermute(far, "core", swap)]
    gate = jnp.sum(
        jnp.where(lane[None, :] == expert, rows[:, 2 * wide :].astype(f32), 0.0), 1, keepdims=True
    )

    units = CORES * hidden
    (outgoing,) = call(
        partial_kernel, [(chips, rows.shape[0], 2 * units)], scalars, rows, *blocks
    )
    incoming = lax.all_to_all(outgoing, "chip", split_axis=0, concat_axis=0, tiled=True)
    both = jnp.sum(incoming.astype(f32), 0)
    pre = both[:, :units]
    back = both[:, units:]
    sig = jax.nn.sigmoid(pre)
    active = (pre * sig).astype(bf16)
    grad_pre = (gate * back * sig * (1.0 + pre * (1.0 - sig))).astype(bf16)
    every = lax.all_gather(jnp.concatenate([active, grad_pre], 1), "chip", axis=0)

    (result,) = call(output_kernel, [rows.shape], scalars, rows, every, *blocks)

    parts_back = lax.all_to_all(
        result.reshape(experts * chips, pairs, -1),
        ("expert", "chip"),
        split_axis=0,
        concat_axis=0,
        tiled=True,
    ).reshape(experts, chips, pairs, -1)
    summed = jnp.sum(parts_back.astype(f32), 0)
    inner_all = jnp.sum(summed[:, :, 2 * wide :], 0)
    full = jnp.concatenate(
        [summed[m, :, :wide] for m in range(chips)]
        + [summed[m, :, wide : 2 * wide] for m in range(chips)]
        + [inner_all],
        1,
    ).astype(bf16)
    expanded = dot(pick, full, ((0,), (0,))).astype(bf16)
    expanded = jnp.pad(expanded, ((0, 0), (0, 7 * LANES))).reshape(nodes, -1, LANES)
    home = lax.all_to_all(expanded, "node", split_axis=0, concat_axis=0, tiled=True)

    home_rows = home[:, : 2 * width // LANES].reshape(nodes, -1)
    total = dot(token_at, home_rows, ((0,), (0,))).astype(bf16)
    inner_rows = home[:, 2 * width // LANES].astype(f32)
    pair_inner = jnp.sum(jnp.where(place[..., None], inner_rows[:, None, None, :], 0.0), 0)
    grad_gates = jnp.sum(
        jnp.where(choices[..., None] == lane, pair_inner[:, :, None, :], 0.0), -1
    ).astype(bf16)
    return (total[:, :width], total[:, width:], grad_gates)


def solution(mesh):
    nodes, members = mesh.devices.shape
    axes = ("node", "expert", "chip", "core")
    fine = Mesh(
        mesh.devices.reshape(nodes, EXPERTS, members // (EXPERTS * CORES), CORES), axes
    )
    placed = (
        P(axes, None),
        P(axes, None),
        P(axes, None),
        P(axes, None, None),
        P(axes, None, None),
        P(None, axes),
        P(axes, None),
    )
    return jax.shard_map(
        per_device,
        mesh=fine,
        in_specs=placed,
        out_specs=(P(axes, None), P(axes, None), P(axes, None, None)),
        check_vma=False,
    )
```

```python
import jax
import jax.numpy as jnp
from jax import lax
from jax.experimental import pallas as pl
from jax.experimental.pallas import tpu as pltpu
from jax.sharding import Mesh, PartitionSpec as P

EXPERTS = 4
CORES = 2
LANES = 128


def dot(a, b, dims):
    return lax.dot_general(a, b, (dims, ((), ())), preferred_element_type=jnp.float32)


def send_kernel(groups, choices, gates, tokens, cotangent, out, wide):
    count, width = tokens.shape
    chunks = width // LANES
    for j in range(chunks):
        at = pl.ds(j * LANES, LANES)
        wide[:, j, :] = tokens[:, at].astype(jnp.float32)
        wide[:, chunks + j, :] = cotangent[:, at].astype(jnp.float32)
    out[...] = jnp.zeros_like(out)
    every_gate = gates[...].astype(jnp.float32)
    row = lax.broadcasted_iota(jnp.int32, (8, LANES), 0)
    lane = lax.broadcasted_iota(jnp.int32, (8, LANES), 1)
    i, j = (lax.broadcasted_iota(jnp.int32, (2, 2), d) for d in range(2))
    for t in range(count):
        rows = wide[t].astype(out.dtype)
        for c in range(2):
            node = groups[t, c]
            out[node, : 2 * chunks, :] = rows
            table = jnp.zeros((8, LANES), jnp.float32)
            for k in range(2):
                gate = jnp.sum(jnp.where((i == c) & (j == k), every_gate[t], 0.0), keepdims=True)
                table += jnp.where((row == 0) & (lane == choices[t, c, k]), gate, 0.0)
            out[node, 2 * chunks :, :] = table.astype(out.dtype)


def home_kernel(groups, choices, home, mixed, grad_tokens, grad_gates, wide):
    count, width = mixed.shape
    chunks = width // LANES
    row = lax.broadcasted_iota(jnp.int32, (8, LANES), 0)
    lane = lax.broadcasted_iota(jnp.int32, (8, LANES), 1)
    i, j = (lax.broadcasted_iota(jnp.int32, (2, 2), d) for d in range(2))
    for t in range(count):
        total = jnp.zeros((2 * chunks, LANES), jnp.float32)
        inner = jnp.zeros((2, 2), jnp.float32)
        for c in range(2):
            node = groups[t, c]
            total += home[node, : 2 * chunks, :].astype(jnp.float32)
            table = home[node, 2 * chunks :, :].astype(jnp.float32)
            for k in range(2):
                value = jnp.sum(
                    jnp.where((row == 0) & (lane == choices[t, c, k]), table, 0.0), keepdims=True
                )
                inner = jnp.where((i == c) & (j == k), value, inner)
        wide[t] = total
        grad_gates[t] = inner.astype(grad_gates.dtype)
    for j in range(chunks):
        at = pl.ds(j * LANES, LANES)
        mixed[:, at] = wide[:, j, :].astype(mixed.dtype)
        grad_tokens[:, at] = wide[:, chunks + j, :].astype(grad_tokens.dtype)


def pack_kernel(chips, up, down, here, ahead, behind, sems):
    wide = here.shape[0] // 2
    tiles = wide // LANES
    copies = []

    def rows(chip, out, at):
        start = pl.multiple_of(chips[chip] * wide, wide)
        copies.append(
            pltpu.make_async_copy(
                up.at[pl.ds(start, wide)], out.at[pl.ds(at, wide)], sems.at[len(copies)]
            )
        )

    def columns(chip, out, at):
        start = pl.multiple_of(chips[chip] * wide, wide)
        for j in range(0, wide, LANES):
            copies.append(
                pltpu.make_async_copy(
                    down.at[:, pl.ds(start + j, LANES)],
                    out.at[pl.ds(at + j, LANES)],
                    sems.at[len(copies)],
                )
            )

    for chip, out in ((1, ahead), (3, behind), (0, here)):
        rows(chip, out, 0)
        columns(chip, out, wide)
    rows(2, ahead, 2 * wide)
    columns(2, behind, 2 * wide)
    for copy in copies:
        copy.start()
    for copy in copies:
        copy.wait()


def partial_kernel(scalars, rows, *refs):
    blocks, out = refs[:-1], refs[-1]
    hidden = blocks[0].shape[1]
    wide = (rows.shape[1] - LANES) // 2
    x, dy = rows[:, :wide], rows[:, wide : 2 * wide]
    for i in range(len(blocks) // CORES):
        pair = blocks[CORES * i : CORES * (i + 1)]
        at = scalars[1 + i]
        up = jnp.concatenate([ref[:wide, :] for ref in pair], 1)
        out[at, :, : CORES * hidden] = dot(x, up, ((1,), (0,))).astype(out.dtype)
        down = jnp.concatenate(
            [
                jnp.concatenate([ref[wide + j : wide + j + LANES, :] for ref in pair], 0)
                for j in range(0, wide, LANES)
            ],
            1,
        )
        out[at, :, CORES * hidden :] = dot(dy, down, ((1,), (1,))).astype(out.dtype)


def output_kernel(scalars, rows, every, *refs):
    blocks, result = refs[:-1], refs[-1]
    hidden = blocks[0].shape[1]
    wide = (rows.shape[1] - LANES) // 2
    chips = len(blocks) // CORES
    count = rows.shape[0]
    lane = lax.broadcasted_iota(jnp.int32, (count, LANES), 1)
    mine = lane == scalars[0]
    gate = jnp.sum(
        jnp.where(mine, rows[:, 2 * wide :].astype(jnp.float32), 0.0), 1, keepdims=True
    )
    active = jnp.concatenate(
        [every[scalars[1 + i], :, : CORES * hidden] for i in range(chips)], 1
    )
    grad_pre = jnp.concatenate(
        [every[scalars[1 + i], :, CORES * hidden :] for i in range(chips)], 1
    )
    inner = jnp.zeros((count, 1), jnp.float32)
    step = 2 * LANES
    for j in range(0, wide, step):
        down = jnp.concatenate(
            [
                jnp.concatenate([ref[wide + j + k : wide + j + k + LANES, :] for ref in blocks], 0)
                for k in range(0, step, LANES)
            ],
            1,
        )
        up = jnp.concatenate([ref[j : j + step, :] for ref in blocks], 1)
        out = dot(active, down, ((1,), (0,)))
        inner += jnp.sum(
            out * rows[:, wide + j : wide + j + step].astype(jnp.float32), 1, keepdims=True
        )
        result[:, j : j + step] = (gate * out).astype(result.dtype)
        result[:, wide + j : wide + j + step] = dot(grad_pre, up, ((1,), (1,))).astype(
            result.dtype
        )
    inner = jnp.where(gate > 0, inner, 0.0)
    result[:, 2 * wide :] = jnp.where(mine, inner, 0.0).astype(result.dtype)


def call(kernel, shapes, scalars, *operands, space=pltpu.VMEM, scratch=()):
    spec = pl.BlockSpec(memory_space=space)
    scalars = scalars if isinstance(scalars, tuple) else (scalars,)
    out = [jax.ShapeDtypeStruct(shape, jnp.bfloat16) for shape in shapes]
    return pl.pallas_call(
        kernel,
        out_shape=out,
        in_specs=[pl.BlockSpec(memory_space=pltpu.SMEM)] * len(scalars) + [spec] * len(operands),
        out_specs=[spec] * len(out),
        scratch_shapes=scratch,
        compiler_params=pltpu.CompilerParams(vmem_limit_bytes=40 * 2**20),
    )(*scalars, *operands)


def per_device(tokens, cotangent, groups, choices, gates, up_weight, down_weight):
    f32, bf16 = jnp.float32, jnp.bfloat16
    tok_count, width = tokens.shape
    nodes = lax.axis_size("node")
    experts = lax.axis_size("expert")
    chips = lax.axis_size("chip")
    hidden = up_weight.shape[1]
    pairs = 2 * tok_count
    wide = width // chips
    expert = lax.axis_index("expert")
    chip = lax.axis_index("chip")
    lane = jnp.arange(LANES, dtype=jnp.int32)

    slot_rows = 2 * width // LANES
    wide_rows = pltpu.VMEM((tok_count, slot_rows, LANES), f32)
    (sent,) = call(
        send_kernel,
        [(nodes, slot_rows + 8, LANES)],
        (groups, choices),
        gates,
        tokens,
        cotangent,
        scratch=[wide_rows],
    )

    ahead_of = [(i, (i + 1) % chips) for i in range(chips)]
    behind_of = [(i, (i - 1) % chips) for i in range(chips)]
    targets = jnp.stack([(chip + s) % chips for s in range(chips)]).astype(jnp.int32)
    here, ahead, behind = call(
        pack_kernel,
        [(2 * wide, hidden), (3 * wide, hidden), (3 * wide, hidden)],
        targets,
        up_weight,
        down_weight,
        space=pl.ANY,
        scratch=[pltpu.SemaphoreType.DMA((chips * (wide // LANES + 1),))],
    )
    ahead = lax.ppermute(ahead, "chip", ahead_of)
    behind = lax.ppermute(behind, "chip", behind_of)
    recv = lax.all_to_all(sent, "node", split_axis=0, concat_axis=0, tiled=True)
    swap = [(0, 1), (1, 0)]
    blocks = []
    for block in (here, ahead, behind):
        blocks += [block, lax.ppermute(block, "core", swap)]
    far_up = lax.ppermute(ahead[2 * wide :], "chip", ahead_of)
    far_down = lax.ppermute(behind[2 * wide :], "chip", behind_of)
    recv, far_up, far_down = lax.optimization_barrier((recv, far_up, far_down))
    far = jnp.concatenate([far_up, far_down], 0)
    blocks += [far, lax.ppermute(far, "core", swap)]
    scalars = jnp.stack(
        [expert, chip, (chip + chips - 1) % chips, (chip + 1) % chips, (chip + 2) % chips]
    ).astype(jnp.int32)

    used = jnp.any(recv[:, 2 * width // LANES, :] > 0, 1)
    rank = jnp.cumsum(used.astype(jnp.int32)) - 1
    slot = jnp.arange(pairs, dtype=jnp.int32)
    pick = ((rank[None, :] == slot[:, None]) & used[None, :]).astype(bf16)
    mine = dot(pick, recv.reshape(nodes, -1), ((1,), (0,))).astype(bf16)
    parts = jnp.stack(
        [
            jnp.concatenate(
                [
                    mine[:, m * wide : (m + 1) * wide],
                    mine[:, width + m * wide : width + (m + 1) * wide],
                    mine[:, 2 * width : 2 * width + LANES],
                ],
                1,
            )
            for m in range(chips)
        ]
    )
    spread = jnp.broadcast_to(parts[None], (experts,) + parts.shape).reshape(
        experts * chips, pairs, -1
    )
    rows = lax.all_to_all(
        spread, ("expert", "chip"), split_axis=0, concat_axis=0, tiled=True
    ).reshape(experts * chips * pairs, -1)
    gate = jnp.sum(
        jnp.where(lane[None, :] == expert, rows[:, 2 * wide :].astype(f32), 0.0), 1, keepdims=True
    )

    units = CORES * hidden
    (outgoing,) = call(
        partial_kernel, [(chips, rows.shape[0], 2 * units)], scalars, rows, *blocks
    )
    incoming = lax.all_to_all(outgoing, "chip", split_axis=0, concat_axis=0, tiled=True)
    both = jnp.sum(incoming.astype(f32), 0)
    pre = both[:, :units]
    back = both[:, units:]
    sig = jax.nn.sigmoid(pre)
    active = (pre * sig).astype(bf16)
    grad_pre = (gate * back * sig * (1.0 + pre * (1.0 - sig))).astype(bf16)
    every = lax.all_gather(jnp.concatenate([active, grad_pre], 1), "chip", axis=0)

    (result,) = call(output_kernel, [rows.shape], scalars, rows, every, *blocks)

    parts_back = lax.all_to_all(
        result.reshape(experts * chips, pairs, -1),
        ("expert", "chip"),
        split_axis=0,
        concat_axis=0,
        tiled=True,
    ).reshape(experts, chips, pairs, -1)
    summed = jnp.sum(parts_back.astype(f32), 0)
    inner_all = jnp.sum(summed[:, :, 2 * wide :], 0)
    full = jnp.concatenate(
        [summed[m, :, :wide] for m in range(chips)]
        + [summed[m, :, wide : 2 * wide] for m in range(chips)]
        + [inner_all],
        1,
    ).astype(bf16)
    expanded = dot(pick, full, ((0,), (0,))).astype(bf16)
    expanded = jnp.pad(expanded, ((0, 0), (0, 7 * LANES))).reshape(nodes, -1, LANES)
    home = lax.all_to_all(expanded, "node", split_axis=0, concat_axis=0, tiled=True)

    return call(
        home_kernel,
        [tokens.shape, tokens.shape, gates.shape],
        (groups, choices),
        home,
        scratch=[wide_rows],
    )


def solution(mesh):
    nodes, members = mesh.devices.shape
    axes = ("node", "expert", "chip", "core")
    fine = Mesh(
        mesh.devices.reshape(nodes, EXPERTS, members // (EXPERTS * CORES), CORES), axes
    )
    placed = (
        P(axes, None),
        P(axes, None),
        P(axes, None),
        P(axes, None, None),
        P(axes, None, None),
        P(None, axes),
        P(axes, None),
    )
    return jax.shard_map(
        per_device,
        mesh=fine,
        in_specs=placed,
        out_specs=(P(axes, None), P(axes, None), P(axes, None, None)),
        check_vma=False,
    )
```

```python
import jax
import jax.numpy as jnp
from jax import lax
from jax.experimental import pallas as pl
from jax.experimental.pallas import tpu as pltpu
from jax.sharding import Mesh, PartitionSpec as P

EXPERTS = 4
CORES = 2
LANES = 128


def dot(a, b, dims):
    return lax.dot_general(a, b, (dims, ((), ())), preferred_element_type=jnp.float32)


def send_kernel(groups, choices, gates, tokens, cotangent, out, narrow, wide, sems):
    count, width = tokens.shape
    chunks = width // LANES
    copies = [
        pltpu.make_async_copy(ref, narrow.at[i], sems.at[i])
        for i, ref in enumerate((tokens, cotangent))
    ]
    for copy in copies:
        copy.start()
    out[...] = jnp.zeros_like(out)
    every_gate = gates[...].astype(jnp.float32)
    row = lax.broadcasted_iota(jnp.int32, (8, LANES), 0)
    lane = lax.broadcasted_iota(jnp.int32, (8, LANES), 1)
    i, j = (lax.broadcasted_iota(jnp.int32, (2, count), d) for d in range(2))
    for t in range(count):
        for c in range(2):
            table = jnp.zeros((8, LANES), jnp.float32)
            for k in range(2):
                gate = jnp.sum(jnp.where((i == k) & (j == t), every_gate[c], 0.0), keepdims=True)
                table += jnp.where((row == 0) & (lane == choices[c, k, t]), gate, 0.0)
            out[groups[c, t], 2 * chunks :, :] = table.astype(out.dtype)
    for i, copy in enumerate(copies):
        copy.wait()
        for j in range(chunks):
            wide[:, i * chunks + j, :] = narrow[i, :, j * LANES : (j + 1) * LANES].astype(
                jnp.float32
            )
    for t in range(count):
        rows = wide[t].astype(out.dtype)
        for c in range(2):
            out[groups[c, t], : 2 * chunks, :] = rows


def home_kernel(groups, choices, home, mixed, grad_tokens, grad_gates, wide):
    count, width = mixed.shape
    chunks = width // LANES
    row = lax.broadcasted_iota(jnp.int32, (8, LANES), 0)
    lane = lax.broadcasted_iota(jnp.int32, (8, LANES), 1)
    i, j = (lax.broadcasted_iota(jnp.int32, (2, count), d) for d in range(2))
    inner = [jnp.zeros((2, count), jnp.float32) for c in range(2)]
    for t in range(count):
        total = jnp.zeros((2 * chunks, LANES), jnp.float32)
        for c in range(2):
            node = groups[c, t]
            total += home[node, : 2 * chunks, :].astype(jnp.float32)
            table = home[node, 2 * chunks :, :].astype(jnp.float32)
            for k in range(2):
                value = jnp.sum(
                    jnp.where((row == 0) & (lane == choices[c, k, t]), table, 0.0), keepdims=True
                )
                inner[c] = jnp.where((i == k) & (j == t), value, inner[c])
        wide[t] = total
    for c in range(2):
        grad_gates[c] = inner[c].astype(grad_gates.dtype)
    for j in range(chunks):
        at = pl.ds(j * LANES, LANES)
        mixed[:, at] = wide[:, j, :].astype(mixed.dtype)
        grad_tokens[:, at] = wide[:, chunks + j, :].astype(grad_tokens.dtype)


def pack_kernel(chips, up, down, here, ahead, behind, far_up, far_down, sems):
    wide = far_up.shape[0]
    copies = []

    def rows(chip, out, at):
        start = pl.multiple_of(chips[chip] * wide, wide)
        copies.append(
            pltpu.make_async_copy(
                up.at[pl.ds(start, wide)], out.at[pl.ds(at, wide)], sems.at[len(copies)]
            )
        )

    def columns(chip, out, at):
        start = pl.multiple_of(chips[chip] * wide, wide)
        for j in range(0, wide, LANES):
            copies.append(
                pltpu.make_async_copy(
                    down.at[:, pl.ds(start + j, LANES)],
                    out.at[pl.ds(at + j, LANES)],
                    sems.at[len(copies)],
                )
            )

    for chip, out in ((1, ahead), (3, behind), (0, here)):
        rows(chip, out, 0)
        columns(chip, out, wide)
    rows(2, far_up, 0)
    columns(2, far_down, 0)
    for copy in copies:
        copy.start()
    for copy in copies:
        copy.wait()


def pieces(refs, wide):
    whole = [(ref.at[pl.ds(0, wide)], ref.at[pl.ds(wide, wide)]) for ref in refs[:-4]]
    return whole + [(refs[-4], refs[-2]), (refs[-3], refs[-1])]


def partial_kernel(scalars, rows, *refs):
    out = refs[-1]
    hidden = refs[0].shape[1]
    wide = (rows.shape[1] - LANES) // 2
    blocks = pieces(refs[:-1], wide)
    x, dy = rows[:, :wide], rows[:, wide : 2 * wide]
    for i in range(len(blocks) // CORES):
        pair = blocks[CORES * i : CORES * (i + 1)]
        at = scalars[1 + i]
        up = jnp.concatenate([u[...] for u, _ in pair], 1)
        out[at, :, : CORES * hidden] = dot(x, up, ((1,), (0,))).astype(out.dtype)
        down = jnp.concatenate(
            [
                jnp.concatenate([d[j : j + LANES, :] for _, d in pair], 0)
                for j in range(0, wide, LANES)
            ],
            1,
        )
        out[at, :, CORES * hidden :] = dot(dy, down, ((1,), (1,))).astype(out.dtype)


def output_kernel(scalars, rows, every, *refs):
    result = refs[-1]
    hidden = refs[0].shape[1]
    wide = (rows.shape[1] - LANES) // 2
    blocks = pieces(refs[:-1], wide)
    chips = len(blocks) // CORES
    count = rows.shape[0]
    lane = lax.broadcasted_iota(jnp.int32, (count, LANES), 1)
    mine = lane == scalars[0]
    gate = jnp.sum(
        jnp.where(mine, rows[:, 2 * wide :].astype(jnp.float32), 0.0), 1, keepdims=True
    )
    active = jnp.concatenate(
        [every[scalars[1 + i], :, : CORES * hidden] for i in range(chips)], 1
    )
    grad_pre = jnp.concatenate(
        [every[scalars[1 + i], :, CORES * hidden :] for i in range(chips)], 1
    )
    inner = jnp.zeros((count, 1), jnp.float32)
    step = 2 * LANES
    for j in range(0, wide, step):
        down = jnp.concatenate(
            [
                jnp.concatenate([d[j + k : j + k + LANES, :] for _, d in blocks], 0)
                for k in range(0, step, LANES)
            ],
            1,
        )
        up = jnp.concatenate([u[j : j + step, :] for u, _ in blocks], 1)
        out = dot(active, down, ((1,), (0,)))
        inner += jnp.sum(
            out * rows[:, wide + j : wide + j + step].astype(jnp.float32), 1, keepdims=True
        )
        result[:, j : j + step] = (gate * out).astype(result.dtype)
        result[:, wide + j : wide + j + step] = dot(grad_pre, up, ((1,), (1,))).astype(
            result.dtype
        )
    inner = jnp.where(gate > 0, inner, 0.0)
    result[:, 2 * wide :] = jnp.where(mine, inner, 0.0).astype(result.dtype)


def call(kernel, shapes, scalars, *operands, hbm=0, scratch=()):
    spec = pl.BlockSpec(memory_space=pltpu.VMEM)
    far = pl.BlockSpec(memory_space=pltpu.HBM)
    scalars = scalars if isinstance(scalars, tuple) else (scalars,)
    out = [jax.ShapeDtypeStruct(shape, jnp.bfloat16) for shape in shapes]
    return pl.pallas_call(
        kernel,
        out_shape=out,
        in_specs=[pl.BlockSpec(memory_space=pltpu.SMEM)] * len(scalars)
        + [spec] * (len(operands) - hbm)
        + [far] * hbm,
        out_specs=[spec] * len(out),
        scratch_shapes=scratch,
        compiler_params=pltpu.CompilerParams(vmem_limit_bytes=40 * 2**20),
    )(*scalars, *operands)


def per_device(tokens, cotangent, groups, choices, gates, up_weight, down_weight):
    f32, bf16 = jnp.float32, jnp.bfloat16
    tok_count, width = tokens.shape
    nodes = lax.axis_size("node")
    experts = lax.axis_size("expert")
    chips = lax.axis_size("chip")
    hidden = up_weight.shape[1]
    pairs = 2 * tok_count
    wide = width // chips
    expert = lax.axis_index("expert")
    chip = lax.axis_index("chip")
    lane = jnp.arange(LANES, dtype=jnp.int32)

    slot_rows = 2 * width // LANES
    groups, choices = groups.T, choices.transpose(1, 2, 0)
    wide_rows = pltpu.VMEM((tok_count, slot_rows, LANES), f32)
    (sent,) = call(
        send_kernel,
        [(nodes, slot_rows + 8, LANES)],
        (groups, choices),
        gates.transpose(1, 2, 0),
        tokens,
        cotangent,
        hbm=2,
        scratch=[
            pltpu.VMEM((2,) + tokens.shape, bf16),
            wide_rows,
            pltpu.SemaphoreType.DMA((2,)),
        ],
    )

    ahead_of = [(i, (i + 1) % chips) for i in range(chips)]
    behind_of = [(i, (i - 1) % chips) for i in range(chips)]
    targets = jnp.stack([(chip + s) % chips for s in range(chips)]).astype(jnp.int32)
    here, ahead, behind, far_up, far_down = call(
        pack_kernel,
        [(2 * wide, hidden)] * 3 + [(wide, hidden)] * 2,
        targets,
        up_weight,
        down_weight,
        hbm=2,
        scratch=[pltpu.SemaphoreType.DMA((chips * (wide // LANES + 1),))],
    )
    swap = [(0, 1), (1, 0)]
    far_up = lax.ppermute(far_up, "chip", ahead_of)
    far_down = lax.ppermute(far_down, "chip", behind_of)
    ahead = lax.ppermute(ahead, "chip", ahead_of)
    behind = lax.ppermute(behind, "chip", behind_of)
    here_too = lax.ppermute(here, "core", swap)
    recv = lax.all_to_all(sent, "node", split_axis=0, concat_axis=0, tiled=True)
    recv, here_too, ahead, behind, far_up, far_down = lax.optimization_barrier(
        (recv, here_too, ahead, behind, far_up, far_down)
    )
    far_up = lax.ppermute(far_up, "chip", ahead_of)
    far_down = lax.ppermute(far_down, "chip", behind_of)
    blocks = [here, here_too]
    for block in (ahead, behind, far_up, far_down):
        blocks += [block, lax.ppermute(block, "core", swap)]
    scalars = jnp.stack(
        [expert, chip, (chip + chips - 1) % chips, (chip + 1) % chips, (chip + 2) % chips]
    ).astype(jnp.int32)

    used = jnp.any(recv[:, 2 * width // LANES, :] > 0, 1)
    rank = jnp.cumsum(used.astype(jnp.int32)) - 1
    slot = jnp.arange(pairs, dtype=jnp.int32)
    pick = ((rank[None, :] == slot[:, None]) & used[None, :]).astype(bf16)
    mine = dot(pick, recv.reshape(nodes, -1), ((1,), (0,))).astype(bf16)
    parts = jnp.stack(
        [
            jnp.concatenate(
                [
                    mine[:, m * wide : (m + 1) * wide],
                    mine[:, width + m * wide : width + (m + 1) * wide],
                    mine[:, 2 * width : 2 * width + LANES],
                ],
                1,
            )
            for m in range(chips)
        ]
    )
    spread = jnp.broadcast_to(parts[None], (experts,) + parts.shape).reshape(
        experts * chips, pairs, -1
    )
    rows = lax.all_to_all(
        spread, ("expert", "chip"), split_axis=0, concat_axis=0, tiled=True
    ).reshape(experts * chips * pairs, -1)
    gate = jnp.sum(
        jnp.where(lane[None, :] == expert, rows[:, 2 * wide :].astype(f32), 0.0), 1, keepdims=True
    )

    units = CORES * hidden
    (outgoing,) = call(
        partial_kernel, [(chips, rows.shape[0], 2 * units)], scalars, rows, *blocks
    )
    incoming = lax.all_to_all(outgoing, "chip", split_axis=0, concat_axis=0, tiled=True)
    both = jnp.sum(incoming.astype(f32), 0)
    pre = both[:, :units]
    back = both[:, units:]
    sig = jax.nn.sigmoid(pre)
    active = (pre * sig).astype(bf16)
    grad_pre = (gate * back * sig * (1.0 + pre * (1.0 - sig))).astype(bf16)
    every = lax.all_gather(jnp.concatenate([active, grad_pre], 1), "chip", axis=0)

    (result,) = call(output_kernel, [rows.shape], scalars, rows, every, *blocks)

    parts_back = lax.all_to_all(
        result.reshape(experts * chips, pairs, -1),
        ("expert", "chip"),
        split_axis=0,
        concat_axis=0,
        tiled=True,
    ).reshape(experts, chips, pairs, -1)
    summed = jnp.sum(parts_back.astype(f32), 0)
    inner_all = jnp.sum(summed[:, :, 2 * wide :], 0)
    full = jnp.concatenate(
        [summed[m, :, :wide] for m in range(chips)]
        + [summed[m, :, wide : 2 * wide] for m in range(chips)]
        + [inner_all],
        1,
    ).astype(bf16)
    expanded = dot(pick, full, ((0,), (0,))).astype(bf16)
    expanded = jnp.pad(expanded, ((0, 0), (0, 7 * LANES))).reshape(nodes, -1, LANES)
    home = lax.all_to_all(expanded, "node", split_axis=0, concat_axis=0, tiled=True)

    mixed, grad_tokens, grad_gates = call(
        home_kernel,
        [tokens.shape, tokens.shape, choices.shape],
        (groups, choices),
        home,
        scratch=[wide_rows],
    )
    return mixed, grad_tokens, grad_gates.transpose(2, 0, 1)


def solution(mesh):
    nodes, members = mesh.devices.shape
    axes = ("node", "expert", "chip", "core")
    fine = Mesh(
        mesh.devices.reshape(nodes, EXPERTS, members // (EXPERTS * CORES), CORES), axes
    )
    placed = (
        P(axes, None),
        P(axes, None),
        P(axes, None),
        P(axes, None, None),
        P(axes, None, None),
        P(None, axes),
        P(axes, None),
    )
    return jax.shard_map(
        per_device,
        mesh=fine,
        in_specs=placed,
        out_specs=(P(axes, None), P(axes, None), P(axes, None, None)),
        check_vma=False,
    )
```

```python
import jax
import jax.numpy as jnp
from jax import lax
from jax.experimental import pallas as pl
from jax.experimental.pallas import tpu as pltpu
from jax.sharding import Mesh, PartitionSpec as P

EXPERTS = 4
CORES = 2
LANES = 128


def dot(a, b, dims):
    return lax.dot_general(a, b, (dims, ((), ())), preferred_element_type=jnp.float32)


def small_copies(pairs, sems):
    copies = [pltpu.make_async_copy(a, b, sems.at[i]) for i, (a, b) in enumerate(pairs)]
    for copy in copies:
        copy.start()
    return copies


def send_kernel(
    gates, groups_at, choices_at, tokens, cotangent, out, groups, choices, narrow, wide, sems
):
    count, width = tokens.shape
    chunks = width // LANES
    first, second, *copies = small_copies(
        [
            (groups_at, groups),
            (choices_at, choices),
            (tokens, narrow.at[0]),
            (cotangent, narrow.at[1]),
        ],
        sems,
    )
    out[...] = jnp.zeros_like(out)
    first.wait()
    second.wait()
    every_gate = gates[...].astype(jnp.float32)
    row = lax.broadcasted_iota(jnp.int32, (8, LANES), 0)
    lane = lax.broadcasted_iota(jnp.int32, (8, LANES), 1)
    i, j = (lax.broadcasted_iota(jnp.int32, (2, count), d) for d in range(2))
    for t in range(count):
        for c in range(2):
            table = jnp.zeros((8, LANES), jnp.float32)
            for k in range(2):
                gate = jnp.sum(jnp.where((i == k) & (j == t), every_gate[c], 0.0), keepdims=True)
                table += jnp.where((row == 0) & (lane == choices[c, k, t]), gate, 0.0)
            out[groups[c, t], 2 * chunks :, :] = table.astype(out.dtype)
    for i, copy in enumerate(copies):
        copy.wait()
        for j in range(chunks):
            wide[:, i * chunks + j, :] = narrow[i, :, j * LANES : (j + 1) * LANES].astype(
                jnp.float32
            )
    for t in range(count):
        rows = wide[t].astype(out.dtype)
        for c in range(2):
            out[groups[c, t], : 2 * chunks, :] = rows


def home_kernel(
    home, groups_at, choices_at, mixed, grad_tokens, grad_gates, groups, choices, wide, sems
):
    count, width = mixed.shape
    chunks = width // LANES
    row = lax.broadcasted_iota(jnp.int32, (8, LANES), 0)
    lane = lax.broadcasted_iota(jnp.int32, (8, LANES), 1)
    i, j = (lax.broadcasted_iota(jnp.int32, (2, count), d) for d in range(2))
    inner = [jnp.zeros((2, count), jnp.float32) for c in range(2)]
    for copy in small_copies([(groups_at, groups), (choices_at, choices)], sems):
        copy.wait()
    for t in range(count):
        total = jnp.zeros((2 * chunks, LANES), jnp.float32)
        for c in range(2):
            node = groups[c, t]
            total += home[node, : 2 * chunks, :].astype(jnp.float32)
            table = home[node, 2 * chunks :, :].astype(jnp.float32)
            for k in range(2):
                value = jnp.sum(
                    jnp.where((row == 0) & (lane == choices[c, k, t]), table, 0.0), keepdims=True
                )
                inner[c] = jnp.where((i == k) & (j == t), value, inner[c])
        wide[t] = total
    for c in range(2):
        grad_gates[c] = inner[c].astype(grad_gates.dtype)
    for j in range(chunks):
        at = pl.ds(j * LANES, LANES)
        mixed[:, at] = wide[:, j, :].astype(mixed.dtype)
        grad_tokens[:, at] = wide[:, chunks + j, :].astype(grad_tokens.dtype)


def pack_kernel(chips, up, down, here, ahead, behind, far_up, far_down, sems):
    wide = far_up.shape[0]
    copies = []

    def rows(chip, out, at):
        start = pl.multiple_of(chips[chip] * wide, wide)
        copies.append(
            pltpu.make_async_copy(
                up.at[pl.ds(start, wide)], out.at[pl.ds(at, wide)], sems.at[len(copies)]
            )
        )

    def columns(chip, out, at):
        start = pl.multiple_of(chips[chip] * wide, wide)
        for j in range(0, wide, LANES):
            copies.append(
                pltpu.make_async_copy(
                    down.at[:, pl.ds(start + j, LANES)],
                    out.at[pl.ds(at + j, LANES)],
                    sems.at[len(copies)],
                )
            )

    for chip, out in ((1, ahead), (3, behind), (0, here)):
        rows(chip, out, 0)
        columns(chip, out, wide)
    rows(2, far_up, 0)
    columns(2, far_down, 0)
    for copy in copies:
        copy.start()
    for copy in copies:
        copy.wait()


def pieces(refs, wide):
    whole = [(ref.at[pl.ds(0, wide)], ref.at[pl.ds(wide, wide)]) for ref in refs[:-4]]
    return whole + [(refs[-4], refs[-2]), (refs[-3], refs[-1])]


def chip_sums(rows, pair, out):
    wide = pair[0][0].shape[0]
    units = out.shape[1] // 2
    up = jnp.concatenate([u[...] for u, _ in pair], 1)
    out[:, :units] = dot(rows[:, :wide], up, ((1,), (0,))).astype(out.dtype)
    down = jnp.concatenate(
        [
            jnp.concatenate([d[j : j + LANES, :] for _, d in pair], 0)
            for j in range(0, wide, LANES)
        ],
        1,
    )
    out[:, units:] = dot(rows[:, wide : 2 * wide], down, ((1,), (1,))).astype(out.dtype)


def near_kernel(scalars, rows, *refs):
    blocks, (out, sums, sems) = refs[:-3], refs[-3:]
    wide = (rows.shape[1] - LANES) // 2
    halves = [(ref.at[pl.ds(0, wide)], ref.at[pl.ds(wide, wide)]) for ref in blocks]
    copies = []
    for i in range(len(blocks) // CORES):
        chip_sums(rows, halves[CORES * i : CORES * (i + 1)], sums.at[i])
        copies.append(pltpu.make_async_copy(sums.at[i], out.at[scalars[1 + i]], sems.at[i]))
        copies[-1].start()
    for copy in copies:
        copy.wait()


def far_kernel(scalars, rows, up, up_too, down, down_too, sums, out, block, sem):
    chip_sums(rows, [(up, down), (up_too, down_too)], block)
    copy = pltpu.make_async_copy(block, out.at[scalars[4]], sem)
    copy.start()
    copy.wait()


def output_kernel(scalars, rows, every, *refs):
    result = refs[-1]
    hidden = refs[0].shape[1]
    wide = (rows.shape[1] - LANES) // 2
    blocks = pieces(refs[:-1], wide)
    chips = len(blocks) // CORES
    count = rows.shape[0]
    lane = lax.broadcasted_iota(jnp.int32, (count, LANES), 1)
    mine = lane == scalars[0]
    gate = jnp.sum(
        jnp.where(mine, rows[:, 2 * wide :].astype(jnp.float32), 0.0), 1, keepdims=True
    )
    active = jnp.concatenate(
        [every[scalars[1 + i], :, : CORES * hidden] for i in range(chips)], 1
    )
    grad_pre = jnp.concatenate(
        [every[scalars[1 + i], :, CORES * hidden :] for i in range(chips)], 1
    )
    inner = jnp.zeros((count, 1), jnp.float32)
    step = 2 * LANES
    for j in range(0, wide, step):
        down = jnp.concatenate(
            [
                jnp.concatenate([d[j + k : j + k + LANES, :] for _, d in blocks], 0)
                for k in range(0, step, LANES)
            ],
            1,
        )
        up = jnp.concatenate([u[j : j + step, :] for u, _ in blocks], 1)
        out = dot(active, down, ((1,), (0,)))
        inner += jnp.sum(
            out * rows[:, wide + j : wide + j + step].astype(jnp.float32), 1, keepdims=True
        )
        result[:, j : j + step] = (gate * out).astype(result.dtype)
        result[:, wide + j : wide + j + step] = dot(grad_pre, up, ((1,), (1,))).astype(
            result.dtype
        )
    inner = jnp.where(gate > 0, inner, 0.0)
    result[:, 2 * wide :] = jnp.where(mine, inner, 0.0).astype(result.dtype)


def call(kernel, shapes, scalars, *operands, hbm=0, scratch=(), aliases=None, out_any=False):
    small, near, far = (
        pl.BlockSpec(memory_space=space) for space in (pltpu.SMEM, pltpu.VMEM, pltpu.HBM)
    )
    count = len(operands) - hbm
    scalars = scalars if isinstance(scalars, tuple) else (scalars,)
    scalars = [pltpu.with_memory_space_constraint(v, pltpu.SMEM) for v in scalars]
    held = operands[count:]
    if out_any:
        far = pl.BlockSpec(memory_space=pl.ANY)
    else:
        held = [pltpu.with_memory_space_constraint(v, pltpu.HBM) for v in held]
    return pl.pallas_call(
        kernel,
        out_shape=[jax.ShapeDtypeStruct(shape, jnp.bfloat16) for shape in shapes],
        in_specs=[small] * len(scalars) + [near] * count + [far] * hbm,
        out_specs=[far if out_any else near] * len(shapes),
        scratch_shapes=scratch,
        input_output_aliases=aliases or {},
        compiler_params=pltpu.CompilerParams(vmem_limit_bytes=20 * 2**20),
    )(*scalars, *operands[:count], *held)


def per_device(tokens, cotangent, groups, choices, gates, up_weight, down_weight):
    f32, bf16 = jnp.float32, jnp.bfloat16
    tok_count, width = tokens.shape
    nodes = lax.axis_size("node")
    experts = lax.axis_size("expert")
    chips = lax.axis_size("chip")
    hidden = up_weight.shape[1]
    pairs = 2 * tok_count
    wide = width // chips
    expert = lax.axis_index("expert")
    chip = lax.axis_index("chip")
    lane = jnp.arange(LANES, dtype=jnp.int32)

    slot_rows = 2 * width // LANES
    groups, choices = groups.T, choices.transpose(1, 2, 0)
    tables = [pltpu.SMEM(v.shape, jnp.int32) for v in (groups, choices)]
    wide_rows = pltpu.VMEM((tok_count, slot_rows, LANES), f32)
    (sent,) = call(
        send_kernel,
        [(nodes, slot_rows + 8, LANES)],
        (),
        gates.transpose(1, 2, 0),
        groups,
        choices,
        tokens,
        cotangent,
        hbm=4,
        scratch=[
            *tables,
            pltpu.VMEM((2,) + tokens.shape, bf16),
            wide_rows,
            pltpu.SemaphoreType.DMA((4,)),
        ],
    )

    ahead_of = [(i, (i + 1) % chips) for i in range(chips)]
    behind_of = [(i, (i - 1) % chips) for i in range(chips)]
    targets = jnp.stack([(chip + s) % chips for s in range(chips)]).astype(jnp.int32)
    here, ahead, behind, far_up, far_down = call(
        pack_kernel,
        [(2 * wide, hidden)] * 3 + [(wide, hidden)] * 2,
        targets,
        up_weight,
        down_weight,
        hbm=2,
        scratch=[pltpu.SemaphoreType.DMA((chips * (wide // LANES + 1),))],
    )
    swap = [(0, 1), (1, 0)]
    far_up = lax.ppermute(far_up, "chip", ahead_of)
    far_down = lax.ppermute(far_down, "chip", behind_of)
    ahead = lax.ppermute(ahead, "chip", ahead_of)
    behind = lax.ppermute(behind, "chip", behind_of)
    here_too = lax.ppermute(here, "core", swap)
    recv = lax.all_to_all(sent, "node", split_axis=0, concat_axis=0, tiled=True)
    recv, here_too, ahead, behind, far_up, far_down = lax.optimization_barrier(
        (recv, here_too, ahead, behind, far_up, far_down)
    )
    far_up = lax.ppermute(far_up, "chip", ahead_of)
    far_down = lax.ppermute(far_down, "chip", behind_of)
    near = [here, here_too]
    for block in (ahead, behind):
        near += [block, lax.ppermute(block, "core", swap)]
    scalars = jnp.stack(
        [expert, chip, (chip + chips - 1) % chips, (chip + 1) % chips, (chip + 2) % chips]
    ).astype(jnp.int32)

    used = jnp.any(recv[:, 2 * width // LANES, :] > 0, 1)
    rank = jnp.cumsum(used.astype(jnp.int32)) - 1
    slot = jnp.arange(pairs, dtype=jnp.int32)
    pick = ((rank[None, :] == slot[:, None]) & used[None, :]).astype(bf16)
    mine = dot(pick, recv.reshape(nodes, -1), ((1,), (0,))).astype(bf16)
    parts = jnp.stack(
        [
            jnp.concatenate(
                [
                    mine[:, m * wide : (m + 1) * wide],
                    mine[:, width + m * wide : width + (m + 1) * wide],
                    mine[:, 2 * width : 2 * width + LANES],
                ],
                1,
            )
            for m in range(chips)
        ]
    )
    spread = jnp.broadcast_to(parts[None], (experts,) + parts.shape).reshape(
        experts * chips, pairs, -1
    )
    rows = lax.all_to_all(
        spread, ("expert", "chip"), split_axis=0, concat_axis=0, tiled=True
    ).reshape(experts * chips * pairs, -1)
    rows, far_up, far_down = lax.optimization_barrier((rows, far_up, far_down))
    far = []
    for block in (far_up, far_down):
        far += [block, lax.ppermute(block, "core", swap)]
    gate = jnp.sum(
        jnp.where(lane[None, :] == expert, rows[:, 2 * wide :].astype(f32), 0.0), 1, keepdims=True
    )

    units = CORES * hidden
    (outgoing,) = call(
        near_kernel,
        [(chips, rows.shape[0], 2 * units)],
        scalars,
        rows,
        *near,
        scratch=[
            pltpu.VMEM((chips - 1, rows.shape[0], 2 * units), bf16),
            pltpu.SemaphoreType.DMA((chips - 1,)),
        ],
        out_any=True,
    )
    (outgoing,) = call(
        far_kernel,
        [outgoing.shape],
        scalars,
        rows,
        *far,
        outgoing,
        hbm=1,
        scratch=[pltpu.VMEM(outgoing.shape[1:], bf16), pltpu.SemaphoreType.DMA],
        aliases={6: 0},
        out_any=True,
    )
    incoming = lax.all_to_all(outgoing, "chip", split_axis=0, concat_axis=0, tiled=True)
    both = jnp.sum(incoming.astype(f32), 0)
    pre = both[:, :units]
    back = both[:, units:]
    sig = jax.nn.sigmoid(pre)
    active = (pre * sig).astype(bf16)
    grad_pre = (gate * back * sig * (1.0 + pre * (1.0 - sig))).astype(bf16)
    every = lax.all_gather(jnp.concatenate([active, grad_pre], 1), "chip", axis=0)

    (result,) = call(output_kernel, [rows.shape], scalars, rows, every, *near, *far)

    parts_back = lax.all_to_all(
        result.reshape(experts * chips, pairs, -1),
        ("expert", "chip"),
        split_axis=0,
        concat_axis=0,
        tiled=True,
    ).reshape(experts, chips, pairs, -1)
    summed = jnp.sum(parts_back.astype(f32), 0)
    inner_all = jnp.sum(summed[:, :, 2 * wide :], 0)
    full = jnp.concatenate(
        [summed[m, :, :wide] for m in range(chips)]
        + [summed[m, :, wide : 2 * wide] for m in range(chips)]
        + [inner_all],
        1,
    ).astype(bf16)
    expanded = dot(pick, full, ((0,), (0,))).astype(bf16)
    expanded = jnp.pad(expanded, ((0, 0), (0, 7 * LANES))).reshape(nodes, -1, LANES)
    home = lax.all_to_all(expanded, "node", split_axis=0, concat_axis=0, tiled=True)

    mixed, grad_tokens, grad_gates = call(
        home_kernel,
        [tokens.shape, tokens.shape, choices.shape],
        (),
        home,
        groups,
        choices,
        hbm=2,
        scratch=[*tables, wide_rows, pltpu.SemaphoreType.DMA((2,))],
    )
    return mixed, grad_tokens, grad_gates.transpose(2, 0, 1)


def solution(mesh):
    nodes, members = mesh.devices.shape
    axes = ("node", "expert", "chip", "core")
    fine = Mesh(
        mesh.devices.reshape(nodes, EXPERTS, members // (EXPERTS * CORES), CORES), axes
    )
    placed = (
        P(axes, None),
        P(axes, None),
        P(axes, None),
        P(axes, None, None),
        P(axes, None, None),
        P(None, axes),
        P(axes, None),
    )
    return jax.shard_map(
        per_device,
        mesh=fine,
        in_specs=placed,
        out_specs=(P(axes, None), P(axes, None), P(axes, None, None)),
        check_vma=False,
    )
```

```python
import jax
import jax.numpy as jnp
from jax import lax
from jax.experimental import pallas as pl
from jax.experimental.pallas import tpu as pltpu
from jax.sharding import Mesh, PartitionSpec as P

EXPERTS = 4
CORES = 2
SIDES = 2
LANES = 128


def dot(a, b, dims):
    return lax.dot_general(a, b, (dims, ((), ())), preferred_element_type=jnp.float32)


def small_copies(pairs, sems):
    copies = [pltpu.make_async_copy(a, b, sems.at[i]) for i, (a, b) in enumerate(pairs)]
    for copy in copies:
        copy.start()
    return copies


def send_kernel(
    gates, groups_at, choices_at, tokens, cotangent, out, groups, choices, narrow, wide, sems
):
    count, width = tokens.shape
    chunks = width // LANES
    first, second, *copies = small_copies(
        [
            (groups_at, groups),
            (choices_at, choices),
            (tokens, narrow.at[0]),
            (cotangent, narrow.at[1]),
        ],
        sems,
    )
    out[...] = jnp.zeros_like(out)
    first.wait()
    second.wait()
    every_gate = gates[...].astype(jnp.float32)
    row = lax.broadcasted_iota(jnp.int32, (8, LANES), 0)
    lane = lax.broadcasted_iota(jnp.int32, (8, LANES), 1)
    i, j = (lax.broadcasted_iota(jnp.int32, (2, count), d) for d in range(2))
    for t in range(count):
        for c in range(2):
            table = jnp.zeros((8, LANES), jnp.float32)
            for k in range(2):
                gate = jnp.sum(jnp.where((i == k) & (j == t), every_gate[c], 0.0), keepdims=True)
                table += jnp.where((row == 0) & (lane == choices[c, k, t]), gate, 0.0)
            out[groups[c, t], 2 * chunks :, :] = table.astype(out.dtype)
    for i, copy in enumerate(copies):
        copy.wait()
        for j in range(chunks):
            wide[:, i * chunks + j, :] = narrow[i, :, j * LANES : (j + 1) * LANES].astype(
                jnp.float32
            )
    for t in range(count):
        rows = wide[t].astype(out.dtype)
        for c in range(2):
            out[groups[c, t], : 2 * chunks, :] = rows


def home_kernel(
    home, groups_at, choices_at, mixed, grad_tokens, grad_gates, groups, choices, wide, sems
):
    count, width = mixed.shape
    chunks = width // LANES
    row = lax.broadcasted_iota(jnp.int32, (8, LANES), 0)
    lane = lax.broadcasted_iota(jnp.int32, (8, LANES), 1)
    i, j = (lax.broadcasted_iota(jnp.int32, (2, count), d) for d in range(2))
    inner = [jnp.zeros((2, count), jnp.float32) for c in range(2)]
    for copy in small_copies([(groups_at, groups), (choices_at, choices)], sems):
        copy.wait()
    for t in range(count):
        total = jnp.zeros((2 * chunks, LANES), jnp.float32)
        for c in range(2):
            node = groups[c, t]
            total += home[node, : 2 * chunks, :].astype(jnp.float32)
            table = home[node, 2 * chunks :, :].astype(jnp.float32)
            for k in range(2):
                value = jnp.sum(
                    jnp.where((row == 0) & (lane == choices[c, k, t]), table, 0.0), keepdims=True
                )
                inner[c] = jnp.where((i == k) & (j == t), value, inner[c])
        wide[t] = total
    for c in range(2):
        grad_gates[c] = inner[c].astype(grad_gates.dtype)
    for j in range(chunks):
        at = pl.ds(j * LANES, LANES)
        mixed[:, at] = wide[:, j, :].astype(mixed.dtype)
        grad_tokens[:, at] = wide[:, chunks + j, :].astype(grad_tokens.dtype)


def pack_kernel(sides, up, down, here, give_up, give_down, sems):
    half = give_up.shape[0]
    copies = []
    for i, (rows, tiles) in enumerate(
        ((give_up, give_down), (here.at[pl.ds(0, half)], here.at[pl.ds(half, half)]))
    ):
        start = pl.multiple_of(sides[1 - i] * half, half)
        copies.append((up.at[pl.ds(start, half)], rows))
        for j in range(0, half, LANES):
            copies.append((down.at[:, pl.ds(start + j, LANES)], tiles.at[pl.ds(j, LANES)]))
    for copy in small_copies(copies, sems):
        copy.wait()


def chip_sums(rows, pair, out):
    half = pair[0][0].shape[0]
    units = out.shape[1] // 2
    up = jnp.concatenate([u[...] for u, _ in pair], 1)
    out[:, :units] = dot(rows[:, :half], up, ((1,), (0,))).astype(out.dtype)
    down = jnp.concatenate(
        [
            jnp.concatenate([d[j : j + LANES, :] for _, d in pair], 0)
            for j in range(0, half, LANES)
        ],
        1,
    )
    out[:, units:] = dot(rows[:, half : 2 * half], down, ((1,), (1,))).astype(out.dtype)


def halves(refs):
    half = refs[0].shape[0] // 2
    return [(ref.at[pl.ds(0, half)], ref.at[pl.ds(half, half)]) for ref in refs]


def own_kernel(rows, here, here_too, out):
    chip_sums(rows, halves((here, here_too)), out)


def partner_kernel(rows, up, up_too, down, down_too, out):
    chip_sums(rows, [(up, down), (up_too, down_too)], out)


def output_kernel(scalars, rows, own, partner, here, here_too, up, up_too, down, down_too, result):
    blocks = halves((here, here_too)) + [(up, down), (up_too, down_too)]
    half = up.shape[0]
    units = own.shape[1] // 2
    count = rows.shape[0]
    lane = lax.broadcasted_iota(jnp.int32, (count, LANES), 1)
    mine = lane == scalars[0]
    gate = jnp.sum(
        jnp.where(mine, rows[:, 2 * half :].astype(jnp.float32), 0.0), 1, keepdims=True
    )
    active = jnp.concatenate([own[:, :units], partner[:, :units]], 1)
    grad_pre = jnp.concatenate([own[:, units:], partner[:, units:]], 1)
    inner = jnp.zeros((count, 1), jnp.float32)
    step = 2 * LANES
    for j in range(0, half, step):
        tiles = jnp.concatenate(
            [
                jnp.concatenate([d[j + k : j + k + LANES, :] for _, d in blocks], 0)
                for k in range(0, step, LANES)
            ],
            1,
        )
        ups = jnp.concatenate([u[j : j + step, :] for u, _ in blocks], 1)
        out = dot(active, tiles, ((1,), (0,)))
        inner += jnp.sum(
            out * rows[:, half + j : half + j + step].astype(jnp.float32), 1, keepdims=True
        )
        result[:, j : j + step] = (gate * out).astype(result.dtype)
        result[:, half + j : half + j + step] = dot(grad_pre, ups, ((1,), (1,))).astype(
            result.dtype
        )
    inner = jnp.where(gate > 0, inner, 0.0)
    result[:, 2 * half :] = jnp.where(mine, inner, 0.0).astype(result.dtype)


def call(kernel, shapes, scalars, *operands, hbm=0, scratch=(), dtype=jnp.bfloat16):
    small, near, far = (
        pl.BlockSpec(memory_space=space) for space in (pltpu.SMEM, pltpu.VMEM, pltpu.HBM)
    )
    count = len(operands) - hbm
    held = [pltpu.with_memory_space_constraint(v, pltpu.HBM) for v in operands[count:]]
    return pl.pallas_call(
        kernel,
        out_shape=[jax.ShapeDtypeStruct(shape, dtype) for shape in shapes],
        in_specs=[small] * len(scalars) + [near] * count + [far] * hbm,
        out_specs=[near] * len(shapes),
        scratch_shapes=scratch,
        compiler_params=pltpu.CompilerParams(vmem_limit_bytes=24 * 2**20),
    )(*scalars, *operands[:count], *held)


def per_device(tokens, cotangent, groups, choices, gates, up_weight, down_weight):
    f32, bf16 = jnp.float32, jnp.bfloat16
    tok_count, width = tokens.shape
    nodes = lax.axis_size("node")
    experts = lax.axis_size("expert")
    couples = lax.axis_size("pair")
    sides = lax.axis_size("side")
    group = ("expert", "pair", "side")
    hidden = up_weight.shape[1]
    pairs = 2 * tok_count
    half = width // sides
    expert = lax.axis_index("expert")
    side = lax.axis_index("side")
    lane = jnp.arange(LANES, dtype=jnp.int32)

    slot_rows = 2 * width // LANES
    groups, choices = groups.T, choices.transpose(1, 2, 0)
    tables = [pltpu.SMEM(v.shape, jnp.int32) for v in (groups, choices)]
    wide_rows = pltpu.VMEM((tok_count, slot_rows, LANES), f32)
    (sent,) = call(
        send_kernel,
        [(nodes, slot_rows + 8, LANES)],
        (),
        gates.transpose(1, 2, 0),
        groups,
        choices,
        tokens,
        cotangent,
        hbm=4,
        scratch=[
            *tables,
            pltpu.VMEM((2,) + tokens.shape, bf16),
            wide_rows,
            pltpu.SemaphoreType.DMA((4,)),
        ],
    )

    swap = [(0, 1), (1, 0)]
    here, give_up, give_down = call(
        pack_kernel,
        [(2 * half, hidden), (half, hidden), (half, hidden)],
        (jnp.stack([side, 1 - side]).astype(jnp.int32),),
        up_weight,
        down_weight,
        hbm=2,
        scratch=[pltpu.SemaphoreType.DMA((sides * (half // LANES + 1),))],
    )
    up = lax.ppermute(give_up, "side", swap)
    here_too = lax.ppermute(here, "core", swap)
    recv = lax.all_to_all(sent, "node", split_axis=0, concat_axis=0, tiled=True)
    recv, up, here_too = lax.optimization_barrier((recv, up, here_too))
    down = lax.ppermute(give_down, "side", swap)
    up_too = lax.ppermute(up, "core", swap)

    used = jnp.any(recv[:, 2 * width // LANES, :] > 0, 1)
    rank = jnp.cumsum(used.astype(jnp.int32)) - 1
    slot = jnp.arange(pairs, dtype=jnp.int32)
    pick = ((rank[None, :] == slot[:, None]) & used[None, :]).astype(bf16)
    mine = dot(pick, recv.reshape(nodes, -1), ((1,), (0,))).astype(bf16)
    parts = jnp.stack(
        [
            jnp.concatenate(
                [
                    mine[:, m * half : (m + 1) * half],
                    mine[:, width + m * half : width + (m + 1) * half],
                    mine[:, 2 * width : 2 * width + LANES],
                ],
                1,
            )
            for m in range(sides)
        ]
    )
    spread = jnp.broadcast_to(parts[None], (experts * couples,) + parts.shape).reshape(
        experts * couples * sides, pairs, -1
    )
    rows = lax.all_to_all(spread, group, split_axis=0, concat_axis=0, tiled=True)
    rows, down = lax.optimization_barrier((rows, down))
    down_too = lax.ppermute(down, "core", swap)
    rows = rows.reshape(experts * couples * sides * pairs, -1)
    gate = jnp.sum(
        jnp.where(lane[None, :] == expert, rows[:, 2 * half :].astype(f32), 0.0), 1, keepdims=True
    )

    units = CORES * hidden
    sums_shape = (rows.shape[0], 2 * units)
    (outgoing,) = call(partner_kernel, [sums_shape], (), rows, up, up_too, down, down_too)
    incoming = lax.ppermute(outgoing, "side", swap)
    (both,) = call(own_kernel, [sums_shape], (), rows, here, here_too, dtype=f32)
    both = both + incoming.astype(f32)
    pre = both[:, :units]
    back = both[:, units:]
    sig = jax.nn.sigmoid(pre)
    active = (pre * sig).astype(bf16)
    grad_pre = (gate * back * sig * (1.0 + pre * (1.0 - sig))).astype(bf16)
    own = jnp.concatenate([active, grad_pre], 1)
    partner = lax.ppermute(own, "side", swap)

    (result,) = call(
        output_kernel,
        [rows.shape],
        (expert.astype(jnp.int32).reshape(1),),
        rows,
        own,
        partner,
        here,
        here_too,
        up,
        up_too,
        down,
        down_too,
    )

    parts_back = lax.all_to_all(
        result.reshape(experts * couples * sides, pairs, -1),
        group,
        split_axis=0,
        concat_axis=0,
        tiled=True,
    ).reshape(experts * couples, sides, pairs, -1)
    summed = jnp.sum(parts_back.astype(f32), 0)
    inner_all = jnp.sum(summed[:, :, 2 * half :], 0)
    full = jnp.concatenate(
        [summed[m, :, :half] for m in range(sides)]
        + [summed[m, :, half : 2 * half] for m in range(sides)]
        + [inner_all],
        1,
    ).astype(bf16)
    expanded = dot(pick, full, ((0,), (0,))).astype(bf16)
    expanded = jnp.pad(expanded, ((0, 0), (0, 7 * LANES))).reshape(nodes, -1, LANES)
    home = lax.all_to_all(expanded, "node", split_axis=0, concat_axis=0, tiled=True)

    mixed, grad_tokens, grad_gates = call(
        home_kernel,
        [tokens.shape, tokens.shape, choices.shape],
        (),
        home,
        groups,
        choices,
        hbm=2,
        scratch=[*tables, wide_rows, pltpu.SemaphoreType.DMA((2,))],
    )
    return mixed, grad_tokens, grad_gates.transpose(2, 0, 1)


def solution(mesh):
    nodes, members = mesh.devices.shape
    axes = ("node", "expert", "pair", "side", "core")
    couples = members // (EXPERTS * SIDES * CORES)
    fine = Mesh(mesh.devices.reshape(nodes, EXPERTS, couples, SIDES, CORES), axes)
    placed = (
        P(axes, None),
        P(axes, None),
        P(axes, None),
        P(axes, None, None),
        P(axes, None, None),
        P(None, axes),
        P(axes, None),
    )
    return jax.shard_map(
        per_device,
        mesh=fine,
        in_specs=placed,
        out_specs=(P(axes, None), P(axes, None), P(axes, None, None)),
        check_vma=False,
    )
```

```python
import jax
import jax.numpy as jnp
from jax import lax
from jax.experimental import pallas as pl
from jax.experimental.pallas import tpu as pltpu
from jax.sharding import Mesh, PartitionSpec as P

EXPERTS = 4
CORES = 2
LANES = 128


def dot(a, b, dims):
    return lax.dot_general(a, b, (dims, ((), ())), preferred_element_type=jnp.float32)


def small_copies(pairs, sems):
    copies = [pltpu.make_async_copy(a, b, sems.at[i]) for i, (a, b) in enumerate(pairs)]
    for copy in copies:
        copy.start()
    return copies


def send_kernel(
    gates, groups_at, choices_at, tokens, cotangent, out, groups, choices, narrow, wide, sems
):
    count, width = tokens.shape
    chunks = width // LANES
    first, second, *copies = small_copies(
        [
            (groups_at, groups),
            (choices_at, choices),
            (tokens, narrow.at[0]),
            (cotangent, narrow.at[1]),
        ],
        sems,
    )
    out[...] = jnp.zeros_like(out)
    first.wait()
    second.wait()
    every_gate = gates[...].astype(jnp.float32)
    row = lax.broadcasted_iota(jnp.int32, (8, LANES), 0)
    lane = lax.broadcasted_iota(jnp.int32, (8, LANES), 1)
    i, j = (lax.broadcasted_iota(jnp.int32, (2, count), d) for d in range(2))
    for t in range(count):
        for c in range(2):
            table = jnp.zeros((8, LANES), jnp.float32)
            for k in range(2):
                gate = jnp.sum(jnp.where((i == k) & (j == t), every_gate[c], 0.0), keepdims=True)
                table += jnp.where((row == 0) & (lane == choices[c, k, t]), gate, 0.0)
            out[groups[c, t], 2 * chunks :, :] = table.astype(out.dtype)
    for i, copy in enumerate(copies):
        copy.wait()
        for j in range(chunks):
            wide[:, i * chunks + j, :] = narrow[i, :, j * LANES : (j + 1) * LANES].astype(
                jnp.float32
            )
    for t in range(count):
        rows = wide[t].astype(out.dtype)
        for c in range(2):
            out[groups[c, t], : 2 * chunks, :] = rows


def home_kernel(
    home, groups_at, choices_at, mixed, grad_tokens, grad_gates, groups, choices, wide, sems
):
    count, width = mixed.shape
    chunks = width // LANES
    row = lax.broadcasted_iota(jnp.int32, (8, LANES), 0)
    lane = lax.broadcasted_iota(jnp.int32, (8, LANES), 1)
    i, j = (lax.broadcasted_iota(jnp.int32, (2, count), d) for d in range(2))
    inner = [jnp.zeros((2, count), jnp.float32) for c in range(2)]
    for copy in small_copies([(groups_at, groups), (choices_at, choices)], sems):
        copy.wait()
    for t in range(count):
        total = jnp.zeros((2 * chunks, LANES), jnp.float32)
        for c in range(2):
            node = groups[c, t]
            total += home[node, : 2 * chunks, :].astype(jnp.float32)
            table = home[node, 2 * chunks :, :].astype(jnp.float32)
            for k in range(2):
                value = jnp.sum(
                    jnp.where((row == 0) & (lane == choices[c, k, t]), table, 0.0), keepdims=True
                )
                inner[c] = jnp.where((i == k) & (j == t), value, inner[c])
        wide[t] = total
    for c in range(2):
        grad_gates[c] = inner[c].astype(grad_gates.dtype)
    for j in range(chunks):
        at = pl.ds(j * LANES, LANES)
        mixed[:, at] = wide[:, j, :].astype(mixed.dtype)
        grad_tokens[:, at] = wide[:, chunks + j, :].astype(grad_tokens.dtype)


def pack_kernel(chips, up, down, here, ahead, behind, far_up, far_down, sems):
    wide = far_up.shape[0]
    copies = []

    def rows(chip, out, at):
        start = pl.multiple_of(chips[chip] * wide, wide)
        copies.append(
            pltpu.make_async_copy(
                up.at[pl.ds(start, wide)], out.at[pl.ds(at, wide)], sems.at[len(copies)]
            )
        )

    def columns(chip, out, at):
        start = pl.multiple_of(chips[chip] * wide, wide)
        for j in range(0, wide, LANES):
            copies.append(
                pltpu.make_async_copy(
                    down.at[:, pl.ds(start + j, LANES)],
                    out.at[pl.ds(at + j, LANES)],
                    sems.at[len(copies)],
                )
            )

    for chip, out in ((1, ahead), (3, behind), (0, here)):
        rows(chip, out, 0)
        columns(chip, out, wide)
    rows(2, far_up, 0)
    columns(2, far_down, 0)
    for copy in copies:
        copy.start()
    for copy in copies:
        copy.wait()


def merge_kernel(ahead, behind, far_up, far_down, out, sems):
    at = 0
    copies = []
    for ref in (ahead, behind, far_up, far_down):
        copies.append((ref, out.at[pl.ds(at, ref.shape[0])]))
        at += ref.shape[0]
    for copy in small_copies(copies, sems):
        copy.wait()


def pieces(refs):
    here, here_too, ahead, behind, far_up, far_down, merged = refs
    wide = far_up.shape[0]
    found = []
    for i, own in enumerate((here, ahead, behind, None)):
        other, start = (merged, 2 * (i - 1) * wide) if i else (here_too, 0)
        found += [
            (own.at[pl.ds(0, wide)], own.at[pl.ds(wide, wide)]) if own is not None else (far_up, far_down),
            (other.at[pl.ds(start, wide)], other.at[pl.ds(start + wide, wide)]),
        ]
    return found


def partial_kernel(scalars, rows, *refs):
    blocks, out = pieces(refs[:-1]), refs[-1]
    hidden = refs[0].shape[1]
    wide = (rows.shape[1] - LANES) // 2
    x, dy = rows[:, :wide], rows[:, wide : 2 * wide]
    for i in range(len(blocks) // CORES):
        pair = blocks[CORES * i : CORES * (i + 1)]
        at = scalars[1 + i]
        up = jnp.concatenate([u[...] for u, _ in pair], 1)
        out[at, :, : CORES * hidden] = dot(x, up, ((1,), (0,))).astype(out.dtype)
        down = jnp.concatenate(
            [
                jnp.concatenate([d[j : j + LANES, :] for _, d in pair], 0)
                for j in range(0, wide, LANES)
            ],
            1,
        )
        out[at, :, CORES * hidden :] = dot(dy, down, ((1,), (1,))).astype(out.dtype)


def output_kernel(scalars, rows, every, *refs):
    result = refs[-1]
    hidden = refs[0].shape[1]
    wide = (rows.shape[1] - LANES) // 2
    blocks = pieces(refs[:-1])
    chips = len(blocks) // CORES
    count = rows.shape[0]
    lane = lax.broadcasted_iota(jnp.int32, (count, LANES), 1)
    mine = lane == scalars[0]
    gate = jnp.sum(
        jnp.where(mine, rows[:, 2 * wide :].astype(jnp.float32), 0.0), 1, keepdims=True
    )
    active = jnp.concatenate(
        [every[scalars[1 + i], :, : CORES * hidden] for i in range(chips)], 1
    )
    grad_pre = jnp.concatenate(
        [every[scalars[1 + i], :, CORES * hidden :] for i in range(chips)], 1
    )
    inner = jnp.zeros((count, 1), jnp.float32)
    step = 2 * LANES
    for j in range(0, wide, step):
        down = jnp.concatenate(
            [
                jnp.concatenate([d[j + k : j + k + LANES, :] for _, d in blocks], 0)
                for k in range(0, step, LANES)
            ],
            1,
        )
        up = jnp.concatenate([u[j : j + step, :] for u, _ in blocks], 1)
        out = dot(active, down, ((1,), (0,)))
        inner += jnp.sum(
            out * rows[:, wide + j : wide + j + step].astype(jnp.float32), 1, keepdims=True
        )
        result[:, j : j + step] = (gate * out).astype(result.dtype)
        result[:, wide + j : wide + j + step] = dot(grad_pre, up, ((1,), (1,))).astype(
            result.dtype
        )
    inner = jnp.where(gate > 0, inner, 0.0)
    result[:, 2 * wide :] = jnp.where(mine, inner, 0.0).astype(result.dtype)


def call(kernel, shapes, scalars, *operands, hbm=0, scratch=()):
    small, near, far = (
        pl.BlockSpec(memory_space=space) for space in (pltpu.SMEM, pltpu.VMEM, pltpu.HBM)
    )
    count = len(operands) - hbm
    held = [pltpu.with_memory_space_constraint(v, pltpu.HBM) for v in operands[count:]]
    return pl.pallas_call(
        kernel,
        out_shape=[jax.ShapeDtypeStruct(shape, jnp.bfloat16) for shape in shapes],
        in_specs=[small] * len(scalars) + [near] * count + [far] * hbm,
        out_specs=[near] * len(shapes),
        scratch_shapes=scratch,
        compiler_params=pltpu.CompilerParams(vmem_limit_bytes=24 * 2**20),
    )(*scalars, *operands[:count], *held)


def per_device(tokens, cotangent, groups, choices, gates, up_weight, down_weight):
    f32, bf16 = jnp.float32, jnp.bfloat16
    tok_count, width = tokens.shape
    nodes = lax.axis_size("node")
    experts = lax.axis_size("expert")
    chips = lax.axis_size("chip")
    hidden = up_weight.shape[1]
    pairs = 2 * tok_count
    wide = width // chips
    expert = lax.axis_index("expert")
    chip = lax.axis_index("chip")
    lane = jnp.arange(LANES, dtype=jnp.int32)

    slot_rows = 2 * width // LANES
    groups, choices = groups.T, choices.transpose(1, 2, 0)
    tables = [pltpu.SMEM(v.shape, jnp.int32) for v in (groups, choices)]
    wide_rows = pltpu.VMEM((tok_count, slot_rows, LANES), f32)
    (sent,) = call(
        send_kernel,
        [(nodes, slot_rows + 8, LANES)],
        (),
        gates.transpose(1, 2, 0),
        groups,
        choices,
        tokens,
        cotangent,
        hbm=4,
        scratch=[
            *tables,
            pltpu.VMEM((2,) + tokens.shape, bf16),
            wide_rows,
            pltpu.SemaphoreType.DMA((4,)),
        ],
    )

    ahead_of = [(i, (i + 1) % chips) for i in range(chips)]
    behind_of = [(i, (i - 1) % chips) for i in range(chips)]
    targets = jnp.stack([(chip + s) % chips for s in range(chips)]).astype(jnp.int32)
    here, ahead, behind, far_up, far_down = call(
        pack_kernel,
        [(2 * wide, hidden)] * 3 + [(wide, hidden)] * 2,
        (targets,),
        up_weight,
        down_weight,
        hbm=2,
        scratch=[pltpu.SemaphoreType.DMA((chips * (wide // LANES + 1),))],
    )
    swap = [(0, 1), (1, 0)]
    far_up = lax.ppermute(far_up, "chip", ahead_of)
    far_down = lax.ppermute(far_down, "chip", behind_of)
    ahead = lax.ppermute(ahead, "chip", ahead_of)
    behind = lax.ppermute(behind, "chip", behind_of)
    here_too = lax.ppermute(here, "core", swap)
    recv = lax.all_to_all(sent, "node", split_axis=0, concat_axis=0, tiled=True)
    far_up = lax.ppermute(far_up, "chip", ahead_of)
    far_down = lax.ppermute(far_down, "chip", behind_of)
    recv, here_too, ahead, behind, far_up, far_down = lax.optimization_barrier(
        (recv, here_too, ahead, behind, far_up, far_down)
    )
    (merged,) = call(
        merge_kernel,
        [(2 * (chips - 1) * wide, hidden)],
        (),
        ahead,
        behind,
        far_up,
        far_down,
        scratch=[pltpu.SemaphoreType.DMA((4,))],
    )
    merged = lax.ppermute(merged, "core", swap)
    blocks = (here, here_too, ahead, behind, far_up, far_down, merged)
    scalars = jnp.stack(
        [expert, chip, (chip + chips - 1) % chips, (chip + 1) % chips, (chip + 2) % chips]
    ).astype(jnp.int32)

    used = jnp.any(recv[:, 2 * width // LANES, :] > 0, 1)
    rank = jnp.cumsum(used.astype(jnp.int32)) - 1
    slot = jnp.arange(pairs, dtype=jnp.int32)
    pick = ((rank[None, :] == slot[:, None]) & used[None, :]).astype(bf16)
    mine = dot(pick, recv.reshape(nodes, -1), ((1,), (0,))).astype(bf16)
    parts = jnp.stack(
        [
            jnp.concatenate(
                [
                    mine[:, m * wide : (m + 1) * wide],
                    mine[:, width + m * wide : width + (m + 1) * wide],
                    mine[:, 2 * width : 2 * width + LANES],
                ],
                1,
            )
            for m in range(chips)
        ]
    )
    spread = jnp.broadcast_to(parts[None], (experts,) + parts.shape).reshape(
        experts * chips, pairs, -1
    )
    rows = lax.all_to_all(
        spread, ("expert", "chip"), split_axis=0, concat_axis=0, tiled=True
    ).reshape(experts * chips * pairs, -1)
    gate = jnp.sum(
        jnp.where(lane[None, :] == expert, rows[:, 2 * wide :].astype(f32), 0.0), 1, keepdims=True
    )

    units = CORES * hidden
    (outgoing,) = call(
        partial_kernel, [(chips, rows.shape[0], 2 * units)], (scalars,), rows, *blocks
    )
    incoming = lax.all_to_all(outgoing, "chip", split_axis=0, concat_axis=0, tiled=True)
    both = jnp.sum(incoming.astype(f32), 0)
    pre = both[:, :units]
    back = both[:, units:]
    sig = jax.nn.sigmoid(pre)
    active = (pre * sig).astype(bf16)
    grad_pre = (gate * back * sig * (1.0 + pre * (1.0 - sig))).astype(bf16)
    every = lax.all_gather(jnp.concatenate([active, grad_pre], 1), "chip", axis=0)

    (result,) = call(output_kernel, [rows.shape], (scalars,), rows, every, *blocks)

    parts_back = lax.all_to_all(
        result.reshape(experts * chips, pairs, -1),
        ("expert", "chip"),
        split_axis=0,
        concat_axis=0,
        tiled=True,
    ).reshape(experts, chips, pairs, -1)
    summed = jnp.sum(parts_back.astype(f32), 0)
    inner_all = jnp.sum(summed[:, :, 2 * wide :], 0)
    full = jnp.concatenate(
        [summed[m, :, :wide] for m in range(chips)]
        + [summed[m, :, wide : 2 * wide] for m in range(chips)]
        + [inner_all],
        1,
    ).astype(bf16)
    expanded = dot(pick, full, ((0,), (0,))).astype(bf16)
    expanded = jnp.pad(expanded, ((0, 0), (0, 7 * LANES))).reshape(nodes, -1, LANES)
    home = lax.all_to_all(expanded, "node", split_axis=0, concat_axis=0, tiled=True)

    mixed, grad_tokens, grad_gates = call(
        home_kernel,
        [tokens.shape, tokens.shape, choices.shape],
        (),
        home,
        groups,
        choices,
        hbm=2,
        scratch=[*tables, wide_rows, pltpu.SemaphoreType.DMA((2,))],
    )
    return mixed, grad_tokens, grad_gates.transpose(2, 0, 1)


def solution(mesh):
    nodes, members = mesh.devices.shape
    axes = ("node", "expert", "chip", "core")
    fine = Mesh(
        mesh.devices.reshape(nodes, EXPERTS, members // (EXPERTS * CORES), CORES), axes
    )
    placed = (
        P(axes, None),
        P(axes, None),
        P(axes, None),
        P(axes, None, None),
        P(axes, None, None),
        P(None, axes),
        P(axes, None),
    )
    return jax.shard_map(
        per_device,
        mesh=fine,
        in_specs=placed,
        out_specs=(P(axes, None), P(axes, None), P(axes, None, None)),
        check_vma=False,
    )
```

```python
import jax
import jax.numpy as jnp
from jax import lax
from jax.experimental import pallas as pl
from jax.experimental.pallas import tpu as pltpu
from jax.sharding import Mesh, PartitionSpec as P

EXPERTS = 4
CORES = 2
LANES = 128


def dot(a, b, dims):
    return lax.dot_general(a, b, (dims, ((), ())), preferred_element_type=jnp.float32)


def small_copies(pairs, sems):
    copies = [pltpu.make_async_copy(a, b, sems.at[i]) for i, (a, b) in enumerate(pairs)]
    for copy in copies:
        copy.start()
    return copies


def send_kernel(
    gates, groups_at, choices_at, tokens, cotangent, out, groups, choices, narrow, wide, sems
):
    count, width = tokens.shape
    chunks = width // LANES
    first, second, *copies = small_copies(
        [
            (groups_at, groups),
            (choices_at, choices),
            (tokens, narrow.at[0]),
            (cotangent, narrow.at[1]),
        ],
        sems,
    )
    out[...] = jnp.zeros_like(out)
    first.wait()
    second.wait()
    every_gate = gates[...].astype(jnp.float32)
    row = lax.broadcasted_iota(jnp.int32, (8, LANES), 0)
    lane = lax.broadcasted_iota(jnp.int32, (8, LANES), 1)
    i, j = (lax.broadcasted_iota(jnp.int32, (2, count), d) for d in range(2))
    for t in range(count):
        for c in range(2):
            table = jnp.zeros((8, LANES), jnp.float32)
            for k in range(2):
                gate = jnp.sum(jnp.where((i == k) & (j == t), every_gate[c], 0.0), keepdims=True)
                table += jnp.where((row == 0) & (lane == choices[c, k, t]), gate, 0.0)
            out[groups[c, t], 2 * chunks :, :] = table.astype(out.dtype)
    for i, copy in enumerate(copies):
        copy.wait()
        for j in range(chunks):
            wide[:, i * chunks + j, :] = narrow[i, :, j * LANES : (j + 1) * LANES].astype(
                jnp.float32
            )
    for t in range(count):
        rows = wide[t].astype(out.dtype)
        for c in range(2):
            out[groups[c, t], : 2 * chunks, :] = rows


def home_kernel(
    home, groups_at, choices_at, mixed, grad_tokens, grad_gates, groups, choices, wide, sems
):
    count, width = mixed.shape
    chunks = width // LANES
    row = lax.broadcasted_iota(jnp.int32, (8, LANES), 0)
    lane = lax.broadcasted_iota(jnp.int32, (8, LANES), 1)
    i, j = (lax.broadcasted_iota(jnp.int32, (2, count), d) for d in range(2))
    inner = [jnp.zeros((2, count), jnp.float32) for c in range(2)]
    for copy in small_copies([(groups_at, groups), (choices_at, choices)], sems):
        copy.wait()
    for t in range(count):
        total = jnp.zeros((2 * chunks, LANES), jnp.float32)
        for c in range(2):
            node = groups[c, t]
            total += home[node, : 2 * chunks, :].astype(jnp.float32)
            table = home[node, 2 * chunks :, :].astype(jnp.float32)
            for k in range(2):
                value = jnp.sum(
                    jnp.where((row == 0) & (lane == choices[c, k, t]), table, 0.0), keepdims=True
                )
                inner[c] = jnp.where((i == k) & (j == t), value, inner[c])
        wide[t] = total
    for c in range(2):
        grad_gates[c] = inner[c].astype(grad_gates.dtype)
    for j in range(chunks):
        at = pl.ds(j * LANES, LANES)
        mixed[:, at] = wide[:, j, :].astype(mixed.dtype)
        grad_tokens[:, at] = wide[:, chunks + j, :].astype(grad_tokens.dtype)


def pack_kernel(chips, up, down, here, ahead, behind, far_up, far_down, sems):
    wide = far_up.shape[0]
    copies = []

    def rows(chip, out, at):
        start = pl.multiple_of(chips[chip] * wide, wide)
        copies.append(
            pltpu.make_async_copy(
                up.at[pl.ds(start, wide)], out.at[pl.ds(at, wide)], sems.at[len(copies)]
            )
        )

    def columns(chip, out, at):
        start = pl.multiple_of(chips[chip] * wide, wide)
        for j in range(0, wide, LANES):
            copies.append(
                pltpu.make_async_copy(
                    down.at[:, pl.ds(start + j, LANES)],
                    out.at[pl.ds(at + j, LANES)],
                    sems.at[len(copies)],
                )
            )

    for chip, out in ((1, ahead), (3, behind), (0, here)):
        rows(chip, out, 0)
        columns(chip, out, wide)
    rows(2, far_up, 0)
    columns(2, far_down, 0)
    for copy in copies:
        copy.start()
    for copy in copies:
        copy.wait()


def fetch(refs, held, sems, cuts):
    wide = held.shape[1] // 2
    halves = [(ref.at[pl.ds(0, wide)], ref.at[pl.ds(wide, wide)]) for ref in refs[:-4]]
    halves += [(refs[-4], refs[-3]), (refs[-2], refs[-1])]
    found = []
    for k, (low, high) in enumerate(zip((0,) + cuts, cuts + (wide,))):
        at = pl.ds(low, high - low)
        found.append(
            [
                [
                    pltpu.make_async_copy(
                        ref.at[at],
                        held.at[i, pl.ds(half * wide + low, high - low)],
                        sems.at[k, i, half],
                    )
                    for half, ref in enumerate(pair)
                ]
                for i, pair in enumerate(halves)
            ]
        )
    for cut in found:
        for pair in cut:
            for copy in pair:
                copy.start()
    return found


def partial_kernel(scalars, rows, *refs):
    *blocks, out, held, sems = refs
    count, _, hidden = held.shape
    wide = held.shape[1] // 2
    (copies,) = fetch(blocks, held, sems, ())
    x, dy = rows[:, :wide], rows[:, wide : 2 * wide]
    for i in range(count // CORES):
        pair = range(CORES * i, CORES * (i + 1))
        for m in pair:
            for copy in copies[m]:
                copy.wait()
        at = scalars[1 + i]
        up = jnp.concatenate([held[m, :wide, :] for m in pair], 1)
        out[at, :, : CORES * hidden] = dot(x, up, ((1,), (0,))).astype(out.dtype)
        down = jnp.concatenate(
            [
                jnp.concatenate([held[m, wide + j : wide + j + LANES, :] for m in pair], 0)
                for j in range(0, wide, LANES)
            ],
            1,
        )
        out[at, :, CORES * hidden :] = dot(dy, down, ((1,), (1,))).astype(out.dtype)


def output_kernel(scalars, rows, every, *refs):
    *blocks, result, held, sems = refs
    many, _, hidden = held.shape
    wide = held.shape[1] // 2
    step = 2 * LANES
    cut = (wide // step // 2 + 1) * step
    copies = fetch(blocks, held, sems, (cut,))
    chips = many // CORES
    count = rows.shape[0]
    lane = lax.broadcasted_iota(jnp.int32, (count, LANES), 1)
    mine = lane == scalars[0]
    gate = jnp.sum(
        jnp.where(mine, rows[:, 2 * wide :].astype(jnp.float32), 0.0), 1, keepdims=True
    )
    active = jnp.concatenate(
        [every[scalars[1 + i], :, : CORES * hidden] for i in range(chips)], 1
    )
    grad_pre = jnp.concatenate(
        [every[scalars[1 + i], :, CORES * hidden :] for i in range(chips)], 1
    )
    inner = jnp.zeros((count, 1), jnp.float32)
    for j in range(0, wide, step):
        if j in (0, cut):
            for pair in copies[j // cut]:
                for copy in pair:
                    copy.wait()
        down = jnp.concatenate(
            [
                jnp.concatenate(
                    [held[m, wide + j + k : wide + j + k + LANES, :] for m in range(many)], 0
                )
                for k in range(0, step, LANES)
            ],
            1,
        )
        up = jnp.concatenate([held[m, j : j + step, :] for m in range(many)], 1)
        out = dot(active, down, ((1,), (0,)))
        inner += jnp.sum(
            out * rows[:, wide + j : wide + j + step].astype(jnp.float32), 1, keepdims=True
        )
        result[:, j : j + step] = (gate * out).astype(result.dtype)
        result[:, wide + j : wide + j + step] = dot(grad_pre, up, ((1,), (1,))).astype(
            result.dtype
        )
    inner = jnp.where(gate > 0, inner, 0.0)
    result[:, 2 * wide :] = jnp.where(mine, inner, 0.0).astype(result.dtype)


def call(kernel, shapes, scalars, *operands, hbm=0, scratch=(), out_hbm=False, loose=0):
    small, near, far = (
        pl.BlockSpec(memory_space=space) for space in (pltpu.SMEM, pltpu.VMEM, pltpu.HBM)
    )
    count = len(operands) - hbm
    fixed = len(operands) - loose
    held = [pltpu.with_memory_space_constraint(v, pltpu.HBM) for v in operands[count:fixed]]
    held += operands[fixed:]
    anywhere = pl.BlockSpec(memory_space=pl.ANY)
    return pl.pallas_call(
        kernel,
        out_shape=[jax.ShapeDtypeStruct(shape, jnp.bfloat16) for shape in shapes],
        in_specs=[small] * len(scalars) + [near] * count + [far] * (hbm - loose) + [anywhere] * loose,
        out_specs=[far if out_hbm else near] * len(shapes),
        scratch_shapes=scratch,
        compiler_params=pltpu.CompilerParams(vmem_limit_bytes=24 * 2**20),
    )(*scalars, *operands[:count], *held)


def per_device(tokens, cotangent, groups, choices, gates, up_weight, down_weight):
    f32, bf16 = jnp.float32, jnp.bfloat16
    tok_count, width = tokens.shape
    nodes = lax.axis_size("node")
    experts = lax.axis_size("expert")
    chips = lax.axis_size("chip")
    hidden = up_weight.shape[1]
    pairs = 2 * tok_count
    wide = width // chips
    expert = lax.axis_index("expert")
    chip = lax.axis_index("chip")
    lane = jnp.arange(LANES, dtype=jnp.int32)

    slot_rows = 2 * width // LANES
    groups, choices = groups.T, choices.transpose(1, 2, 0)
    tables = [pltpu.SMEM(v.shape, jnp.int32) for v in (groups, choices)]
    wide_rows = pltpu.VMEM((tok_count, slot_rows, LANES), f32)
    (sent,) = call(
        send_kernel,
        [(nodes, slot_rows + 8, LANES)],
        (),
        gates.transpose(1, 2, 0),
        groups,
        choices,
        tokens,
        cotangent,
        hbm=4,
        scratch=[
            *tables,
            pltpu.VMEM((2,) + tokens.shape, bf16),
            wide_rows,
            pltpu.SemaphoreType.DMA((4,)),
        ],
    )

    ahead_of = [(i, (i + 1) % chips) for i in range(chips)]
    behind_of = [(i, (i - 1) % chips) for i in range(chips)]
    targets = jnp.stack([(chip + s) % chips for s in range(chips)]).astype(jnp.int32)
    here, ahead, behind, far_up, far_down = call(
        pack_kernel,
        [(2 * wide, hidden)] * 3 + [(wide, hidden)] * 2,
        (targets,),
        up_weight,
        down_weight,
        hbm=2,
        scratch=[pltpu.SemaphoreType.DMA((chips * (wide // LANES + 1),))],
        out_hbm=True,
    )
    here, ahead, behind, far_up, far_down, sent = lax.optimization_barrier(
        (here, ahead, behind, far_up, far_down, sent)
    )
    swap = [(0, 1), (1, 0)]
    far_up = lax.ppermute(far_up, "chip", ahead_of)
    far_down = lax.ppermute(far_down, "chip", behind_of)
    ahead = lax.ppermute(ahead, "chip", ahead_of)
    behind = lax.ppermute(behind, "chip", behind_of)
    here_too = lax.ppermute(here, "core", swap)
    far_up = lax.ppermute(far_up, "chip", ahead_of)
    far_down = lax.ppermute(far_down, "chip", behind_of)
    near = (here, here_too)
    for block in (ahead, behind):
        near += (block, lax.ppermute(block, "core", swap))
    recv = lax.all_to_all(sent, "node", split_axis=0, concat_axis=0, tiled=True)
    recv, near, far_up, far_down = lax.optimization_barrier((recv, near, far_up, far_down))
    blocks = near + (far_up, far_down)
    for block in (far_up, far_down):
        blocks += (lax.ppermute(block, "core", swap),)
    held = [
        pltpu.VMEM((chips * CORES, 2 * wide, hidden), bf16),
        pltpu.SemaphoreType.DMA((2, chips * CORES, 2)),
    ]
    scalars = jnp.stack(
        [expert, chip, (chip + chips - 1) % chips, (chip + 1) % chips, (chip + 2) % chips]
    ).astype(jnp.int32)

    used = jnp.any(recv[:, 2 * width // LANES, :] > 0, 1)
    rank = jnp.cumsum(used.astype(jnp.int32)) - 1
    slot = jnp.arange(pairs, dtype=jnp.int32)
    pick = ((rank[None, :] == slot[:, None]) & used[None, :]).astype(bf16)
    mine = dot(pick, recv.reshape(nodes, -1), ((1,), (0,))).astype(bf16)
    parts = jnp.stack(
        [
            jnp.concatenate(
                [
                    mine[:, m * wide : (m + 1) * wide],
                    mine[:, width + m * wide : width + (m + 1) * wide],
                    mine[:, 2 * width : 2 * width + LANES],
                ],
                1,
            )
            for m in range(chips)
        ]
    )
    spread = jnp.broadcast_to(parts[None], (experts,) + parts.shape).reshape(
        experts * chips, pairs, -1
    )
    rows = lax.all_to_all(
        spread, ("expert", "chip"), split_axis=0, concat_axis=0, tiled=True
    ).reshape(experts * chips * pairs, -1)
    gate = jnp.sum(
        jnp.where(lane[None, :] == expert, rows[:, 2 * wide :].astype(f32), 0.0), 1, keepdims=True
    )

    units = CORES * hidden
    (outgoing,) = call(
        partial_kernel,
        [(chips, rows.shape[0], 2 * units)],
        (scalars,),
        rows,
        *blocks,
        hbm=len(blocks),
        loose=2,
        scratch=held,
    )
    incoming = lax.all_to_all(outgoing, "chip", split_axis=0, concat_axis=0, tiled=True)
    both = jnp.sum(incoming.astype(f32), 0)
    pre = both[:, :units]
    back = both[:, units:]
    sig = jax.nn.sigmoid(pre)
    active = (pre * sig).astype(bf16)
    grad_pre = (gate * back * sig * (1.0 + pre * (1.0 - sig))).astype(bf16)
    every = lax.all_gather(jnp.concatenate([active, grad_pre], 1), "chip", axis=0)

    (result,) = call(
        output_kernel,
        [rows.shape],
        (scalars,),
        rows,
        every,
        *blocks,
        hbm=len(blocks),
        loose=2,
        scratch=held,
    )

    parts_back = lax.all_to_all(
        result.reshape(experts * chips, pairs, -1),
        ("expert", "chip"),
        split_axis=0,
        concat_axis=0,
        tiled=True,
    ).reshape(experts, chips, pairs, -1)
    summed = jnp.sum(parts_back.astype(f32), 0)
    inner_all = jnp.sum(summed[:, :, 2 * wide :], 0)
    full = jnp.concatenate(
        [summed[m, :, :wide] for m in range(chips)]
        + [summed[m, :, wide : 2 * wide] for m in range(chips)]
        + [inner_all],
        1,
    ).astype(bf16)
    expanded = dot(pick, full, ((0,), (0,))).astype(bf16)
    expanded = jnp.pad(expanded, ((0, 0), (0, 7 * LANES))).reshape(nodes, -1, LANES)
    home = lax.all_to_all(expanded, "node", split_axis=0, concat_axis=0, tiled=True)

    mixed, grad_tokens, grad_gates = call(
        home_kernel,
        [tokens.shape, tokens.shape, choices.shape],
        (),
        home,
        groups,
        choices,
        hbm=2,
        scratch=[*tables, wide_rows, pltpu.SemaphoreType.DMA((2,))],
    )
    return mixed, grad_tokens, grad_gates.transpose(2, 0, 1)


def solution(mesh):
    nodes, members = mesh.devices.shape
    axes = ("node", "expert", "chip", "core")
    fine = Mesh(
        mesh.devices.reshape(nodes, EXPERTS, members // (EXPERTS * CORES), CORES), axes
    )
    placed = (
        P(axes, None),
        P(axes, None),
        P(axes, None),
        P(axes, None, None),
        P(axes, None, None),
        P(None, axes),
        P(axes, None),
    )
    return jax.shard_map(
        per_device,
        mesh=fine,
        in_specs=placed,
        out_specs=(P(axes, None), P(axes, None), P(axes, None, None)),
        check_vma=False,
    )
```

```python
import jax
import jax.numpy as jnp
from jax import lax
from jax.experimental import pallas as pl
from jax.experimental.pallas import tpu as pltpu
from jax.sharding import Mesh, PartitionSpec as P

EXPERTS = 4
CORES = 2
LANES = 128


def dot(a, b, dims):
    return lax.dot_general(a, b, (dims, ((), ())), preferred_element_type=jnp.float32)


def small_copies(pairs, sems):
    copies = [pltpu.make_async_copy(a, b, sems.at[i]) for i, (a, b) in enumerate(pairs)]
    for copy in copies:
        copy.start()
    return copies


def send_kernel(
    gates, groups_at, choices_at, tokens, cotangent, out, groups, choices, narrow, wide, sems
):
    count, width = tokens.shape
    chunks = width // LANES
    first, second, *copies = small_copies(
        [
            (groups_at, groups),
            (choices_at, choices),
            (tokens, narrow.at[0]),
            (cotangent, narrow.at[1]),
        ],
        sems,
    )
    out[...] = jnp.zeros_like(out)
    first.wait()
    second.wait()
    every_gate = gates[...].astype(jnp.float32)
    row = lax.broadcasted_iota(jnp.int32, (8, LANES), 0)
    lane = lax.broadcasted_iota(jnp.int32, (8, LANES), 1)
    i, j = (lax.broadcasted_iota(jnp.int32, (2, count), d) for d in range(2))
    for t in range(count):
        for c in range(2):
            table = jnp.zeros((8, LANES), jnp.float32)
            for k in range(2):
                gate = jnp.sum(jnp.where((i == k) & (j == t), every_gate[c], 0.0), keepdims=True)
                table += jnp.where((row == 0) & (lane == choices[c, k, t]), gate, 0.0)
            out[groups[c, t], 2 * chunks :, :] = table.astype(out.dtype)
    for i, copy in enumerate(copies):
        copy.wait()
        for j in range(chunks):
            wide[:, i * chunks + j, :] = narrow[i, :, j * LANES : (j + 1) * LANES].astype(
                jnp.float32
            )
    for t in range(count):
        rows = wide[t].astype(out.dtype)
        for c in range(2):
            out[groups[c, t], : 2 * chunks, :] = rows


def home_kernel(
    home, groups_at, choices_at, mixed, grad_tokens, grad_gates, groups, choices, wide, sems
):
    count, width = mixed.shape
    chunks = width // LANES
    row = lax.broadcasted_iota(jnp.int32, (8, LANES), 0)
    lane = lax.broadcasted_iota(jnp.int32, (8, LANES), 1)
    i, j = (lax.broadcasted_iota(jnp.int32, (2, count), d) for d in range(2))
    inner = [jnp.zeros((2, count), jnp.float32) for c in range(2)]
    for copy in small_copies([(groups_at, groups), (choices_at, choices)], sems):
        copy.wait()
    for t in range(count):
        total = jnp.zeros((2 * chunks, LANES), jnp.float32)
        for c in range(2):
            node = groups[c, t]
            total += home[node, : 2 * chunks, :].astype(jnp.float32)
            table = home[node, 2 * chunks :, :].astype(jnp.float32)
            for k in range(2):
                value = jnp.sum(
                    jnp.where((row == 0) & (lane == choices[c, k, t]), table, 0.0), keepdims=True
                )
                inner[c] = jnp.where((i == k) & (j == t), value, inner[c])
        wide[t] = total
    for c in range(2):
        grad_gates[c] = inner[c].astype(grad_gates.dtype)
    for j in range(chunks):
        at = pl.ds(j * LANES, LANES)
        mixed[:, at] = wide[:, j, :].astype(mixed.dtype)
        grad_tokens[:, at] = wide[:, chunks + j, :].astype(grad_tokens.dtype)


def pack_kernel(chips, up, down, here, ahead, behind, far_up, far_down, sems):
    wide = far_up.shape[0]
    copies = []

    def rows(chip, out, at):
        start = pl.multiple_of(chips[chip] * wide, wide)
        copies.append(
            pltpu.make_async_copy(
                up.at[pl.ds(start, wide)], out.at[pl.ds(at, wide)], sems.at[len(copies)]
            )
        )

    def columns(chip, out, at):
        start = pl.multiple_of(chips[chip] * wide, wide)
        for j in range(0, wide, LANES):
            copies.append(
                pltpu.make_async_copy(
                    down.at[:, pl.ds(start + j, LANES)],
                    out.at[pl.ds(at + j, LANES)],
                    sems.at[len(copies)],
                )
            )

    for chip, out in ((1, ahead), (3, behind), (0, here)):
        rows(chip, out, 0)
        columns(chip, out, wide)
    rows(2, far_up, 0)
    columns(2, far_down, 0)
    for copy in copies:
        copy.start()
    for copy in copies:
        copy.wait()


def fetch(refs, held, sems, cuts):
    wide = held.shape[1] // 2
    halves = [(ref.at[pl.ds(0, wide)], ref.at[pl.ds(wide, wide)]) for ref in refs[:-4]]
    halves += [(refs[-4], refs[-3]), (refs[-2], refs[-1])]
    found = []
    for k, (low, high) in enumerate(zip((0,) + cuts, cuts + (wide,))):
        at = pl.ds(low, high - low)
        found.append(
            [
                [
                    pltpu.make_async_copy(
                        ref.at[at],
                        held.at[i, pl.ds(half * wide + low, high - low)],
                        sems.at[k, i, half],
                    )
                    for half, ref in enumerate(pair)
                ]
                for i, pair in enumerate(halves)
            ]
        )
    return found


def run_ahead(groups):
    for group in groups[:2]:
        for copy in group:
            copy.start()
    for i, group in enumerate(groups):
        for copy in group:
            copy.wait()
        if i + 2 < len(groups):
            for copy in groups[i + 2]:
                copy.start()
        yield


def flat(lists):
    return [item for items in lists for item in items]


def mark_kernel(scalars, *refs):
    for i in range(scalars.shape[0]):
        refs[-1][i] = scalars[i]


def mark(scalars, *arrays):
    small = pl.BlockSpec(memory_space=pltpu.SMEM)
    return pl.pallas_call(
        mark_kernel,
        out_shape=jax.ShapeDtypeStruct(scalars.shape, scalars.dtype),
        in_specs=[small] + [pl.BlockSpec(memory_space=pl.ANY)] * len(arrays),
        out_specs=small,
        cost_estimate=pl.CostEstimate(flops=10**11, bytes_accessed=4096, transcendentals=0),
    )(scalars, *arrays)


def partial_kernel(scalars, rows, *refs):
    *blocks, out, held, sems = refs
    count, _, hidden = held.shape
    wide = held.shape[1] // 2
    (copies,) = fetch(blocks, held, sems, ())
    arrived = run_ahead([flat(copies[i : i + CORES]) for i in range(0, count, CORES)])
    x, dy = rows[:, :wide], rows[:, wide : 2 * wide]
    for i in range(count // CORES):
        pair = range(CORES * i, CORES * (i + 1))
        next(arrived)
        at = scalars[1 + i]
        up = jnp.concatenate([held[m, :wide, :] for m in pair], 1)
        out[at, :, : CORES * hidden] = dot(x, up, ((1,), (0,))).astype(out.dtype)
        down = jnp.concatenate(
            [
                jnp.concatenate([held[m, wide + j : wide + j + LANES, :] for m in pair], 0)
                for j in range(0, wide, LANES)
            ],
            1,
        )
        out[at, :, CORES * hidden :] = dot(dy, down, ((1,), (1,))).astype(out.dtype)


def output_kernel(scalars, rows, every, *refs):
    *blocks, result, held, sems = refs
    many, _, hidden = held.shape
    wide = held.shape[1] // 2
    step = 2 * LANES
    cuts = tuple(range(2 * step, wide, 2 * step))
    arrived = run_ahead([flat(cut) for cut in fetch(blocks, held, sems, cuts)])
    chips = many // CORES
    count = rows.shape[0]
    lane = lax.broadcasted_iota(jnp.int32, (count, LANES), 1)
    mine = lane == scalars[0]
    gate = jnp.sum(
        jnp.where(mine, rows[:, 2 * wide :].astype(jnp.float32), 0.0), 1, keepdims=True
    )
    active = jnp.concatenate(
        [every[scalars[1 + i], :, : CORES * hidden] for i in range(chips)], 1
    )
    grad_pre = jnp.concatenate(
        [every[scalars[1 + i], :, CORES * hidden :] for i in range(chips)], 1
    )
    inner = jnp.zeros((count, 1), jnp.float32)
    for j in range(0, wide, step):
        if j == 0 or j in cuts:
            next(arrived)
        down = jnp.concatenate(
            [
                jnp.concatenate(
                    [held[m, wide + j + k : wide + j + k + LANES, :] for m in range(many)], 0
                )
                for k in range(0, step, LANES)
            ],
            1,
        )
        up = jnp.concatenate([held[m, j : j + step, :] for m in range(many)], 1)
        out = dot(active, down, ((1,), (0,)))
        inner += jnp.sum(
            out * rows[:, wide + j : wide + j + step].astype(jnp.float32), 1, keepdims=True
        )
        result[:, j : j + step] = (gate * out).astype(result.dtype)
        result[:, wide + j : wide + j + step] = dot(grad_pre, up, ((1,), (1,))).astype(
            result.dtype
        )
    inner = jnp.where(gate > 0, inner, 0.0)
    result[:, 2 * wide :] = jnp.where(mine, inner, 0.0).astype(result.dtype)


def call(kernel, shapes, scalars, *operands, hbm=0, scratch=(), out_hbm=False, loose=0):
    small, near, far = (
        pl.BlockSpec(memory_space=space) for space in (pltpu.SMEM, pltpu.VMEM, pltpu.HBM)
    )
    count = len(operands) - hbm
    fixed = len(operands) - loose
    held = [pltpu.with_memory_space_constraint(v, pltpu.HBM) for v in operands[count:fixed]]
    held += operands[fixed:]
    anywhere = pl.BlockSpec(memory_space=pl.ANY)
    return pl.pallas_call(
        kernel,
        out_shape=[jax.ShapeDtypeStruct(shape, jnp.bfloat16) for shape in shapes],
        in_specs=[small] * len(scalars) + [near] * count + [far] * (hbm - loose) + [anywhere] * loose,
        out_specs=[far if out_hbm else near] * len(shapes),
        scratch_shapes=scratch,
        compiler_params=pltpu.CompilerParams(vmem_limit_bytes=24 * 2**20),
    )(*scalars, *operands[:count], *held)


def per_device(tokens, cotangent, groups, choices, gates, up_weight, down_weight):
    f32, bf16 = jnp.float32, jnp.bfloat16
    tok_count, width = tokens.shape
    nodes = lax.axis_size("node")
    experts = lax.axis_size("expert")
    chips = lax.axis_size("chip")
    hidden = up_weight.shape[1]
    pairs = 2 * tok_count
    wide = width // chips
    expert = lax.axis_index("expert")
    chip = lax.axis_index("chip")
    lane = jnp.arange(LANES, dtype=jnp.int32)

    slot_rows = 2 * width // LANES
    groups, choices = groups.T, choices.transpose(1, 2, 0)
    tables = [pltpu.SMEM(v.shape, jnp.int32) for v in (groups, choices)]
    wide_rows = pltpu.VMEM((tok_count, slot_rows, LANES), f32)
    (sent,) = call(
        send_kernel,
        [(nodes, slot_rows + 8, LANES)],
        (),
        gates.transpose(1, 2, 0),
        groups,
        choices,
        tokens,
        cotangent,
        hbm=4,
        scratch=[
            *tables,
            pltpu.VMEM((2,) + tokens.shape, bf16),
            wide_rows,
            pltpu.SemaphoreType.DMA((4,)),
        ],
    )

    ahead_of = [(i, (i + 1) % chips) for i in range(chips)]
    behind_of = [(i, (i - 1) % chips) for i in range(chips)]
    targets = jnp.stack([(chip + s) % chips for s in range(chips)]).astype(jnp.int32)
    here, ahead, behind, far_up, far_down = call(
        pack_kernel,
        [(2 * wide, hidden)] * 3 + [(wide, hidden)] * 2,
        (targets,),
        up_weight,
        down_weight,
        hbm=2,
        scratch=[pltpu.SemaphoreType.DMA((chips * (wide // LANES + 1),))],
        out_hbm=True,
    )
    here, ahead, behind, far_up, far_down, sent = lax.optimization_barrier(
        (here, ahead, behind, far_up, far_down, sent)
    )
    swap = [(0, 1), (1, 0)]
    far_up = lax.ppermute(far_up, "chip", ahead_of)
    far_down = lax.ppermute(far_down, "chip", behind_of)
    ahead = lax.ppermute(ahead, "chip", ahead_of)
    behind = lax.ppermute(behind, "chip", behind_of)
    here_too = lax.ppermute(here, "core", swap)
    scalars = jnp.stack(
        [expert, chip, (chip + chips - 1) % chips, (chip + 1) % chips, (chip + 2) % chips]
    ).astype(jnp.int32)
    scalars = mark(scalars, ahead, behind, far_up, far_down)
    ahead, behind, far_up, far_down, scalars = lax.optimization_barrier(
        (ahead, behind, far_up, far_down, scalars)
    )
    far_up = lax.ppermute(far_up, "chip", ahead_of)
    far_down = lax.ppermute(far_down, "chip", behind_of)
    near = (here, here_too)
    for block in (ahead, behind):
        near += (block, lax.ppermute(block, "core", swap))
    recv = lax.all_to_all(sent, "node", split_axis=0, concat_axis=0, tiled=True)
    recv, near, far_up, far_down = lax.optimization_barrier((recv, near, far_up, far_down))
    blocks = near + (far_up, far_down)
    for block in (far_up, far_down):
        blocks += (lax.ppermute(block, "core", swap),)
    held = [
        pltpu.VMEM((chips * CORES, 2 * wide, hidden), bf16),
        pltpu.SemaphoreType.DMA((4, chips * CORES, 2)),
    ]
    used = jnp.any(recv[:, 2 * width // LANES, :] > 0, 1)
    rank = jnp.cumsum(used.astype(jnp.int32)) - 1
    slot = jnp.arange(pairs, dtype=jnp.int32)
    pick = ((rank[None, :] == slot[:, None]) & used[None, :]).astype(bf16)
    mine = dot(pick, recv.reshape(nodes, -1), ((1,), (0,))).astype(bf16)
    parts = jnp.stack(
        [
            jnp.concatenate(
                [
                    mine[:, m * wide : (m + 1) * wide],
                    mine[:, width + m * wide : width + (m + 1) * wide],
                    mine[:, 2 * width : 2 * width + LANES],
                ],
                1,
            )
            for m in range(chips)
        ]
    )
    spread = jnp.broadcast_to(parts[None], (experts,) + parts.shape).reshape(
        experts * chips, pairs, -1
    )
    rows = lax.all_to_all(
        spread, ("expert", "chip"), split_axis=0, concat_axis=0, tiled=True
    ).reshape(experts * chips * pairs, -1)
    gate = jnp.sum(
        jnp.where(lane[None, :] == expert, rows[:, 2 * wide :].astype(f32), 0.0), 1, keepdims=True
    )

    units = CORES * hidden
    (outgoing,) = call(
        partial_kernel,
        [(chips, rows.shape[0], 2 * units)],
        (scalars,),
        rows,
        *blocks,
        hbm=len(blocks),
        loose=2,
        scratch=held,
    )
    incoming = lax.all_to_all(outgoing, "chip", split_axis=0, concat_axis=0, tiled=True)
    both = jnp.sum(incoming.astype(f32), 0)
    pre = both[:, :units]
    back = both[:, units:]
    sig = jax.nn.sigmoid(pre)
    active = (pre * sig).astype(bf16)
    grad_pre = (gate * back * sig * (1.0 + pre * (1.0 - sig))).astype(bf16)
    every = lax.all_gather(jnp.concatenate([active, grad_pre], 1), "chip", axis=0)

    (result,) = call(
        output_kernel,
        [rows.shape],
        (scalars,),
        rows,
        every,
        *blocks,
        hbm=len(blocks),
        loose=2,
        scratch=held,
    )

    parts_back = lax.all_to_all(
        result.reshape(experts * chips, pairs, -1),
        ("expert", "chip"),
        split_axis=0,
        concat_axis=0,
        tiled=True,
    ).reshape(experts, chips, pairs, -1)
    summed = jnp.sum(parts_back.astype(f32), 0)
    inner_all = jnp.sum(summed[:, :, 2 * wide :], 0)
    full = jnp.concatenate(
        [summed[m, :, :wide] for m in range(chips)]
        + [summed[m, :, wide : 2 * wide] for m in range(chips)]
        + [inner_all],
        1,
    ).astype(bf16)
    expanded = dot(pick, full, ((0,), (0,))).astype(bf16)
    expanded = jnp.pad(expanded, ((0, 0), (0, 7 * LANES))).reshape(nodes, -1, LANES)
    home = lax.all_to_all(expanded, "node", split_axis=0, concat_axis=0, tiled=True)

    mixed, grad_tokens, grad_gates = call(
        home_kernel,
        [tokens.shape, tokens.shape, choices.shape],
        (),
        home,
        groups,
        choices,
        hbm=2,
        scratch=[*tables, wide_rows, pltpu.SemaphoreType.DMA((2,))],
    )
    return mixed, grad_tokens, grad_gates.transpose(2, 0, 1)


def solution(mesh):
    nodes, members = mesh.devices.shape
    axes = ("node", "expert", "chip", "core")
    fine = Mesh(
        mesh.devices.reshape(nodes, EXPERTS, members // (EXPERTS * CORES), CORES), axes
    )
    placed = (
        P(axes, None),
        P(axes, None),
        P(axes, None),
        P(axes, None, None),
        P(axes, None, None),
        P(None, axes),
        P(axes, None),
    )
    return jax.shard_map(
        per_device,
        mesh=fine,
        in_specs=placed,
        out_specs=(P(axes, None), P(axes, None), P(axes, None, None)),
        check_vma=False,
    )
```

```python
import jax
import jax.numpy as jnp
from jax import lax
from jax.experimental import pallas as pl
from jax.experimental.pallas import tpu as pltpu
from jax.sharding import Mesh, PartitionSpec as P

EXPERTS = 4
CORES = 2
LANES = 128


def dot(a, b, dims):
    return lax.dot_general(a, b, (dims, ((), ())), preferred_element_type=jnp.float32)


def small_copies(pairs, sems):
    copies = [pltpu.make_async_copy(a, b, sems.at[i]) for i, (a, b) in enumerate(pairs)]
    for copy in copies:
        copy.start()
    return copies


def send_kernel(
    gates, groups_at, choices_at, tokens, cotangent, out, groups, choices, narrow, wide, sems
):
    count, width = tokens.shape
    chunks = width // LANES
    first, second, *copies = small_copies(
        [
            (groups_at, groups),
            (choices_at, choices),
            (tokens, narrow.at[0]),
            (cotangent, narrow.at[1]),
        ],
        sems,
    )
    out[...] = jnp.zeros_like(out)
    first.wait()
    second.wait()
    every_gate = gates[...].astype(jnp.float32)
    row = lax.broadcasted_iota(jnp.int32, (8, LANES), 0)
    lane = lax.broadcasted_iota(jnp.int32, (8, LANES), 1)
    i, j = (lax.broadcasted_iota(jnp.int32, (2, count), d) for d in range(2))
    for t in range(count):
        for c in range(2):
            table = jnp.zeros((8, LANES), jnp.float32)
            for k in range(2):
                gate = jnp.sum(jnp.where((i == k) & (j == t), every_gate[c], 0.0), keepdims=True)
                table += jnp.where((row == 0) & (lane == choices[c, k, t]), gate, 0.0)
            out[groups[c, t], 2 * chunks :, :] = table.astype(out.dtype)
    for i, copy in enumerate(copies):
        copy.wait()
        for j in range(chunks):
            wide[:, i * chunks + j, :] = narrow[i, :, j * LANES : (j + 1) * LANES].astype(
                jnp.float32
            )
    for t in range(count):
        rows = wide[t].astype(out.dtype)
        for c in range(2):
            out[groups[c, t], : 2 * chunks, :] = rows


def home_kernel(
    home, groups_at, choices_at, mixed, grad_tokens, grad_gates, groups, choices, wide, sems
):
    count, width = mixed.shape
    chunks = width // LANES
    row = lax.broadcasted_iota(jnp.int32, (8, LANES), 0)
    lane = lax.broadcasted_iota(jnp.int32, (8, LANES), 1)
    i, j = (lax.broadcasted_iota(jnp.int32, (2, count), d) for d in range(2))
    inner = [jnp.zeros((2, count), jnp.float32) for c in range(2)]
    for copy in small_copies([(groups_at, groups), (choices_at, choices)], sems):
        copy.wait()
    for t in range(count):
        total = jnp.zeros((2 * chunks, LANES), jnp.float32)
        for c in range(2):
            node = groups[c, t]
            total += home[node, : 2 * chunks, :].astype(jnp.float32)
            table = home[node, 2 * chunks :, :].astype(jnp.float32)
            for k in range(2):
                value = jnp.sum(
                    jnp.where((row == 0) & (lane == choices[c, k, t]), table, 0.0), keepdims=True
                )
                inner[c] = jnp.where((i == k) & (j == t), value, inner[c])
        wide[t] = total
    for c in range(2):
        grad_gates[c] = inner[c].astype(grad_gates.dtype)
    for j in range(chunks):
        at = pl.ds(j * LANES, LANES)
        mixed[:, at] = wide[:, j, :].astype(mixed.dtype)
        grad_tokens[:, at] = wide[:, chunks + j, :].astype(grad_tokens.dtype)


def pack_kernel(chips, up, down, here, ahead, behind, far_up, far_down, sems):
    wide = far_up.shape[0]
    copies = []

    def rows(chip, out, at):
        start = pl.multiple_of(chips[chip] * wide, wide)
        copies.append(
            pltpu.make_async_copy(
                up.at[pl.ds(start, wide)], out.at[pl.ds(at, wide)], sems.at[len(copies)]
            )
        )

    def columns(chip, out, at):
        start = pl.multiple_of(chips[chip] * wide, wide)
        for j in range(0, wide, LANES):
            copies.append(
                pltpu.make_async_copy(
                    down.at[:, pl.ds(start + j, LANES)],
                    out.at[pl.ds(at + j, LANES)],
                    sems.at[len(copies)],
                )
            )

    for chip, out in ((1, ahead), (3, behind), (0, here)):
        rows(chip, out, 0)
        columns(chip, out, wide)
    rows(2, far_up, 0)
    columns(2, far_down, 0)
    for copy in copies:
        copy.start()
    for copy in copies:
        copy.wait()


def fetch(refs, held, sems, cuts):
    wide = held.shape[1] // 2
    halves = [(ref.at[pl.ds(0, wide)], ref.at[pl.ds(wide, wide)]) for ref in refs[:-4]]
    halves += [(refs[-4], refs[-3]), (refs[-2], refs[-1])]
    found = []
    for k, (low, high) in enumerate(zip((0,) + cuts, cuts + (wide,))):
        at = pl.ds(low, high - low)
        found.append(
            [
                [
                    pltpu.make_async_copy(
                        ref.at[at],
                        held.at[i, pl.ds(half * wide + low, high - low)],
                        sems.at[k, i, half],
                    )
                    for half, ref in enumerate(pair)
                ]
                for i, pair in enumerate(halves)
            ]
        )
    return found


def arrivals(groups):
    for group in groups:
        for copy in group:
            copy.start()
    for group in groups:
        for copy in group:
            copy.wait()
        yield


def flat(lists):
    return [item for items in lists for item in items]


def mark_kernel(scalars, *refs):
    for i in range(scalars.shape[0]):
        refs[-1][i] = scalars[i]


def mark(scalars, *arrays):
    small = pl.BlockSpec(memory_space=pltpu.SMEM)
    return pl.pallas_call(
        mark_kernel,
        out_shape=jax.ShapeDtypeStruct(scalars.shape, scalars.dtype),
        in_specs=[small] + [pl.BlockSpec(memory_space=pl.ANY)] * len(arrays),
        out_specs=small,
        cost_estimate=pl.CostEstimate(flops=10**11, bytes_accessed=4096, transcendentals=0),
    )(scalars, *arrays)


def partial_kernel(scalars, rows, *refs):
    *blocks, out, held, sems = refs
    count, _, hidden = held.shape
    wide = held.shape[1] // 2
    (copies,) = fetch(blocks, held, sems, ())
    arrived = arrivals([flat(copies[i : i + CORES]) for i in range(0, count, CORES)])
    x, dy = rows[:, :wide], rows[:, wide : 2 * wide]
    for i in range(count // CORES):
        pair = range(CORES * i, CORES * (i + 1))
        next(arrived)
        at = scalars[1 + i]
        up = jnp.concatenate([held[m, :wide, :] for m in pair], 1)
        out[at, :, : CORES * hidden] = dot(x, up, ((1,), (0,))).astype(out.dtype)
        down = jnp.concatenate(
            [
                jnp.concatenate([held[m, wide + j : wide + j + LANES, :] for m in pair], 0)
                for j in range(0, wide, LANES)
            ],
            1,
        )
        out[at, :, CORES * hidden :] = dot(dy, down, ((1,), (1,))).astype(out.dtype)


def output_kernel(scalars, rows, every, *refs):
    *blocks, result, held, sems = refs
    many, _, hidden = held.shape
    wide = held.shape[1] // 2
    step = 2 * LANES
    cuts = tuple(range(2 * step, wide, 2 * step))
    arrived = arrivals([flat(cut) for cut in fetch(blocks, held, sems, cuts)])
    chips = many // CORES
    count = rows.shape[0]
    lane = lax.broadcasted_iota(jnp.int32, (count, LANES), 1)
    mine = lane == scalars[0]
    gate = jnp.sum(
        jnp.where(mine, rows[:, 2 * wide :].astype(jnp.float32), 0.0), 1, keepdims=True
    )
    active = jnp.concatenate(
        [every[scalars[1 + i], :, : CORES * hidden] for i in range(chips)], 1
    )
    grad_pre = jnp.concatenate(
        [every[scalars[1 + i], :, CORES * hidden :] for i in range(chips)], 1
    )
    inner = jnp.zeros((count, 1), jnp.float32)
    for j in range(0, wide, step):
        if j == 0 or j in cuts:
            next(arrived)
        down = jnp.concatenate(
            [
                jnp.concatenate(
                    [held[m, wide + j + k : wide + j + k + LANES, :] for m in range(many)], 0
                )
                for k in range(0, step, LANES)
            ],
            1,
        )
        up = jnp.concatenate([held[m, j : j + step, :] for m in range(many)], 1)
        out = dot(active, down, ((1,), (0,)))
        inner += jnp.sum(
            out * rows[:, wide + j : wide + j + step].astype(jnp.float32), 1, keepdims=True
        )
        result[:, j : j + step] = (gate * out).astype(result.dtype)
        result[:, wide + j : wide + j + step] = dot(grad_pre, up, ((1,), (1,))).astype(
            result.dtype
        )
    inner = jnp.where(gate > 0, inner, 0.0)
    result[:, 2 * wide :] = jnp.where(mine, inner, 0.0).astype(result.dtype)


def call(kernel, shapes, scalars, *operands, hbm=0, scratch=(), loose=0):
    small, near, far = (
        pl.BlockSpec(memory_space=space) for space in (pltpu.SMEM, pltpu.VMEM, pltpu.HBM)
    )
    count = len(operands) - hbm
    fixed = len(operands) - loose
    held = [pltpu.with_memory_space_constraint(v, pltpu.HBM) for v in operands[count:fixed]]
    held += operands[fixed:]
    anywhere = pl.BlockSpec(memory_space=pl.ANY)
    return pl.pallas_call(
        kernel,
        out_shape=[jax.ShapeDtypeStruct(shape, jnp.bfloat16) for shape in shapes],
        in_specs=[small] * len(scalars) + [near] * count + [far] * (hbm - loose) + [anywhere] * loose,
        out_specs=[near] * len(shapes),
        scratch_shapes=scratch,
        compiler_params=pltpu.CompilerParams(vmem_limit_bytes=24 * 2**20),
    )(*scalars, *operands[:count], *held)


def per_device(tokens, cotangent, groups, choices, gates, up_weight, down_weight):
    f32, bf16 = jnp.float32, jnp.bfloat16
    tok_count, width = tokens.shape
    nodes = lax.axis_size("node")
    experts = lax.axis_size("expert")
    chips = lax.axis_size("chip")
    hidden = up_weight.shape[1]
    pairs = 2 * tok_count
    wide = width // chips
    expert = lax.axis_index("expert")
    chip = lax.axis_index("chip")
    lane = jnp.arange(LANES, dtype=jnp.int32)

    slot_rows = 2 * width // LANES
    groups, choices = groups.T, choices.transpose(1, 2, 0)
    tables = [pltpu.SMEM(v.shape, jnp.int32) for v in (groups, choices)]
    wide_rows = pltpu.VMEM((tok_count, slot_rows, LANES), f32)
    (sent,) = call(
        send_kernel,
        [(nodes, slot_rows + 8, LANES)],
        (),
        gates.transpose(1, 2, 0),
        groups,
        choices,
        tokens,
        cotangent,
        hbm=4,
        scratch=[
            *tables,
            pltpu.VMEM((2,) + tokens.shape, bf16),
            wide_rows,
            pltpu.SemaphoreType.DMA((4,)),
        ],
    )

    ahead_of = [(i, (i + 1) % chips) for i in range(chips)]
    behind_of = [(i, (i - 1) % chips) for i in range(chips)]
    targets = jnp.stack([(chip + s) % chips for s in range(chips)]).astype(jnp.int32)
    here, ahead, behind, far_up, far_down = call(
        pack_kernel,
        [(2 * wide, hidden)] * 3 + [(wide, hidden)] * 2,
        (targets,),
        up_weight,
        down_weight,
        hbm=2,
        scratch=[pltpu.SemaphoreType.DMA((chips * (wide // LANES + 1),))],
    )
    here, ahead, behind, far_up, far_down, sent = lax.optimization_barrier(
        (here, ahead, behind, far_up, far_down, sent)
    )
    swap = [(0, 1), (1, 0)]
    far_up = lax.ppermute(far_up, "chip", ahead_of)
    far_down = lax.ppermute(far_down, "chip", behind_of)
    ahead = lax.ppermute(ahead, "chip", ahead_of)
    behind = lax.ppermute(behind, "chip", behind_of)
    here_too = lax.ppermute(here, "core", swap)
    scalars = jnp.stack(
        [expert, chip, (chip + chips - 1) % chips, (chip + 1) % chips, (chip + 2) % chips]
    ).astype(jnp.int32)
    far_up = lax.ppermute(far_up, "chip", ahead_of)
    far_down = lax.ppermute(far_down, "chip", behind_of)
    scalars = mark(scalars, ahead, behind, far_up, far_down)
    recv = lax.all_to_all(sent, "node", split_axis=0, concat_axis=0, tiled=True)
    recv, here_too, ahead, behind, far_up, far_down, scalars = lax.optimization_barrier(
        (recv, here_too, ahead, behind, far_up, far_down, scalars)
    )
    blocks = (here, here_too)
    for block in (ahead, behind):
        blocks += (block, lax.ppermute(block, "core", swap))
    blocks += (far_up, far_down)
    for block in (far_up, far_down):
        blocks += (lax.ppermute(block, "core", swap),)
    held = [
        pltpu.VMEM((chips * CORES, 2 * wide, hidden), bf16),
        pltpu.SemaphoreType.DMA((4, chips * CORES, 2)),
    ]
    used = jnp.any(recv[:, 2 * width // LANES, :] > 0, 1)
    rank = jnp.cumsum(used.astype(jnp.int32)) - 1
    slot = jnp.arange(pairs, dtype=jnp.int32)
    pick = ((rank[None, :] == slot[:, None]) & used[None, :]).astype(bf16)
    mine = dot(pick, recv.reshape(nodes, -1), ((1,), (0,))).astype(bf16)
    parts = jnp.stack(
        [
            jnp.concatenate(
                [
                    mine[:, m * wide : (m + 1) * wide],
                    mine[:, width + m * wide : width + (m + 1) * wide],
                    mine[:, 2 * width : 2 * width + LANES],
                ],
                1,
            )
            for m in range(chips)
        ]
    )
    spread = jnp.broadcast_to(parts[None], (experts,) + parts.shape).reshape(
        experts * chips, pairs, -1
    )
    rows = lax.all_to_all(
        spread, ("expert", "chip"), split_axis=0, concat_axis=0, tiled=True
    ).reshape(experts * chips * pairs, -1)
    gate = jnp.sum(
        jnp.where(lane[None, :] == expert, rows[:, 2 * wide :].astype(f32), 0.0), 1, keepdims=True
    )

    units = CORES * hidden
    (outgoing,) = call(
        partial_kernel,
        [(chips, rows.shape[0], 2 * units)],
        (scalars,),
        rows,
        *blocks,
        hbm=len(blocks),
        loose=2,
        scratch=held,
    )
    incoming = lax.all_to_all(outgoing, "chip", split_axis=0, concat_axis=0, tiled=True)
    both = jnp.sum(incoming.astype(f32), 0)
    pre = both[:, :units]
    back = both[:, units:]
    sig = jax.nn.sigmoid(pre)
    active = (pre * sig).astype(bf16)
    grad_pre = (gate * back * sig * (1.0 + pre * (1.0 - sig))).astype(bf16)
    every = lax.all_gather(jnp.concatenate([active, grad_pre], 1), "chip", axis=0)

    (result,) = call(
        output_kernel,
        [rows.shape],
        (scalars,),
        rows,
        every,
        *blocks,
        hbm=len(blocks),
        loose=2,
        scratch=held,
    )

    parts_back = lax.all_to_all(
        result.reshape(experts * chips, pairs, -1),
        ("expert", "chip"),
        split_axis=0,
        concat_axis=0,
        tiled=True,
    ).reshape(experts, chips, pairs, -1)
    summed = jnp.sum(parts_back.astype(f32), 0)
    inner_all = jnp.sum(summed[:, :, 2 * wide :], 0)
    full = jnp.concatenate(
        [summed[m, :, :wide] for m in range(chips)]
        + [summed[m, :, wide : 2 * wide] for m in range(chips)]
        + [inner_all],
        1,
    ).astype(bf16)
    expanded = dot(pick, full, ((0,), (0,))).astype(bf16)
    expanded = jnp.pad(expanded, ((0, 0), (0, 7 * LANES))).reshape(nodes, -1, LANES)
    home = lax.all_to_all(expanded, "node", split_axis=0, concat_axis=0, tiled=True)

    mixed, grad_tokens, grad_gates = call(
        home_kernel,
        [tokens.shape, tokens.shape, choices.shape],
        (),
        home,
        groups,
        choices,
        hbm=2,
        scratch=[*tables, wide_rows, pltpu.SemaphoreType.DMA((2,))],
    )
    return mixed, grad_tokens, grad_gates.transpose(2, 0, 1)


def solution(mesh):
    nodes, members = mesh.devices.shape
    axes = ("node", "expert", "chip", "core")
    fine = Mesh(
        mesh.devices.reshape(nodes, EXPERTS, members // (EXPERTS * CORES), CORES), axes
    )
    placed = (
        P(axes, None),
        P(axes, None),
        P(axes, None),
        P(axes, None, None),
        P(axes, None, None),
        P(None, axes),
        P(axes, None),
    )
    return jax.shard_map(
        per_device,
        mesh=fine,
        in_specs=placed,
        out_specs=(P(axes, None), P(axes, None), P(axes, None, None)),
        check_vma=False,
    )
```

```python
import jax
import jax.numpy as jnp
from jax import lax
from jax.experimental import pallas as pl
from jax.experimental.pallas import tpu as pltpu
from jax.sharding import Mesh, PartitionSpec as P

EXPERTS = 4
CORES = 2
LANES = 128


def dot(a, b, dims):
    return lax.dot_general(a, b, (dims, ((), ())), preferred_element_type=jnp.float32)


def small_copies(pairs, sems):
    copies = [pltpu.make_async_copy(a, b, sems.at[i]) for i, (a, b) in enumerate(pairs)]
    for copy in copies:
        copy.start()
    return copies


def send_kernel(
    gates, groups_at, choices_at, tokens, cotangent, out, groups, choices, narrow, wide, sems
):
    count, width = tokens.shape
    chunks = width // LANES
    first, second, *copies = small_copies(
        [
            (groups_at, groups),
            (choices_at, choices),
            (tokens, narrow.at[0]),
            (cotangent, narrow.at[1]),
        ],
        sems,
    )
    out[...] = jnp.zeros_like(out)
    first.wait()
    second.wait()
    every_gate = gates[...].astype(jnp.float32)
    row = lax.broadcasted_iota(jnp.int32, (8, LANES), 0)
    lane = lax.broadcasted_iota(jnp.int32, (8, LANES), 1)
    i, j = (lax.broadcasted_iota(jnp.int32, (2, count), d) for d in range(2))
    for t in range(count):
        for c in range(2):
            table = jnp.zeros((8, LANES), jnp.float32)
            for k in range(2):
                gate = jnp.sum(jnp.where((i == k) & (j == t), every_gate[c], 0.0), keepdims=True)
                table += jnp.where((row == 0) & (lane == choices[c, k, t]), gate, 0.0)
            out[groups[c, t], 2 * chunks :, :] = table.astype(out.dtype)
    for i, copy in enumerate(copies):
        copy.wait()
        for j in range(chunks):
            wide[:, i * chunks + j, :] = narrow[i, :, j * LANES : (j + 1) * LANES].astype(
                jnp.float32
            )
    for t in range(count):
        rows = wide[t].astype(out.dtype)
        for c in range(2):
            out[groups[c, t], : 2 * chunks, :] = rows


def home_kernel(
    home, groups_at, choices_at, mixed, grad_tokens, grad_gates, groups, choices, wide, sems
):
    count, width = mixed.shape
    chunks = width // LANES
    row = lax.broadcasted_iota(jnp.int32, (8, LANES), 0)
    lane = lax.broadcasted_iota(jnp.int32, (8, LANES), 1)
    i, j = (lax.broadcasted_iota(jnp.int32, (2, count), d) for d in range(2))
    inner = [jnp.zeros((2, count), jnp.float32) for c in range(2)]
    for copy in small_copies([(groups_at, groups), (choices_at, choices)], sems):
        copy.wait()
    for t in range(count):
        total = jnp.zeros((2 * chunks, LANES), jnp.float32)
        for c in range(2):
            node = groups[c, t]
            total += home[node, : 2 * chunks, :].astype(jnp.float32)
            table = home[node, 2 * chunks :, :].astype(jnp.float32)
            for k in range(2):
                value = jnp.sum(
                    jnp.where((row == 0) & (lane == choices[c, k, t]), table, 0.0), keepdims=True
                )
                inner[c] = jnp.where((i == k) & (j == t), value, inner[c])
        wide[t] = total
    for c in range(2):
        grad_gates[c] = inner[c].astype(grad_gates.dtype)
    for j in range(chunks):
        at = pl.ds(j * LANES, LANES)
        mixed[:, at] = wide[:, j, :].astype(mixed.dtype)
        grad_tokens[:, at] = wide[:, chunks + j, :].astype(grad_tokens.dtype)


def pack_kernel(chips, up, down, here, ahead, behind, far_up, far_down, sems):
    wide = far_up.shape[0]
    copies = []

    def rows(chip, out, at):
        start = pl.multiple_of(chips[chip] * wide, wide)
        copies.append(
            pltpu.make_async_copy(
                up.at[pl.ds(start, wide)], out.at[pl.ds(at, wide)], sems.at[len(copies)]
            )
        )

    def columns(chip, out, at):
        start = pl.multiple_of(chips[chip] * wide, wide)
        for j in range(0, wide, LANES):
            copies.append(
                pltpu.make_async_copy(
                    down.at[:, pl.ds(start + j, LANES)],
                    out.at[pl.ds(at + j, LANES)],
                    sems.at[len(copies)],
                )
            )

    for chip, out in ((1, ahead), (3, behind), (0, here)):
        rows(chip, out, 0)
        columns(chip, out, wide)
    rows(2, far_up, 0)
    columns(2, far_down, 0)
    for copy in copies:
        copy.start()
    for copy in copies:
        copy.wait()


def fetch(refs, held, sems, cuts):
    wide = held.shape[1] // 2
    halves = [(ref.at[pl.ds(0, wide)], ref.at[pl.ds(wide, wide)]) for ref in refs[:-4]]
    halves += [(refs[-4], refs[-3]), (refs[-2], refs[-1])]
    found = []
    for k, (low, high) in enumerate(zip((0,) + cuts, cuts + (wide,))):
        at = pl.ds(low, high - low)
        found.append(
            [
                [
                    pltpu.make_async_copy(
                        ref.at[at],
                        held.at[i, pl.ds(half * wide + low, high - low)],
                        sems.at[k, i, half],
                    )
                    for half, ref in enumerate(pair)
                ]
                for i, pair in enumerate(halves)
            ]
        )
    return found


def arrivals(groups):
    for group in groups:
        for copy in group:
            copy.start()
    for group in groups:
        for copy in group:
            copy.wait()
        yield


def flat(lists):
    return [item for items in lists for item in items]


def mark_kernel(scalars, *refs):
    for i in range(scalars.shape[0]):
        refs[-1][i] = scalars[i]


def mark(scalars, *arrays):
    small = pl.BlockSpec(memory_space=pltpu.SMEM)
    return pl.pallas_call(
        mark_kernel,
        out_shape=jax.ShapeDtypeStruct(scalars.shape, scalars.dtype),
        in_specs=[small] + [pl.BlockSpec(memory_space=pl.ANY)] * len(arrays),
        out_specs=small,
        cost_estimate=pl.CostEstimate(flops=25 * 10**9, bytes_accessed=4096, transcendentals=0),
    )(scalars, *arrays)


def partial_kernel(scalars, rows, *refs):
    *blocks, out, held, sems = refs
    count, _, hidden = held.shape
    wide = held.shape[1] // 2
    (copies,) = fetch(blocks, held, sems, ())
    arrived = arrivals([flat(copies[i : i + CORES]) for i in range(0, count, CORES)])
    x, dy = rows[:, :wide], rows[:, wide : 2 * wide]
    for i in range(count // CORES):
        pair = range(CORES * i, CORES * (i + 1))
        next(arrived)
        at = scalars[1 + i]
        up = jnp.concatenate([held[m, :wide, :] for m in pair], 1)
        out[at, :, : CORES * hidden] = dot(x, up, ((1,), (0,))).astype(out.dtype)
        down = jnp.concatenate(
            [
                jnp.concatenate([held[m, wide + j : wide + j + LANES, :] for m in pair], 0)
                for j in range(0, wide, LANES)
            ],
            1,
        )
        out[at, :, CORES * hidden :] = dot(dy, down, ((1,), (1,))).astype(out.dtype)


def output_kernel(scalars, rows, every, *refs):
    *blocks, result, held, sems = refs
    many, _, hidden = held.shape
    wide = held.shape[1] // 2
    step = 2 * LANES
    cuts = tuple(range(2 * step, wide, 2 * step))
    arrived = arrivals([flat(cut) for cut in fetch(blocks, held, sems, cuts)])
    chips = many // CORES
    count = rows.shape[0]
    lane = lax.broadcasted_iota(jnp.int32, (count, LANES), 1)
    mine = lane == scalars[0]
    gate = jnp.sum(
        jnp.where(mine, rows[:, 2 * wide :].astype(jnp.float32), 0.0), 1, keepdims=True
    )
    active = jnp.concatenate(
        [every[scalars[1 + i], :, : CORES * hidden] for i in range(chips)], 1
    )
    grad_pre = jnp.concatenate(
        [every[scalars[1 + i], :, CORES * hidden :] for i in range(chips)], 1
    )
    inner = jnp.zeros((count, 1), jnp.float32)
    for j in range(0, wide, step):
        if j == 0 or j in cuts:
            next(arrived)
        down = jnp.concatenate(
            [
                jnp.concatenate(
                    [held[m, wide + j + k : wide + j + k + LANES, :] for m in range(many)], 0
                )
                for k in range(0, step, LANES)
            ],
            1,
        )
        up = jnp.concatenate([held[m, j : j + step, :] for m in range(many)], 1)
        out = dot(active, down, ((1,), (0,)))
        inner += jnp.sum(
            out * rows[:, wide + j : wide + j + step].astype(jnp.float32), 1, keepdims=True
        )
        result[:, j : j + step] = (gate * out).astype(result.dtype)
        result[:, wide + j : wide + j + step] = dot(grad_pre, up, ((1,), (1,))).astype(
            result.dtype
        )
    inner = jnp.where(gate > 0, inner, 0.0)
    result[:, 2 * wide :] = jnp.where(mine, inner, 0.0).astype(result.dtype)


def call(kernel, shapes, scalars, *operands, hbm=0, scratch=(), loose=0):
    small, near, far = (
        pl.BlockSpec(memory_space=space) for space in (pltpu.SMEM, pltpu.VMEM, pltpu.HBM)
    )
    count = len(operands) - hbm
    fixed = len(operands) - loose
    held = [pltpu.with_memory_space_constraint(v, pltpu.HBM) for v in operands[count:fixed]]
    held += operands[fixed:]
    anywhere = pl.BlockSpec(memory_space=pl.ANY)
    return pl.pallas_call(
        kernel,
        out_shape=[jax.ShapeDtypeStruct(shape, jnp.bfloat16) for shape in shapes],
        in_specs=[small] * len(scalars) + [near] * count + [far] * (hbm - loose) + [anywhere] * loose,
        out_specs=[near] * len(shapes),
        scratch_shapes=scratch,
        compiler_params=pltpu.CompilerParams(vmem_limit_bytes=24 * 2**20),
    )(*scalars, *operands[:count], *held)


def per_device(tokens, cotangent, groups, choices, gates, up_weight, down_weight):
    f32, bf16 = jnp.float32, jnp.bfloat16
    tok_count, width = tokens.shape
    nodes = lax.axis_size("node")
    experts = lax.axis_size("expert")
    chips = lax.axis_size("chip")
    hidden = up_weight.shape[1]
    pairs = 2 * tok_count
    wide = width // chips
    expert = lax.axis_index("expert")
    chip = lax.axis_index("chip")
    lane = jnp.arange(LANES, dtype=jnp.int32)

    slot_rows = 2 * width // LANES
    groups, choices = groups.T, choices.transpose(1, 2, 0)
    tables = [pltpu.SMEM(v.shape, jnp.int32) for v in (groups, choices)]
    wide_rows = pltpu.VMEM((tok_count, slot_rows, LANES), f32)
    (sent,) = call(
        send_kernel,
        [(nodes, slot_rows + 8, LANES)],
        (),
        gates.transpose(1, 2, 0),
        groups,
        choices,
        tokens,
        cotangent,
        hbm=4,
        scratch=[
            *tables,
            pltpu.VMEM((2,) + tokens.shape, bf16),
            wide_rows,
            pltpu.SemaphoreType.DMA((4,)),
        ],
    )

    ahead_of = [(i, (i + 1) % chips) for i in range(chips)]
    behind_of = [(i, (i - 1) % chips) for i in range(chips)]
    targets = jnp.stack([(chip + s) % chips for s in range(chips)]).astype(jnp.int32)
    here, ahead, behind, far_up, far_down = call(
        pack_kernel,
        [(2 * wide, hidden)] * 3 + [(wide, hidden)] * 2,
        (targets,),
        up_weight,
        down_weight,
        hbm=2,
        scratch=[pltpu.SemaphoreType.DMA((chips * (wide // LANES + 1),))],
    )
    here, ahead, behind, far_up, far_down, sent = lax.optimization_barrier(
        (here, ahead, behind, far_up, far_down, sent)
    )
    swap = [(0, 1), (1, 0)]
    far_up = lax.ppermute(far_up, "chip", ahead_of)
    far_down = lax.ppermute(far_down, "chip", behind_of)
    ahead = lax.ppermute(ahead, "chip", ahead_of)
    behind = lax.ppermute(behind, "chip", behind_of)
    here_too = lax.ppermute(here, "core", swap)
    scalars = jnp.stack(
        [expert, chip, (chip + chips - 1) % chips, (chip + 1) % chips, (chip + 2) % chips]
    ).astype(jnp.int32)
    far_up = lax.ppermute(far_up, "chip", ahead_of)
    far_down = lax.ppermute(far_down, "chip", behind_of)
    scalars = mark(scalars, ahead, behind, far_up, far_down)
    recv = lax.all_to_all(sent, "node", split_axis=0, concat_axis=0, tiled=True)
    near = (here, here_too)
    for block in (ahead, behind):
        near += (block, lax.ppermute(block, "core", swap))
    recv, near, far_up, far_down, scalars = lax.optimization_barrier(
        (recv, near, far_up, far_down, scalars)
    )
    blocks = near + (far_up, far_down)
    for block in (far_up, far_down):
        blocks += (lax.ppermute(block, "core", swap),)
    held = [
        pltpu.VMEM((chips * CORES, 2 * wide, hidden), bf16),
        pltpu.SemaphoreType.DMA((4, chips * CORES, 2)),
    ]
    used = jnp.any(recv[:, 2 * width // LANES, :] > 0, 1)
    rank = jnp.cumsum(used.astype(jnp.int32)) - 1
    slot = jnp.arange(pairs, dtype=jnp.int32)
    pick = ((rank[None, :] == slot[:, None]) & used[None, :]).astype(bf16)
    mine = dot(pick, recv.reshape(nodes, -1), ((1,), (0,))).astype(bf16)
    parts = jnp.stack(
        [
            jnp.concatenate(
                [
                    mine[:, m * wide : (m + 1) * wide],
                    mine[:, width + m * wide : width + (m + 1) * wide],
                    mine[:, 2 * width : 2 * width + LANES],
                ],
                1,
            )
            for m in range(chips)
        ]
    )
    spread = jnp.broadcast_to(parts[None], (experts,) + parts.shape).reshape(
        experts * chips, pairs, -1
    )
    rows = lax.all_to_all(
        spread, ("expert", "chip"), split_axis=0, concat_axis=0, tiled=True
    ).reshape(experts * chips * pairs, -1)
    gate = jnp.sum(
        jnp.where(lane[None, :] == expert, rows[:, 2 * wide :].astype(f32), 0.0), 1, keepdims=True
    )

    units = CORES * hidden
    (outgoing,) = call(
        partial_kernel,
        [(chips, rows.shape[0], 2 * units)],
        (scalars,),
        rows,
        *blocks,
        hbm=len(blocks),
        loose=2,
        scratch=held,
    )
    incoming = lax.all_to_all(outgoing, "chip", split_axis=0, concat_axis=0, tiled=True)
    both = jnp.sum(incoming.astype(f32), 0)
    pre = both[:, :units]
    back = both[:, units:]
    sig = jax.nn.sigmoid(pre)
    active = (pre * sig).astype(bf16)
    grad_pre = (gate * back * sig * (1.0 + pre * (1.0 - sig))).astype(bf16)
    every = lax.all_gather(jnp.concatenate([active, grad_pre], 1), "chip", axis=0)

    (result,) = call(
        output_kernel,
        [rows.shape],
        (scalars,),
        rows,
        every,
        *blocks,
        hbm=len(blocks),
        loose=2,
        scratch=held,
    )

    parts_back = lax.all_to_all(
        result.reshape(experts * chips, pairs, -1),
        ("expert", "chip"),
        split_axis=0,
        concat_axis=0,
        tiled=True,
    ).reshape(experts, chips, pairs, -1)
    summed = jnp.sum(parts_back.astype(f32), 0)
    inner_all = jnp.sum(summed[:, :, 2 * wide :], 0)
    full = jnp.concatenate(
        [summed[m, :, :wide] for m in range(chips)]
        + [summed[m, :, wide : 2 * wide] for m in range(chips)]
        + [inner_all],
        1,
    ).astype(bf16)
    expanded = dot(pick, full, ((0,), (0,))).astype(bf16)
    expanded = jnp.pad(expanded, ((0, 0), (0, 7 * LANES))).reshape(nodes, -1, LANES)
    home = lax.all_to_all(expanded, "node", split_axis=0, concat_axis=0, tiled=True)

    mixed, grad_tokens, grad_gates = call(
        home_kernel,
        [tokens.shape, tokens.shape, choices.shape],
        (),
        home,
        groups,
        choices,
        hbm=2,
        scratch=[*tables, wide_rows, pltpu.SemaphoreType.DMA((2,))],
    )
    return mixed, grad_tokens, grad_gates.transpose(2, 0, 1)


def solution(mesh):
    nodes, members = mesh.devices.shape
    axes = ("node", "expert", "chip", "core")
    fine = Mesh(
        mesh.devices.reshape(nodes, EXPERTS, members // (EXPERTS * CORES), CORES), axes
    )
    placed = (
        P(axes, None),
        P(axes, None),
        P(axes, None),
        P(axes, None, None),
        P(axes, None, None),
        P(None, axes),
        P(axes, None),
    )
    return jax.shard_map(
        per_device,
        mesh=fine,
        in_specs=placed,
        out_specs=(P(axes, None), P(axes, None), P(axes, None, None)),
        check_vma=False,
    )
```

```python
import jax
import jax.numpy as jnp
from jax import lax
from jax.experimental import pallas as pl
from jax.experimental.pallas import tpu as pltpu
from jax.sharding import Mesh, PartitionSpec as P

EXPERTS = 4
CORES = 2
LANES = 128


def dot(a, b, dims):
    return lax.dot_general(a, b, (dims, ((), ())), preferred_element_type=jnp.float32)


def small_copies(pairs, sems):
    copies = [pltpu.make_async_copy(a, b, sems.at[i]) for i, (a, b) in enumerate(pairs)]
    for copy in copies:
        copy.start()
    return copies


def send_kernel(
    gates, groups_at, choices_at, tokens, cotangent, out, groups, choices, narrow, wide, sems
):
    count, width = tokens.shape
    chunks = width // LANES
    first, second, *copies = small_copies(
        [
            (groups_at, groups),
            (choices_at, choices),
            (tokens, narrow.at[0]),
            (cotangent, narrow.at[1]),
        ],
        sems,
    )
    out[...] = jnp.zeros_like(out)
    first.wait()
    second.wait()
    every_gate = gates[...].astype(jnp.float32)
    row = lax.broadcasted_iota(jnp.int32, (8, LANES), 0)
    lane = lax.broadcasted_iota(jnp.int32, (8, LANES), 1)
    i, j = (lax.broadcasted_iota(jnp.int32, (2, count), d) for d in range(2))
    for t in range(count):
        for c in range(2):
            table = jnp.zeros((8, LANES), jnp.float32)
            for k in range(2):
                gate = jnp.sum(jnp.where((i == k) & (j == t), every_gate[c], 0.0), keepdims=True)
                table += jnp.where((row == 0) & (lane == choices[c, k, t]), gate, 0.0)
            out[groups[c, t], 2 * chunks :, :] = table.astype(out.dtype)
    for i, copy in enumerate(copies):
        copy.wait()
        for j in range(chunks):
            wide[:, i * chunks + j, :] = narrow[i, :, j * LANES : (j + 1) * LANES].astype(
                jnp.float32
            )
    for t in range(count):
        rows = wide[t].astype(out.dtype)
        for c in range(2):
            out[groups[c, t], : 2 * chunks, :] = rows


def home_kernel(
    home, groups_at, choices_at, mixed, grad_tokens, grad_gates, groups, choices, wide, sems
):
    count, width = mixed.shape
    chunks = width // LANES
    row = lax.broadcasted_iota(jnp.int32, (8, LANES), 0)
    lane = lax.broadcasted_iota(jnp.int32, (8, LANES), 1)
    i, j = (lax.broadcasted_iota(jnp.int32, (2, count), d) for d in range(2))
    inner = [jnp.zeros((2, count), jnp.float32) for c in range(2)]
    for copy in small_copies([(groups_at, groups), (choices_at, choices)], sems):
        copy.wait()
    for t in range(count):
        total = jnp.zeros((2 * chunks, LANES), jnp.float32)
        for c in range(2):
            node = groups[c, t]
            total += home[node, : 2 * chunks, :].astype(jnp.float32)
            table = home[node, 2 * chunks :, :].astype(jnp.float32)
            for k in range(2):
                value = jnp.sum(
                    jnp.where((row == 0) & (lane == choices[c, k, t]), table, 0.0), keepdims=True
                )
                inner[c] = jnp.where((i == k) & (j == t), value, inner[c])
        wide[t] = total
    for c in range(2):
        grad_gates[c] = inner[c].astype(grad_gates.dtype)
    for j in range(chunks):
        at = pl.ds(j * LANES, LANES)
        mixed[:, at] = wide[:, j, :].astype(mixed.dtype)
        grad_tokens[:, at] = wide[:, chunks + j, :].astype(grad_tokens.dtype)


def pack_kernel(chips, up, down, here, ahead, behind, far_up, far_down, sems):
    wide = far_up.shape[0]
    copies = []

    def rows(chip, out, at):
        start = pl.multiple_of(chips[chip] * wide, wide)
        copies.append(
            pltpu.make_async_copy(
                up.at[pl.ds(start, wide)], out.at[pl.ds(at, wide)], sems.at[len(copies)]
            )
        )

    def columns(chip, out, at):
        start = pl.multiple_of(chips[chip] * wide, wide)
        for j in range(0, wide, LANES):
            copies.append(
                pltpu.make_async_copy(
                    down.at[:, pl.ds(start + j, LANES)],
                    out.at[pl.ds(at + j, LANES)],
                    sems.at[len(copies)],
                )
            )

    for chip, out in ((1, ahead), (3, behind), (0, here)):
        rows(chip, out, 0)
        columns(chip, out, wide)
    rows(2, far_up, 0)
    columns(2, far_down, 0)
    for copy in copies:
        copy.start()
    for copy in copies:
        copy.wait()


def fetch(refs, held, sems, cuts):
    wide = held.shape[1] // 2
    halves = [(ref.at[pl.ds(0, wide)], ref.at[pl.ds(wide, wide)]) for ref in refs[:-4]]
    halves += [(refs[-4], refs[-3]), (refs[-2], refs[-1])]
    found = []
    for k, (low, high) in enumerate(zip((0,) + cuts, cuts + (wide,))):
        at = pl.ds(low, high - low)
        found.append(
            [
                [
                    pltpu.make_async_copy(
                        ref.at[at],
                        held.at[i, pl.ds(half * wide + low, high - low)],
                        sems.at[k, i, half],
                    )
                    for half, ref in enumerate(pair)
                ]
                for i, pair in enumerate(halves)
            ]
        )
    return found


def arrivals(groups):
    for group in groups:
        for copy in group:
            copy.start()
    for group in groups:
        for copy in group:
            copy.wait()
        yield


def flat(lists):
    return [item for items in lists for item in items]


def mark_kernel(scalars, *refs):
    for i in range(scalars.shape[0]):
        refs[-1][i] = scalars[i]


def mark(scalars, *arrays):
    small = pl.BlockSpec(memory_space=pltpu.SMEM)
    return pl.pallas_call(
        mark_kernel,
        out_shape=jax.ShapeDtypeStruct(scalars.shape, scalars.dtype),
        in_specs=[small] + [pl.BlockSpec(memory_space=pl.ANY)] * len(arrays),
        out_specs=small,
        cost_estimate=pl.CostEstimate(flops=10**11, bytes_accessed=4096, transcendentals=0),
    )(scalars, *arrays)


def partial_kernel(scalars, rows, *refs):
    *blocks, out, held, sems = refs
    count, _, hidden = held.shape
    wide = held.shape[1] // 2
    (copies,) = fetch(blocks, held, sems, ())
    arrived = arrivals([flat(copies[i : i + CORES]) for i in range(0, count, CORES)])
    x, dy = rows[:, :wide], rows[:, wide : 2 * wide]
    for i in range(count // CORES):
        pair = range(CORES * i, CORES * (i + 1))
        next(arrived)
        at = scalars[1 + i]
        up = jnp.concatenate([held[m, :wide, :] for m in pair], 1)
        out[at, :, : CORES * hidden] = dot(x, up, ((1,), (0,))).astype(out.dtype)
        down = jnp.concatenate(
            [
                jnp.concatenate([held[m, wide + j : wide + j + LANES, :] for m in pair], 0)
                for j in range(0, wide, LANES)
            ],
            1,
        )
        out[at, :, CORES * hidden :] = dot(dy, down, ((1,), (1,))).astype(out.dtype)


def output_kernel(scalars, rows, every, *refs):
    *blocks, result, held, sems = refs
    many, _, hidden = held.shape
    wide = held.shape[1] // 2
    step = 2 * LANES
    cuts = tuple(range(2 * step, wide, 2 * step))
    arrived = arrivals([flat(cut) for cut in fetch(blocks, held, sems, cuts)])
    chips = many // CORES
    count = rows.shape[0]
    lane = lax.broadcasted_iota(jnp.int32, (count, LANES), 1)
    mine = lane == scalars[0]
    gate = jnp.sum(
        jnp.where(mine, rows[:, 2 * wide :].astype(jnp.float32), 0.0), 1, keepdims=True
    )
    active = jnp.concatenate(
        [every[scalars[1 + i], :, : CORES * hidden] for i in range(chips)], 1
    )
    grad_pre = jnp.concatenate(
        [every[scalars[1 + i], :, CORES * hidden :] for i in range(chips)], 1
    )
    inner = jnp.zeros((count, 1), jnp.float32)
    for j in range(0, wide, step):
        if j == 0 or j in cuts:
            next(arrived)
        down = jnp.concatenate(
            [
                jnp.concatenate(
                    [held[m, wide + j + k : wide + j + k + LANES, :] for m in range(many)], 0
                )
                for k in range(0, step, LANES)
            ],
            1,
        )
        up = jnp.concatenate([held[m, j : j + step, :] for m in range(many)], 1)
        out = dot(active, down, ((1,), (0,)))
        inner += jnp.sum(
            out * rows[:, wide + j : wide + j + step].astype(jnp.float32), 1, keepdims=True
        )
        result[:, j : j + step] = (gate * out).astype(result.dtype)
        result[:, wide + j : wide + j + step] = dot(grad_pre, up, ((1,), (1,))).astype(
            result.dtype
        )
    inner = jnp.where(gate > 0, inner, 0.0)
    result[:, 2 * wide :] = jnp.where(mine, inner, 0.0).astype(result.dtype)


def call(kernel, shapes, scalars, *operands, hbm=0, scratch=(), loose=0):
    small, near, far = (
        pl.BlockSpec(memory_space=space) for space in (pltpu.SMEM, pltpu.VMEM, pltpu.HBM)
    )
    count = len(operands) - hbm
    fixed = len(operands) - loose
    held = [pltpu.with_memory_space_constraint(v, pltpu.HBM) for v in operands[count:fixed]]
    held += operands[fixed:]
    anywhere = pl.BlockSpec(memory_space=pl.ANY)
    return pl.pallas_call(
        kernel,
        out_shape=[jax.ShapeDtypeStruct(shape, jnp.bfloat16) for shape in shapes],
        in_specs=[small] * len(scalars) + [near] * count + [far] * (hbm - loose) + [anywhere] * loose,
        out_specs=[near] * len(shapes),
        scratch_shapes=scratch,
        compiler_params=pltpu.CompilerParams(vmem_limit_bytes=24 * 2**20),
    )(*scalars, *operands[:count], *held)


def per_device(tokens, cotangent, groups, choices, gates, up_weight, down_weight):
    f32, bf16 = jnp.float32, jnp.bfloat16
    tok_count, width = tokens.shape
    nodes = lax.axis_size("node")
    experts = lax.axis_size("expert")
    chips = lax.axis_size("chip")
    hidden = up_weight.shape[1]
    pairs = 2 * tok_count
    wide = width // chips
    expert = lax.axis_index("expert")
    chip = lax.axis_index("chip")
    lane = jnp.arange(LANES, dtype=jnp.int32)

    slot_rows = 2 * width // LANES
    groups, choices = groups.T, choices.transpose(1, 2, 0)
    tables = [pltpu.SMEM(v.shape, jnp.int32) for v in (groups, choices)]
    wide_rows = pltpu.VMEM((tok_count, slot_rows, LANES), f32)
    (sent,) = call(
        send_kernel,
        [(nodes, slot_rows + 8, LANES)],
        (),
        gates.transpose(1, 2, 0),
        groups,
        choices,
        tokens,
        cotangent,
        hbm=4,
        scratch=[
            *tables,
            pltpu.VMEM((2,) + tokens.shape, bf16),
            wide_rows,
            pltpu.SemaphoreType.DMA((4,)),
        ],
    )

    ahead_of = [(i, (i + 1) % chips) for i in range(chips)]
    behind_of = [(i, (i - 1) % chips) for i in range(chips)]
    targets = jnp.stack([(chip + s) % chips for s in range(chips)]).astype(jnp.int32)
    here, ahead, behind, far_up, far_down = call(
        pack_kernel,
        [(2 * wide, hidden)] * 3 + [(wide, hidden)] * 2,
        (targets,),
        up_weight,
        down_weight,
        hbm=2,
        scratch=[pltpu.SemaphoreType.DMA((chips * (wide // LANES + 1),))],
    )
    here, ahead, behind, far_up, far_down, sent = lax.optimization_barrier(
        (here, ahead, behind, far_up, far_down, sent)
    )
    swap = [(0, 1), (1, 0)]
    far_up = lax.ppermute(far_up, "chip", ahead_of)
    far_down = lax.ppermute(far_down, "chip", behind_of)
    ahead = lax.ppermute(ahead, "chip", ahead_of)
    behind = lax.ppermute(behind, "chip", behind_of)
    here_too = lax.ppermute(here, "core", swap)
    scalars = jnp.stack(
        [expert, chip, (chip + chips - 1) % chips, (chip + 1) % chips, (chip + 2) % chips]
    ).astype(jnp.int32)
    scalars = mark(scalars, ahead, behind, far_up, far_down)
    ahead, behind, far_up, far_down, scalars = lax.optimization_barrier(
        (ahead, behind, far_up, far_down, scalars)
    )
    far_up = lax.ppermute(far_up, "chip", ahead_of)
    far_down = lax.ppermute(far_down, "chip", behind_of)
    recv = lax.all_to_all(sent, "node", split_axis=0, concat_axis=0, tiled=True)
    near = (here, here_too)
    for block in (ahead, behind):
        near += (block, lax.ppermute(block, "core", swap))
    recv, near, far_up, far_down, scalars = lax.optimization_barrier(
        (recv, near, far_up, far_down, scalars)
    )
    blocks = near + (far_up, far_down)
    for block in (far_up, far_down):
        blocks += (lax.ppermute(block, "core", swap),)
    held = [
        pltpu.VMEM((chips * CORES, 2 * wide, hidden), bf16),
        pltpu.SemaphoreType.DMA((4, chips * CORES, 2)),
    ]
    used = jnp.any(recv[:, 2 * width // LANES, :] > 0, 1)
    rank = jnp.cumsum(used.astype(jnp.int32)) - 1
    slot = jnp.arange(pairs, dtype=jnp.int32)
    pick = ((rank[None, :] == slot[:, None]) & used[None, :]).astype(bf16)
    mine = dot(pick, recv.reshape(nodes, -1), ((1,), (0,))).astype(bf16)
    parts = jnp.stack(
        [
            jnp.concatenate(
                [
                    mine[:, m * wide : (m + 1) * wide],
                    mine[:, width + m * wide : width + (m + 1) * wide],
                    mine[:, 2 * width : 2 * width + LANES],
                ],
                1,
            )
            for m in range(chips)
        ]
    )
    spread = jnp.broadcast_to(parts[None], (experts,) + parts.shape).reshape(
        experts * chips, pairs, -1
    )
    rows = lax.all_to_all(
        spread, ("expert", "chip"), split_axis=0, concat_axis=0, tiled=True
    ).reshape(experts * chips * pairs, -1)
    gate = jnp.sum(
        jnp.where(lane[None, :] == expert, rows[:, 2 * wide :].astype(f32), 0.0), 1, keepdims=True
    )

    units = CORES * hidden
    (outgoing,) = call(
        partial_kernel,
        [(chips, rows.shape[0], 2 * units)],
        (scalars,),
        rows,
        *blocks,
        hbm=len(blocks),
        loose=2,
        scratch=held,
    )
    incoming = lax.all_to_all(outgoing, "chip", split_axis=0, concat_axis=0, tiled=True)
    both = jnp.sum(incoming.astype(f32), 0)
    pre = both[:, :units]
    back = both[:, units:]
    sig = jax.nn.sigmoid(pre)
    active = (pre * sig).astype(bf16)
    grad_pre = (gate * back * sig * (1.0 + pre * (1.0 - sig))).astype(bf16)
    every = lax.all_gather(jnp.concatenate([active, grad_pre], 1), "chip", axis=0)

    (result,) = call(
        output_kernel,
        [rows.shape],
        (scalars,),
        rows,
        every,
        *blocks,
        hbm=len(blocks),
        loose=2,
        scratch=held,
    )

    parts_back = lax.all_to_all(
        result.reshape(experts * chips, pairs, -1),
        ("expert", "chip"),
        split_axis=0,
        concat_axis=0,
        tiled=True,
    ).reshape(experts, chips, pairs, -1)
    summed = jnp.sum(parts_back.astype(f32), 0)
    inner_all = jnp.sum(summed[:, :, 2 * wide :], 0)
    full = jnp.concatenate(
        [summed[m, :, :wide] for m in range(chips)]
        + [summed[m, :, wide : 2 * wide] for m in range(chips)]
        + [inner_all],
        1,
    ).astype(bf16)
    expanded = dot(pick, full, ((0,), (0,))).astype(bf16)
    expanded = jnp.pad(expanded, ((0, 0), (0, 7 * LANES))).reshape(nodes, -1, LANES)
    home = lax.all_to_all(expanded, "node", split_axis=0, concat_axis=0, tiled=True)

    mixed, grad_tokens, grad_gates = call(
        home_kernel,
        [tokens.shape, tokens.shape, choices.shape],
        (),
        home,
        groups,
        choices,
        hbm=2,
        scratch=[*tables, wide_rows, pltpu.SemaphoreType.DMA((2,))],
    )
    return mixed, grad_tokens, grad_gates.transpose(2, 0, 1)


def solution(mesh):
    nodes, members = mesh.devices.shape
    axes = ("node", "expert", "chip", "core")
    fine = Mesh(
        mesh.devices.reshape(nodes, EXPERTS, members // (EXPERTS * CORES), CORES), axes
    )
    placed = (
        P(axes, None),
        P(axes, None),
        P(axes, None),
        P(axes, None, None),
        P(axes, None, None),
        P(None, axes),
        P(axes, None),
    )
    return jax.shard_map(
        per_device,
        mesh=fine,
        in_specs=placed,
        out_specs=(P(axes, None), P(axes, None), P(axes, None, None)),
        check_vma=False,
    )
```

```python
import jax
import jax.numpy as jnp
from jax import lax
from jax.experimental import pallas as pl
from jax.experimental.pallas import tpu as pltpu
from jax.sharding import Mesh, PartitionSpec as P

EXPERTS = 4
CORES = 2
LANES = 128


def dot(a, b, dims):
    return lax.dot_general(a, b, (dims, ((), ())), preferred_element_type=jnp.float32)


def small_copies(pairs, sems):
    copies = [pltpu.make_async_copy(a, b, sems.at[i]) for i, (a, b) in enumerate(pairs)]
    for copy in copies:
        copy.start()
    return copies


def send_kernel(
    gates, groups_at, choices_at, tokens, cotangent, out, groups, choices, narrow, wide, sems
):
    count, width = tokens.shape
    chunks = width // LANES
    first, second, *copies = small_copies(
        [
            (groups_at, groups),
            (choices_at, choices),
            (tokens, narrow.at[0]),
            (cotangent, narrow.at[1]),
        ],
        sems,
    )
    out[...] = jnp.zeros_like(out)
    first.wait()
    second.wait()
    every_gate = gates[...].astype(jnp.float32)
    row = lax.broadcasted_iota(jnp.int32, (8, LANES), 0)
    lane = lax.broadcasted_iota(jnp.int32, (8, LANES), 1)
    i, j = (lax.broadcasted_iota(jnp.int32, (2, count), d) for d in range(2))
    for t in range(count):
        for c in range(2):
            table = jnp.zeros((8, LANES), jnp.float32)
            for k in range(2):
                gate = jnp.sum(jnp.where((i == k) & (j == t), every_gate[c], 0.0), keepdims=True)
                table += jnp.where((row == 0) & (lane == choices[c, k, t]), gate, 0.0)
            out[groups[c, t], 2 * chunks :, :] = table.astype(out.dtype)
    for i, copy in enumerate(copies):
        copy.wait()
        for j in range(chunks):
            wide[:, i * chunks + j, :] = narrow[i, :, j * LANES : (j + 1) * LANES].astype(
                jnp.float32
            )
    for t in range(count):
        rows = wide[t].astype(out.dtype)
        for c in range(2):
            out[groups[c, t], : 2 * chunks, :] = rows


def home_kernel(
    home, groups_at, choices_at, mixed, grad_tokens, grad_gates, groups, choices, wide, sems
):
    count, width = mixed.shape
    chunks = width // LANES
    row = lax.broadcasted_iota(jnp.int32, (8, LANES), 0)
    lane = lax.broadcasted_iota(jnp.int32, (8, LANES), 1)
    i, j = (lax.broadcasted_iota(jnp.int32, (2, count), d) for d in range(2))
    inner = [jnp.zeros((2, count), jnp.float32) for c in range(2)]
    for copy in small_copies([(groups_at, groups), (choices_at, choices)], sems):
        copy.wait()
    for t in range(count):
        total = jnp.zeros((2 * chunks, LANES), jnp.float32)
        for c in range(2):
            node = groups[c, t]
            total += home[node, : 2 * chunks, :].astype(jnp.float32)
            table = home[node, 2 * chunks :, :].astype(jnp.float32)
            for k in range(2):
                value = jnp.sum(
                    jnp.where((row == 0) & (lane == choices[c, k, t]), table, 0.0), keepdims=True
                )
                inner[c] = jnp.where((i == k) & (j == t), value, inner[c])
        wide[t] = total
    for c in range(2):
        grad_gates[c] = inner[c].astype(grad_gates.dtype)
    for j in range(chunks):
        at = pl.ds(j * LANES, LANES)
        mixed[:, at] = wide[:, j, :].astype(mixed.dtype)
        grad_tokens[:, at] = wide[:, chunks + j, :].astype(grad_tokens.dtype)


def pack_kernel(chips, up, down, here, ahead, behind, far_up, far_down, sems):
    wide = far_up.shape[0]
    copies = []

    def rows(chip, out, at):
        start = pl.multiple_of(chips[chip] * wide, wide)
        copies.append(
            pltpu.make_async_copy(
                up.at[pl.ds(start, wide)], out.at[pl.ds(at, wide)], sems.at[len(copies)]
            )
        )

    def columns(chip, out, at):
        start = pl.multiple_of(chips[chip] * wide, wide)
        for j in range(0, wide, LANES):
            copies.append(
                pltpu.make_async_copy(
                    down.at[:, pl.ds(start + j, LANES)],
                    out.at[pl.ds(at + j, LANES)],
                    sems.at[len(copies)],
                )
            )

    for chip, out in ((1, ahead), (3, behind), (0, here)):
        rows(chip, out, 0)
        columns(chip, out, wide)
    rows(2, far_up, 0)
    columns(2, far_down, 0)
    for copy in copies:
        copy.start()
    for copy in copies:
        copy.wait()


def fetch(refs, held, sems, cuts):
    wide = held.shape[1] // 2
    halves = [(ref.at[pl.ds(0, wide)], ref.at[pl.ds(wide, wide)]) for ref in refs[:-4]]
    halves += [(refs[-4], refs[-3]), (refs[-2], refs[-1])]
    found = []
    for k, (low, high) in enumerate(zip((0,) + cuts, cuts + (wide,))):
        at = pl.ds(low, high - low)
        found.append(
            [
                [
                    pltpu.make_async_copy(
                        ref.at[at],
                        held.at[i, pl.ds(half * wide + low, high - low)],
                        sems.at[k, i, half],
                    )
                    for half, ref in enumerate(pair)
                ]
                for i, pair in enumerate(halves)
            ]
        )
    return found


def arrivals(groups):
    for group in groups:
        for copy in group:
            copy.start()
    for group in groups:
        for copy in group:
            copy.wait()
        yield


def flat(lists):
    return [item for items in lists for item in items]


def mark_kernel(scalars, *refs):
    for i in range(scalars.shape[0]):
        refs[-1][i] = scalars[i]


def mark(scalars, flops, *arrays):
    small = pl.BlockSpec(memory_space=pltpu.SMEM)
    return pl.pallas_call(
        mark_kernel,
        out_shape=jax.ShapeDtypeStruct(scalars.shape, scalars.dtype),
        in_specs=[small] + [pl.BlockSpec(memory_space=pl.ANY)] * len(arrays),
        out_specs=small,
        cost_estimate=pl.CostEstimate(flops=flops, bytes_accessed=4096, transcendentals=0),
    )(scalars, *arrays)


def partial_kernel(scalars, rows, *refs):
    *blocks, out, held, sems = refs
    count, _, hidden = held.shape
    wide = held.shape[1] // 2
    (copies,) = fetch(blocks, held, sems, ())
    arrived = arrivals([flat(copies[i : i + CORES]) for i in range(0, count, CORES)])
    x, dy = rows[:, :wide], rows[:, wide : 2 * wide]
    for i in range(count // CORES):
        pair = range(CORES * i, CORES * (i + 1))
        next(arrived)
        at = scalars[1 + i]
        up = jnp.concatenate([held[m, :wide, :] for m in pair], 1)
        out[at, :, : CORES * hidden] = dot(x, up, ((1,), (0,))).astype(out.dtype)
        down = jnp.concatenate(
            [
                jnp.concatenate([held[m, wide + j : wide + j + LANES, :] for m in pair], 0)
                for j in range(0, wide, LANES)
            ],
            1,
        )
        out[at, :, CORES * hidden :] = dot(dy, down, ((1,), (1,))).astype(out.dtype)


def output_kernel(scalars, rows, every, *refs):
    *blocks, result, held, sems = refs
    many, _, hidden = held.shape
    wide = held.shape[1] // 2
    step = 2 * LANES
    cuts = tuple(range(2 * step, wide, 2 * step))
    arrived = arrivals([flat(cut) for cut in fetch(blocks, held, sems, cuts)])
    chips = many // CORES
    count = rows.shape[0]
    lane = lax.broadcasted_iota(jnp.int32, (count, LANES), 1)
    mine = lane == scalars[0]
    gate = jnp.sum(
        jnp.where(mine, rows[:, 2 * wide :].astype(jnp.float32), 0.0), 1, keepdims=True
    )
    active = jnp.concatenate(
        [every[scalars[1 + i], :, : CORES * hidden] for i in range(chips)], 1
    )
    grad_pre = jnp.concatenate(
        [every[scalars[1 + i], :, CORES * hidden :] for i in range(chips)], 1
    )
    inner = jnp.zeros((count, 1), jnp.float32)
    for j in range(0, wide, step):
        if j == 0 or j in cuts:
            next(arrived)
        down = jnp.concatenate(
            [
                jnp.concatenate(
                    [held[m, wide + j + k : wide + j + k + LANES, :] for m in range(many)], 0
                )
                for k in range(0, step, LANES)
            ],
            1,
        )
        up = jnp.concatenate([held[m, j : j + step, :] for m in range(many)], 1)
        out = dot(active, down, ((1,), (0,)))
        inner += jnp.sum(
            out * rows[:, wide + j : wide + j + step].astype(jnp.float32), 1, keepdims=True
        )
        result[:, j : j + step] = (gate * out).astype(result.dtype)
        result[:, wide + j : wide + j + step] = dot(grad_pre, up, ((1,), (1,))).astype(
            result.dtype
        )
    inner = jnp.where(gate > 0, inner, 0.0)
    result[:, 2 * wide :] = jnp.where(mine, inner, 0.0).astype(result.dtype)


def call(kernel, shapes, scalars, *operands, hbm=0, scratch=(), loose=0):
    small, near, far = (
        pl.BlockSpec(memory_space=space) for space in (pltpu.SMEM, pltpu.VMEM, pltpu.HBM)
    )
    count = len(operands) - hbm
    fixed = len(operands) - loose
    held = [pltpu.with_memory_space_constraint(v, pltpu.HBM) for v in operands[count:fixed]]
    held += operands[fixed:]
    anywhere = pl.BlockSpec(memory_space=pl.ANY)
    return pl.pallas_call(
        kernel,
        out_shape=[jax.ShapeDtypeStruct(shape, jnp.bfloat16) for shape in shapes],
        in_specs=[small] * len(scalars) + [near] * count + [far] * (hbm - loose) + [anywhere] * loose,
        out_specs=[near] * len(shapes),
        scratch_shapes=scratch,
        compiler_params=pltpu.CompilerParams(vmem_limit_bytes=24 * 2**20),
    )(*scalars, *operands[:count], *held)


def per_device(tokens, cotangent, groups, choices, gates, up_weight, down_weight):
    f32, bf16 = jnp.float32, jnp.bfloat16
    tok_count, width = tokens.shape
    nodes = lax.axis_size("node")
    experts = lax.axis_size("expert")
    chips = lax.axis_size("chip")
    hidden = up_weight.shape[1]
    pairs = 2 * tok_count
    wide = width // chips
    expert = lax.axis_index("expert")
    chip = lax.axis_index("chip")
    lane = jnp.arange(LANES, dtype=jnp.int32)

    slot_rows = 2 * width // LANES
    groups, choices = groups.T, choices.transpose(1, 2, 0)
    tables = [pltpu.SMEM(v.shape, jnp.int32) for v in (groups, choices)]
    wide_rows = pltpu.VMEM((tok_count, slot_rows, LANES), f32)
    (sent,) = call(
        send_kernel,
        [(nodes, slot_rows + 8, LANES)],
        (),
        gates.transpose(1, 2, 0),
        groups,
        choices,
        tokens,
        cotangent,
        hbm=4,
        scratch=[
            *tables,
            pltpu.VMEM((2,) + tokens.shape, bf16),
            wide_rows,
            pltpu.SemaphoreType.DMA((4,)),
        ],
    )

    ahead_of = [(i, (i + 1) % chips) for i in range(chips)]
    behind_of = [(i, (i - 1) % chips) for i in range(chips)]
    targets = jnp.stack([(chip + s) % chips for s in range(chips)]).astype(jnp.int32)
    here, ahead, behind, far_up, far_down = call(
        pack_kernel,
        [(2 * wide, hidden)] * 3 + [(wide, hidden)] * 2,
        (targets,),
        up_weight,
        down_weight,
        hbm=2,
        scratch=[pltpu.SemaphoreType.DMA((chips * (wide // LANES + 1),))],
    )
    here, ahead, behind, far_up, far_down, sent = lax.optimization_barrier(
        (here, ahead, behind, far_up, far_down, sent)
    )
    swap = [(0, 1), (1, 0)]
    far_up = lax.ppermute(far_up, "chip", ahead_of)
    far_down = lax.ppermute(far_down, "chip", behind_of)
    ahead = lax.ppermute(ahead, "chip", ahead_of)
    behind = lax.ppermute(behind, "chip", behind_of)
    here_too = lax.ppermute(here, "core", swap)
    scalars = jnp.stack(
        [expert, chip, (chip + chips - 1) % chips, (chip + 1) % chips, (chip + 2) % chips]
    ).astype(jnp.int32)
    scalars = mark(scalars, 10**11, ahead, behind, far_up, far_down)
    ahead, behind, far_up, far_down, scalars = lax.optimization_barrier(
        (ahead, behind, far_up, far_down, scalars)
    )
    far_up = lax.ppermute(far_up, "chip", ahead_of)
    far_down = lax.ppermute(far_down, "chip", behind_of)
    scalars = mark(scalars, 7 * 10**9, far_up, far_down)
    recv = lax.all_to_all(sent, "node", split_axis=0, concat_axis=0, tiled=True)
    near = (here, here_too)
    for block in (ahead, behind):
        near += (block, lax.ppermute(block, "core", swap))
    recv, near, far_up, far_down, scalars = lax.optimization_barrier(
        (recv, near, far_up, far_down, scalars)
    )
    blocks = near + (far_up, far_down)
    for block in (far_up, far_down):
        blocks += (lax.ppermute(block, "core", swap),)
    held = [
        pltpu.VMEM((chips * CORES, 2 * wide, hidden), bf16),
        pltpu.SemaphoreType.DMA((4, chips * CORES, 2)),
    ]
    used = jnp.any(recv[:, 2 * width // LANES, :] > 0, 1)
    rank = jnp.cumsum(used.astype(jnp.int32)) - 1
    slot = jnp.arange(pairs, dtype=jnp.int32)
    pick = ((rank[None, :] == slot[:, None]) & used[None, :]).astype(bf16)
    mine = dot(pick, recv.reshape(nodes, -1), ((1,), (0,))).astype(bf16)
    parts = jnp.stack(
        [
            jnp.concatenate(
                [
                    mine[:, m * wide : (m + 1) * wide],
                    mine[:, width + m * wide : width + (m + 1) * wide],
                    mine[:, 2 * width : 2 * width + LANES],
                ],
                1,
            )
            for m in range(chips)
        ]
    )
    spread = jnp.broadcast_to(parts[None], (experts,) + parts.shape).reshape(
        experts * chips, pairs, -1
    )
    rows = lax.all_to_all(
        spread, ("expert", "chip"), split_axis=0, concat_axis=0, tiled=True
    ).reshape(experts * chips * pairs, -1)
    gate = jnp.sum(
        jnp.where(lane[None, :] == expert, rows[:, 2 * wide :].astype(f32), 0.0), 1, keepdims=True
    )

    units = CORES * hidden
    (outgoing,) = call(
        partial_kernel,
        [(chips, rows.shape[0], 2 * units)],
        (scalars,),
        rows,
        *blocks,
        hbm=len(blocks),
        loose=2,
        scratch=held,
    )
    incoming = lax.all_to_all(outgoing, "chip", split_axis=0, concat_axis=0, tiled=True)
    both = jnp.sum(incoming.astype(f32), 0)
    pre = both[:, :units]
    back = both[:, units:]
    sig = jax.nn.sigmoid(pre)
    active = (pre * sig).astype(bf16)
    grad_pre = (gate * back * sig * (1.0 + pre * (1.0 - sig))).astype(bf16)
    every = lax.all_gather(jnp.concatenate([active, grad_pre], 1), "chip", axis=0)

    (result,) = call(
        output_kernel,
        [rows.shape],
        (scalars,),
        rows,
        every,
        *blocks,
        hbm=len(blocks),
        loose=2,
        scratch=held,
    )

    parts_back = lax.all_to_all(
        result.reshape(experts * chips, pairs, -1),
        ("expert", "chip"),
        split_axis=0,
        concat_axis=0,
        tiled=True,
    ).reshape(experts, chips, pairs, -1)
    summed = jnp.sum(parts_back.astype(f32), 0)
    inner_all = jnp.sum(summed[:, :, 2 * wide :], 0)
    full = jnp.concatenate(
        [summed[m, :, :wide] for m in range(chips)]
        + [summed[m, :, wide : 2 * wide] for m in range(chips)]
        + [inner_all],
        1,
    ).astype(bf16)
    expanded = dot(pick, full, ((0,), (0,))).astype(bf16)
    expanded = jnp.pad(expanded, ((0, 0), (0, 7 * LANES))).reshape(nodes, -1, LANES)
    home = lax.all_to_all(expanded, "node", split_axis=0, concat_axis=0, tiled=True)

    mixed, grad_tokens, grad_gates = call(
        home_kernel,
        [tokens.shape, tokens.shape, choices.shape],
        (),
        home,
        groups,
        choices,
        hbm=2,
        scratch=[*tables, wide_rows, pltpu.SemaphoreType.DMA((2,))],
    )
    return mixed, grad_tokens, grad_gates.transpose(2, 0, 1)


def solution(mesh):
    nodes, members = mesh.devices.shape
    axes = ("node", "expert", "chip", "core")
    fine = Mesh(
        mesh.devices.reshape(nodes, EXPERTS, members // (EXPERTS * CORES), CORES), axes
    )
    placed = (
        P(axes, None),
        P(axes, None),
        P(axes, None),
        P(axes, None, None),
        P(axes, None, None),
        P(None, axes),
        P(axes, None),
    )
    return jax.shard_map(
        per_device,
        mesh=fine,
        in_specs=placed,
        out_specs=(P(axes, None), P(axes, None), P(axes, None, None)),
        check_vma=False,
    )
```

```python
import jax
import jax.numpy as jnp
from jax import lax
from jax.experimental import pallas as pl
from jax.experimental.pallas import tpu as pltpu
from jax.sharding import Mesh, PartitionSpec as P

EXPERTS = 4
CORES = 2
LANES = 128


def dot(a, b, dims):
    return lax.dot_general(a, b, (dims, ((), ())), preferred_element_type=jnp.float32)


def small_copies(pairs, sems):
    copies = [pltpu.make_async_copy(a, b, sems.at[i]) for i, (a, b) in enumerate(pairs)]
    for copy in copies:
        copy.start()
    return copies


def send_kernel(
    gates, groups_at, choices_at, tokens, cotangent, out, groups, choices, narrow, wide, sems
):
    count, width = tokens.shape
    chunks = width // LANES
    first, second, *copies = small_copies(
        [
            (groups_at, groups),
            (choices_at, choices),
            (tokens, narrow.at[0]),
            (cotangent, narrow.at[1]),
        ],
        sems,
    )
    out[...] = jnp.zeros_like(out)
    first.wait()
    second.wait()
    every_gate = gates[...].astype(jnp.float32)
    row = lax.broadcasted_iota(jnp.int32, (8, LANES), 0)
    lane = lax.broadcasted_iota(jnp.int32, (8, LANES), 1)
    i, j = (lax.broadcasted_iota(jnp.int32, (2, count), d) for d in range(2))
    for t in range(count):
        for c in range(2):
            table = jnp.zeros((8, LANES), jnp.float32)
            for k in range(2):
                gate = jnp.sum(jnp.where((i == k) & (j == t), every_gate[c], 0.0), keepdims=True)
                table += jnp.where((row == 0) & (lane == choices[c, k, t]), gate, 0.0)
            out[groups[c, t], 2 * chunks :, :] = table.astype(out.dtype)
    for i, copy in enumerate(copies):
        copy.wait()
        for j in range(chunks):
            wide[:, i * chunks + j, :] = narrow[i, :, j * LANES : (j + 1) * LANES].astype(
                jnp.float32
            )
    for t in range(count):
        rows = wide[t].astype(out.dtype)
        for c in range(2):
            out[groups[c, t], : 2 * chunks, :] = rows


def home_kernel(
    home, groups_at, choices_at, mixed, grad_tokens, grad_gates, groups, choices, wide, sems
):
    count, width = mixed.shape
    chunks = width // LANES
    row = lax.broadcasted_iota(jnp.int32, (8, LANES), 0)
    lane = lax.broadcasted_iota(jnp.int32, (8, LANES), 1)
    i, j = (lax.broadcasted_iota(jnp.int32, (2, count), d) for d in range(2))
    inner = [jnp.zeros((2, count), jnp.float32) for c in range(2)]
    for copy in small_copies([(groups_at, groups), (choices_at, choices)], sems):
        copy.wait()
    for t in range(count):
        total = jnp.zeros((2 * chunks, LANES), jnp.float32)
        for c in range(2):
            node = groups[c, t]
            total += home[node, : 2 * chunks, :].astype(jnp.float32)
            table = home[node, 2 * chunks :, :].astype(jnp.float32)
            for k in range(2):
                value = jnp.sum(
                    jnp.where((row == 0) & (lane == choices[c, k, t]), table, 0.0), keepdims=True
                )
                inner[c] = jnp.where((i == k) & (j == t), value, inner[c])
        wide[t] = total
    for c in range(2):
        grad_gates[c] = inner[c].astype(grad_gates.dtype)
    for j in range(chunks):
        at = pl.ds(j * LANES, LANES)
        mixed[:, at] = wide[:, j, :].astype(mixed.dtype)
        grad_tokens[:, at] = wide[:, chunks + j, :].astype(grad_tokens.dtype)


def pack_kernel(chips, up, down, here, ahead, behind, far_up, far_down, sems):
    wide = far_up.shape[0]
    copies = []

    def rows(chip, out, at):
        start = pl.multiple_of(chips[chip] * wide, wide)
        copies.append(
            pltpu.make_async_copy(
                up.at[pl.ds(start, wide)], out.at[pl.ds(at, wide)], sems.at[len(copies)]
            )
        )

    def columns(chip, out, at):
        start = pl.multiple_of(chips[chip] * wide, wide)
        for j in range(0, wide, LANES):
            copies.append(
                pltpu.make_async_copy(
                    down.at[:, pl.ds(start + j, LANES)],
                    out.at[pl.ds(at + j, LANES)],
                    sems.at[len(copies)],
                )
            )

    for chip, out in ((1, ahead), (3, behind), (0, here)):
        rows(chip, out, 0)
        columns(chip, out, wide)
    rows(2, far_up, 0)
    columns(2, far_down, 0)
    for copy in copies:
        copy.start()
    for copy in copies:
        copy.wait()


def fetch(refs, held, sems, cuts):
    wide = held.shape[1] // 2
    halves = [(ref.at[pl.ds(0, wide)], ref.at[pl.ds(wide, wide)]) for ref in refs[:-4]]
    halves += [(refs[-4], refs[-3]), (refs[-2], refs[-1])]
    found = []
    for k, (low, high) in enumerate(zip((0,) + cuts, cuts + (wide,))):
        at = pl.ds(low, high - low)
        found.append(
            [
                [
                    pltpu.make_async_copy(
                        ref.at[at],
                        held.at[i, pl.ds(half * wide + low, high - low)],
                        sems.at[k, i, half],
                    )
                    for half, ref in enumerate(pair)
                ]
                for i, pair in enumerate(halves)
            ]
        )
    return found


def arrivals(groups):
    for group in groups:
        for copy in group:
            copy.start()
    for group in groups:
        for copy in group:
            copy.wait()
        yield


def flat(lists):
    return [item for items in lists for item in items]


def mark_kernel(scalars, *refs):
    for i in range(scalars.shape[0]):
        refs[-1][i] = scalars[i]


def mark(scalars, flops, *arrays):
    small = pl.BlockSpec(memory_space=pltpu.SMEM)
    return pl.pallas_call(
        mark_kernel,
        out_shape=jax.ShapeDtypeStruct(scalars.shape, scalars.dtype),
        in_specs=[small] + [pl.BlockSpec(memory_space=pl.ANY)] * len(arrays),
        out_specs=small,
        cost_estimate=pl.CostEstimate(flops=flops, bytes_accessed=4096, transcendentals=0),
    )(scalars, *arrays)


def partial_kernel(scalars, rows, *refs):
    *blocks, out, held, sems = refs
    count, _, hidden = held.shape
    wide = held.shape[1] // 2
    (copies,) = fetch(blocks, held, sems, ())
    arrived = arrivals([flat(copies[i : i + CORES]) for i in range(0, count, CORES)])
    x, dy = rows[:, :wide], rows[:, wide : 2 * wide]
    for i in range(count // CORES):
        pair = range(CORES * i, CORES * (i + 1))
        next(arrived)
        at = scalars[1 + i]
        up = jnp.concatenate([held[m, :wide, :] for m in pair], 1)
        out[at, :, : CORES * hidden] = dot(x, up, ((1,), (0,))).astype(out.dtype)
        down = jnp.concatenate(
            [
                jnp.concatenate([held[m, wide + j : wide + j + LANES, :] for m in pair], 0)
                for j in range(0, wide, LANES)
            ],
            1,
        )
        out[at, :, CORES * hidden :] = dot(dy, down, ((1,), (1,))).astype(out.dtype)


def output_kernel(scalars, rows, every, *refs):
    *blocks, result, held, sems = refs
    many, _, hidden = held.shape
    wide = held.shape[1] // 2
    step = 2 * LANES
    cuts = tuple(range(2 * step, wide, 2 * step))
    arrived = arrivals([flat(cut) for cut in fetch(blocks, held, sems, cuts)])
    chips = many // CORES
    count = rows.shape[0]
    lane = lax.broadcasted_iota(jnp.int32, (count, LANES), 1)
    mine = lane == scalars[0]
    gate = jnp.sum(
        jnp.where(mine, rows[:, 2 * wide :].astype(jnp.float32), 0.0), 1, keepdims=True
    )
    active = jnp.concatenate(
        [every[scalars[1 + i], :, : CORES * hidden] for i in range(chips)], 1
    )
    grad_pre = jnp.concatenate(
        [every[scalars[1 + i], :, CORES * hidden :] for i in range(chips)], 1
    )
    inner = jnp.zeros((count, 1), jnp.float32)
    for j in range(0, wide, step):
        if j == 0 or j in cuts:
            next(arrived)
        down = jnp.concatenate(
            [
                jnp.concatenate(
                    [held[m, wide + j + k : wide + j + k + LANES, :] for m in range(many)], 0
                )
                for k in range(0, step, LANES)
            ],
            1,
        )
        up = jnp.concatenate([held[m, j : j + step, :] for m in range(many)], 1)
        out = dot(active, down, ((1,), (0,)))
        inner += jnp.sum(
            out * rows[:, wide + j : wide + j + step].astype(jnp.float32), 1, keepdims=True
        )
        result[:, j : j + step] = (gate * out).astype(result.dtype)
        result[:, wide + j : wide + j + step] = dot(grad_pre, up, ((1,), (1,))).astype(
            result.dtype
        )
    inner = jnp.where(gate > 0, inner, 0.0)
    result[:, 2 * wide :] = jnp.where(mine, inner, 0.0).astype(result.dtype)


def call(kernel, shapes, scalars, *operands, hbm=0, scratch=(), loose=0):
    small, near, far = (
        pl.BlockSpec(memory_space=space) for space in (pltpu.SMEM, pltpu.VMEM, pltpu.HBM)
    )
    count = len(operands) - hbm
    fixed = len(operands) - loose
    held = [pltpu.with_memory_space_constraint(v, pltpu.HBM) for v in operands[count:fixed]]
    held += operands[fixed:]
    anywhere = pl.BlockSpec(memory_space=pl.ANY)
    return pl.pallas_call(
        kernel,
        out_shape=[jax.ShapeDtypeStruct(shape, jnp.bfloat16) for shape in shapes],
        in_specs=[small] * len(scalars) + [near] * count + [far] * (hbm - loose) + [anywhere] * loose,
        out_specs=[near] * len(shapes),
        scratch_shapes=scratch,
        compiler_params=pltpu.CompilerParams(vmem_limit_bytes=24 * 2**20),
    )(*scalars, *operands[:count], *held)


def per_device(tokens, cotangent, groups, choices, gates, up_weight, down_weight):
    f32, bf16 = jnp.float32, jnp.bfloat16
    tok_count, width = tokens.shape
    nodes = lax.axis_size("node")
    experts = lax.axis_size("expert")
    chips = lax.axis_size("chip")
    hidden = up_weight.shape[1]
    pairs = 2 * tok_count
    wide = width // chips
    expert = lax.axis_index("expert")
    chip = lax.axis_index("chip")
    lane = jnp.arange(LANES, dtype=jnp.int32)

    slot_rows = 2 * width // LANES
    groups, choices = groups.T, choices.transpose(1, 2, 0)
    tables = [pltpu.SMEM(v.shape, jnp.int32) for v in (groups, choices)]
    wide_rows = pltpu.VMEM((tok_count, slot_rows, LANES), f32)
    (sent,) = call(
        send_kernel,
        [(nodes, slot_rows + 8, LANES)],
        (),
        gates.transpose(1, 2, 0),
        groups,
        choices,
        tokens,
        cotangent,
        hbm=4,
        scratch=[
            *tables,
            pltpu.VMEM((2,) + tokens.shape, bf16),
            wide_rows,
            pltpu.SemaphoreType.DMA((4,)),
        ],
    )

    ahead_of = [(i, (i + 1) % chips) for i in range(chips)]
    behind_of = [(i, (i - 1) % chips) for i in range(chips)]
    targets = jnp.stack([(chip + s) % chips for s in range(chips)]).astype(jnp.int32)
    here, ahead, behind, far_up, far_down = call(
        pack_kernel,
        [(2 * wide, hidden)] * 3 + [(wide, hidden)] * 2,
        (targets,),
        up_weight,
        down_weight,
        hbm=2,
        scratch=[pltpu.SemaphoreType.DMA((chips * (wide // LANES + 1),))],
    )
    here, ahead, behind, far_up, far_down, sent = lax.optimization_barrier(
        (here, ahead, behind, far_up, far_down, sent)
    )
    swap = [(0, 1), (1, 0)]
    far_up = lax.ppermute(far_up, "chip", ahead_of)
    far_down = lax.ppermute(far_down, "chip", behind_of)
    ahead = lax.ppermute(ahead, "chip", ahead_of)
    behind = lax.ppermute(behind, "chip", behind_of)
    here_too = lax.ppermute(here, "core", swap)
    scalars = jnp.stack(
        [expert, chip, (chip + chips - 1) % chips, (chip + 1) % chips, (chip + 2) % chips]
    ).astype(jnp.int32)
    scalars = mark(scalars, 10**11, ahead, behind, far_up, far_down)
    ahead, behind, far_up, far_down, scalars = lax.optimization_barrier(
        (ahead, behind, far_up, far_down, scalars)
    )
    far_up = lax.ppermute(far_up, "chip", ahead_of)
    far_down = lax.ppermute(far_down, "chip", behind_of)
    scalars = mark(scalars, 7 * 10**9, far_up, far_down)
    recv = lax.all_to_all(sent, "node", split_axis=0, concat_axis=0, tiled=True)
    held = [
        pltpu.VMEM((chips * CORES, 2 * wide, hidden), bf16),
        pltpu.SemaphoreType.DMA((4, chips * CORES, 2)),
    ]
    used = jnp.any(recv[:, 2 * width // LANES, :] > 0, 1)
    rank = jnp.cumsum(used.astype(jnp.int32)) - 1
    slot = jnp.arange(pairs, dtype=jnp.int32)
    pick = ((rank[None, :] == slot[:, None]) & used[None, :]).astype(bf16)
    mine = dot(pick, recv.reshape(nodes, -1), ((1,), (0,))).astype(bf16)
    parts = jnp.stack(
        [
            jnp.concatenate(
                [
                    mine[:, m * wide : (m + 1) * wide],
                    mine[:, width + m * wide : width + (m + 1) * wide],
                    mine[:, 2 * width : 2 * width + LANES],
                ],
                1,
            )
            for m in range(chips)
        ]
    )
    spread = jnp.broadcast_to(parts[None], (experts,) + parts.shape).reshape(
        experts * chips, pairs, -1
    )
    near = (here, here_too)
    for block in (ahead, behind):
        near += (block, lax.ppermute(block, "core", swap))
    spread, near, far_up, far_down, scalars = lax.optimization_barrier(
        (spread, near, far_up, far_down, scalars)
    )
    blocks = near + (far_up, far_down)
    for block in (far_up, far_down):
        blocks += (lax.ppermute(block, "core", swap),)
    rows = lax.all_to_all(
        spread, ("expert", "chip"), split_axis=0, concat_axis=0, tiled=True
    ).reshape(experts * chips * pairs, -1)
    gate = jnp.sum(
        jnp.where(lane[None, :] == expert, rows[:, 2 * wide :].astype(f32), 0.0), 1, keepdims=True
    )

    units = CORES * hidden
    (outgoing,) = call(
        partial_kernel,
        [(chips, rows.shape[0], 2 * units)],
        (scalars,),
        rows,
        *blocks,
        hbm=len(blocks),
        loose=2,
        scratch=held,
    )
    incoming = lax.all_to_all(outgoing, "chip", split_axis=0, concat_axis=0, tiled=True)
    both = jnp.sum(incoming.astype(f32), 0)
    pre = both[:, :units]
    back = both[:, units:]
    sig = jax.nn.sigmoid(pre)
    active = (pre * sig).astype(bf16)
    grad_pre = (gate * back * sig * (1.0 + pre * (1.0 - sig))).astype(bf16)
    every = lax.all_gather(jnp.concatenate([active, grad_pre], 1), "chip", axis=0)

    (result,) = call(
        output_kernel,
        [rows.shape],
        (scalars,),
        rows,
        every,
        *blocks,
        hbm=len(blocks),
        loose=2,
        scratch=held,
    )

    parts_back = lax.all_to_all(
        result.reshape(experts * chips, pairs, -1),
        ("expert", "chip"),
        split_axis=0,
        concat_axis=0,
        tiled=True,
    ).reshape(experts, chips, pairs, -1)
    summed = jnp.sum(parts_back.astype(f32), 0)
    inner_all = jnp.sum(summed[:, :, 2 * wide :], 0)
    full = jnp.concatenate(
        [summed[m, :, :wide] for m in range(chips)]
        + [summed[m, :, wide : 2 * wide] for m in range(chips)]
        + [inner_all],
        1,
    ).astype(bf16)
    expanded = dot(pick, full, ((0,), (0,))).astype(bf16)
    expanded = jnp.pad(expanded, ((0, 0), (0, 7 * LANES))).reshape(nodes, -1, LANES)
    home = lax.all_to_all(expanded, "node", split_axis=0, concat_axis=0, tiled=True)

    mixed, grad_tokens, grad_gates = call(
        home_kernel,
        [tokens.shape, tokens.shape, choices.shape],
        (),
        home,
        groups,
        choices,
        hbm=2,
        scratch=[*tables, wide_rows, pltpu.SemaphoreType.DMA((2,))],
    )
    return mixed, grad_tokens, grad_gates.transpose(2, 0, 1)


def solution(mesh):
    nodes, members = mesh.devices.shape
    axes = ("node", "expert", "chip", "core")
    fine = Mesh(
        mesh.devices.reshape(nodes, EXPERTS, members // (EXPERTS * CORES), CORES), axes
    )
    placed = (
        P(axes, None),
        P(axes, None),
        P(axes, None),
        P(axes, None, None),
        P(axes, None, None),
        P(None, axes),
        P(axes, None),
    )
    return jax.shard_map(
        per_device,
        mesh=fine,
        in_specs=placed,
        out_specs=(P(axes, None), P(axes, None), P(axes, None, None)),
        check_vma=False,
    )
```

```python
import jax
import jax.numpy as jnp
from jax import lax
from jax.experimental import pallas as pl
from jax.experimental.pallas import tpu as pltpu
from jax.sharding import Mesh, PartitionSpec as P

EXPERTS = 4
CORES = 2
LANES = 128


def dot(a, b, dims):
    return lax.dot_general(a, b, (dims, ((), ())), preferred_element_type=jnp.float32)


def small_copies(pairs, sems):
    copies = [pltpu.make_async_copy(a, b, sems.at[i]) for i, (a, b) in enumerate(pairs)]
    for copy in copies:
        copy.start()
    return copies


def send_kernel(
    gates, groups_at, choices_at, tokens, cotangent, out, groups, choices, narrow, wide, sems
):
    count, width = tokens.shape
    chunks = width // LANES
    first, second, *copies = small_copies(
        [
            (groups_at, groups),
            (choices_at, choices),
            (tokens, narrow.at[0]),
            (cotangent, narrow.at[1]),
        ],
        sems,
    )
    out[...] = jnp.zeros_like(out)
    first.wait()
    second.wait()
    every_gate = gates[...].astype(jnp.float32)
    row = lax.broadcasted_iota(jnp.int32, (8, LANES), 0)
    lane = lax.broadcasted_iota(jnp.int32, (8, LANES), 1)
    i, j = (lax.broadcasted_iota(jnp.int32, (2, count), d) for d in range(2))
    for t in range(count):
        for c in range(2):
            table = jnp.zeros((8, LANES), jnp.float32)
            for k in range(2):
                gate = jnp.sum(jnp.where((i == k) & (j == t), every_gate[c], 0.0), keepdims=True)
                table += jnp.where((row == 0) & (lane == choices[c, k, t]), gate, 0.0)
            out[groups[c, t], 2 * chunks :, :] = table.astype(out.dtype)
    for i, copy in enumerate(copies):
        copy.wait()
        for j in range(chunks):
            wide[:, i * chunks + j, :] = narrow[i, :, j * LANES : (j + 1) * LANES].astype(
                jnp.float32
            )
    for t in range(count):
        rows = wide[t].astype(out.dtype)
        for c in range(2):
            out[groups[c, t], : 2 * chunks, :] = rows


def home_kernel(
    home, groups_at, choices_at, mixed, grad_tokens, grad_gates, groups, choices, wide, sems
):
    count, width = mixed.shape
    chunks = width // LANES
    row = lax.broadcasted_iota(jnp.int32, (8, LANES), 0)
    lane = lax.broadcasted_iota(jnp.int32, (8, LANES), 1)
    i, j = (lax.broadcasted_iota(jnp.int32, (2, count), d) for d in range(2))
    inner = [jnp.zeros((2, count), jnp.float32) for c in range(2)]
    for copy in small_copies([(groups_at, groups), (choices_at, choices)], sems):
        copy.wait()
    for t in range(count):
        total = jnp.zeros((2 * chunks, LANES), jnp.float32)
        for c in range(2):
            node = groups[c, t]
            total += home[node, : 2 * chunks, :].astype(jnp.float32)
            table = home[node, 2 * chunks :, :].astype(jnp.float32)
            for k in range(2):
                value = jnp.sum(
                    jnp.where((row == 0) & (lane == choices[c, k, t]), table, 0.0), keepdims=True
                )
                inner[c] = jnp.where((i == k) & (j == t), value, inner[c])
        wide[t] = total
    for c in range(2):
        grad_gates[c] = inner[c].astype(grad_gates.dtype)
    for j in range(chunks):
        at = pl.ds(j * LANES, LANES)
        mixed[:, at] = wide[:, j, :].astype(mixed.dtype)
        grad_tokens[:, at] = wide[:, chunks + j, :].astype(grad_tokens.dtype)


def pack_kernel(chips, up, down, here, ahead, behind, far_up, far_down, sems):
    wide = far_up.shape[0]
    copies = []

    def rows(chip, out, at):
        start = pl.multiple_of(chips[chip] * wide, wide)
        copies.append(
            pltpu.make_async_copy(
                up.at[pl.ds(start, wide)], out.at[pl.ds(at, wide)], sems.at[len(copies)]
            )
        )

    def columns(chip, out, at):
        start = pl.multiple_of(chips[chip] * wide, wide)
        for j in range(0, wide, LANES):
            copies.append(
                pltpu.make_async_copy(
                    down.at[:, pl.ds(start + j, LANES)],
                    out.at[pl.ds(at + j, LANES)],
                    sems.at[len(copies)],
                )
            )

    for chip, out in ((1, ahead), (3, behind), (0, here)):
        rows(chip, out, 0)
        columns(chip, out, wide)
    rows(2, far_up, 0)
    columns(2, far_down, 0)
    for copy in copies:
        copy.start()
    for copy in copies:
        copy.wait()


def fetch(refs, held, sems, cuts):
    wide = held.shape[1] // 2
    halves = [(ref.at[pl.ds(0, wide)], ref.at[pl.ds(wide, wide)]) for ref in refs[:-4]]
    halves += [(refs[-4], refs[-3]), (refs[-2], refs[-1])]
    found = []
    for k, (low, high) in enumerate(zip((0,) + cuts, cuts + (wide,))):
        at = pl.ds(low, high - low)
        found.append(
            [
                [
                    pltpu.make_async_copy(
                        ref.at[at],
                        held.at[i, pl.ds(half * wide + low, high - low)],
                        sems.at[k, i, half],
                    )
                    for half, ref in enumerate(pair)
                ]
                for i, pair in enumerate(halves)
            ]
        )
    return found


def arrivals(groups):
    for group in groups:
        for copy in group:
            copy.start()
    for group in groups:
        for copy in group:
            copy.wait()
        yield


def flat(lists):
    return [item for items in lists for item in items]


def mark_kernel(*refs):
    pass


def mark(scalars, flops, *arrays):
    spec = pl.BlockSpec(memory_space=pl.ANY)
    return pl.pallas_call(
        mark_kernel,
        out_shape=jax.ShapeDtypeStruct(scalars.shape, scalars.dtype),
        in_specs=[spec] * (1 + len(arrays)),
        out_specs=spec,
        input_output_aliases={0: 0},
        cost_estimate=pl.CostEstimate(flops=flops, bytes_accessed=4096, transcendentals=0),
    )(scalars, *arrays)


def partial_kernel(scalars, rows, *refs):
    *blocks, out, held, sems = refs
    count, _, hidden = held.shape
    wide = held.shape[1] // 2
    (copies,) = fetch(blocks, held, sems, ())
    arrived = arrivals([flat(copies[i : i + CORES]) for i in range(0, count, CORES)])
    x, dy = rows[:, :wide], rows[:, wide : 2 * wide]
    for i in range(count // CORES):
        pair = range(CORES * i, CORES * (i + 1))
        next(arrived)
        at = scalars[1 + i]
        up = jnp.concatenate([held[m, :wide, :] for m in pair], 1)
        out[at, :, : CORES * hidden] = dot(x, up, ((1,), (0,))).astype(out.dtype)
        down = jnp.concatenate(
            [
                jnp.concatenate([held[m, wide + j : wide + j + LANES, :] for m in pair], 0)
                for j in range(0, wide, LANES)
            ],
            1,
        )
        out[at, :, CORES * hidden :] = dot(dy, down, ((1,), (1,))).astype(out.dtype)


def output_kernel(scalars, rows, every, *refs):
    *blocks, result, held, sems = refs
    many, _, hidden = held.shape
    wide = held.shape[1] // 2
    step = 2 * LANES
    cuts = tuple(range(2 * step, wide, 2 * step))
    arrived = arrivals([flat(cut) for cut in fetch(blocks, held, sems, cuts)])
    chips = many // CORES
    count = rows.shape[0]
    lane = lax.broadcasted_iota(jnp.int32, (count, LANES), 1)
    mine = lane == scalars[0]
    gate = jnp.sum(
        jnp.where(mine, rows[:, 2 * wide :].astype(jnp.float32), 0.0), 1, keepdims=True
    )
    active = jnp.concatenate(
        [every[scalars[1 + i], :, : CORES * hidden] for i in range(chips)], 1
    )
    grad_pre = jnp.concatenate(
        [every[scalars[1 + i], :, CORES * hidden :] for i in range(chips)], 1
    )
    inner = jnp.zeros((count, 1), jnp.float32)
    for j in range(0, wide, step):
        if j == 0 or j in cuts:
            next(arrived)
        down = jnp.concatenate(
            [
                jnp.concatenate(
                    [held[m, wide + j + k : wide + j + k + LANES, :] for m in range(many)], 0
                )
                for k in range(0, step, LANES)
            ],
            1,
        )
        up = jnp.concatenate([held[m, j : j + step, :] for m in range(many)], 1)
        out = dot(active, down, ((1,), (0,)))
        inner += jnp.sum(
            out * rows[:, wide + j : wide + j + step].astype(jnp.float32), 1, keepdims=True
        )
        result[:, j : j + step] = (gate * out).astype(result.dtype)
        result[:, wide + j : wide + j + step] = dot(grad_pre, up, ((1,), (1,))).astype(
            result.dtype
        )
    inner = jnp.where(gate > 0, inner, 0.0)
    result[:, 2 * wide :] = jnp.where(mine, inner, 0.0).astype(result.dtype)


def call(kernel, shapes, scalars, *operands, hbm=0, scratch=(), loose=0):
    small, near, far = (
        pl.BlockSpec(memory_space=space) for space in (pltpu.SMEM, pltpu.VMEM, pltpu.HBM)
    )
    count = len(operands) - hbm
    fixed = len(operands) - loose
    held = [pltpu.with_memory_space_constraint(v, pltpu.HBM) for v in operands[count:fixed]]
    held += operands[fixed:]
    anywhere = pl.BlockSpec(memory_space=pl.ANY)
    return pl.pallas_call(
        kernel,
        out_shape=[jax.ShapeDtypeStruct(shape, jnp.bfloat16) for shape in shapes],
        in_specs=[small] * len(scalars) + [near] * count + [far] * (hbm - loose) + [anywhere] * loose,
        out_specs=[near] * len(shapes),
        scratch_shapes=scratch,
        compiler_params=pltpu.CompilerParams(vmem_limit_bytes=24 * 2**20),
    )(*scalars, *operands[:count], *held)


def per_device(tokens, cotangent, groups, choices, gates, up_weight, down_weight):
    f32, bf16 = jnp.float32, jnp.bfloat16
    tok_count, width = tokens.shape
    nodes = lax.axis_size("node")
    experts = lax.axis_size("expert")
    chips = lax.axis_size("chip")
    hidden = up_weight.shape[1]
    pairs = 2 * tok_count
    wide = width // chips
    expert = lax.axis_index("expert")
    chip = lax.axis_index("chip")
    lane = jnp.arange(LANES, dtype=jnp.int32)

    slot_rows = 2 * width // LANES
    groups, choices = groups.T, choices.transpose(1, 2, 0)
    tables = [pltpu.SMEM(v.shape, jnp.int32) for v in (groups, choices)]
    wide_rows = pltpu.VMEM((tok_count, slot_rows, LANES), f32)
    (sent,) = call(
        send_kernel,
        [(nodes, slot_rows + 8, LANES)],
        (),
        gates.transpose(1, 2, 0),
        groups,
        choices,
        tokens,
        cotangent,
        hbm=4,
        scratch=[
            *tables,
            pltpu.VMEM((2,) + tokens.shape, bf16),
            wide_rows,
            pltpu.SemaphoreType.DMA((4,)),
        ],
    )

    ahead_of = [(i, (i + 1) % chips) for i in range(chips)]
    behind_of = [(i, (i - 1) % chips) for i in range(chips)]
    targets = jnp.stack([(chip + s) % chips for s in range(chips)]).astype(jnp.int32)
    here, ahead, behind, far_up, far_down = call(
        pack_kernel,
        [(2 * wide, hidden)] * 3 + [(wide, hidden)] * 2,
        (targets,),
        up_weight,
        down_weight,
        hbm=2,
        scratch=[pltpu.SemaphoreType.DMA((chips * (wide // LANES + 1),))],
    )
    here, ahead, behind, far_up, far_down, sent = lax.optimization_barrier(
        (here, ahead, behind, far_up, far_down, sent)
    )
    swap = [(0, 1), (1, 0)]
    far_up = lax.ppermute(far_up, "chip", ahead_of)
    far_down = lax.ppermute(far_down, "chip", behind_of)
    ahead = lax.ppermute(ahead, "chip", ahead_of)
    behind = lax.ppermute(behind, "chip", behind_of)
    here_too = lax.ppermute(here, "core", swap)
    scalars = jnp.stack(
        [expert, chip, (chip + chips - 1) % chips, (chip + 1) % chips, (chip + 2) % chips]
    ).astype(jnp.int32)
    scalars = mark(scalars, 10**11, ahead, behind, far_up, far_down)
    ahead, behind, far_up, far_down, scalars = lax.optimization_barrier(
        (ahead, behind, far_up, far_down, scalars)
    )
    far_up = lax.ppermute(far_up, "chip", ahead_of)
    far_down = lax.ppermute(far_down, "chip", behind_of)
    scalars = mark(scalars, 7 * 10**9, far_up, far_down)
    recv = lax.all_to_all(sent, "node", split_axis=0, concat_axis=0, tiled=True)
    near = (here, here_too)
    for block in (ahead, behind):
        near += (block, lax.ppermute(block, "core", swap))
    recv, near, far_up, far_down, scalars = lax.optimization_barrier(
        (recv, near, far_up, far_down, scalars)
    )
    blocks = near + (far_up, far_down)
    for block in (far_up, far_down):
        blocks += (lax.ppermute(block, "core", swap),)
    held = [
        pltpu.VMEM((chips * CORES, 2 * wide, hidden), bf16),
        pltpu.SemaphoreType.DMA((4, chips * CORES, 2)),
    ]
    used = jnp.any(recv[:, 2 * width // LANES, :] > 0, 1)
    rank = jnp.cumsum(used.astype(jnp.int32)) - 1
    slot = jnp.arange(pairs, dtype=jnp.int32)
    pick = ((rank[None, :] == slot[:, None]) & used[None, :]).astype(bf16)
    mine = dot(pick, recv.reshape(nodes, -1), ((1,), (0,))).astype(bf16)
    parts = jnp.stack(
        [
            jnp.concatenate(
                [
                    mine[:, m * wide : (m + 1) * wide],
                    mine[:, width + m * wide : width + (m + 1) * wide],
                    mine[:, 2 * width : 2 * width + LANES],
                ],
                1,
            )
            for m in range(chips)
        ]
    )
    spread = jnp.broadcast_to(parts[None], (experts,) + parts.shape).reshape(
        experts * chips, pairs, -1
    )
    rows = lax.all_to_all(
        spread, ("expert", "chip"), split_axis=0, concat_axis=0, tiled=True
    ).reshape(experts * chips * pairs, -1)
    gate = jnp.sum(
        jnp.where(lane[None, :] == expert, rows[:, 2 * wide :].astype(f32), 0.0), 1, keepdims=True
    )

    units = CORES * hidden
    (outgoing,) = call(
        partial_kernel,
        [(chips, rows.shape[0], 2 * units)],
        (scalars,),
        rows,
        *blocks,
        hbm=len(blocks),
        loose=2,
        scratch=held,
    )
    incoming = lax.all_to_all(outgoing, "chip", split_axis=0, concat_axis=0, tiled=True)
    both = jnp.sum(incoming.astype(f32), 0)
    pre = both[:, :units]
    back = both[:, units:]
    sig = jax.nn.sigmoid(pre)
    active = (pre * sig).astype(bf16)
    grad_pre = (gate * back * sig * (1.0 + pre * (1.0 - sig))).astype(bf16)
    every = lax.all_gather(jnp.concatenate([active, grad_pre], 1), "chip", axis=0)

    (result,) = call(
        output_kernel,
        [rows.shape],
        (scalars,),
        rows,
        every,
        *blocks,
        hbm=len(blocks),
        loose=2,
        scratch=held,
    )

    parts_back = lax.all_to_all(
        result.reshape(experts * chips, pairs, -1),
        ("expert", "chip"),
        split_axis=0,
        concat_axis=0,
        tiled=True,
    ).reshape(experts, chips, pairs, -1)
    summed = jnp.sum(parts_back.astype(f32), 0)
    inner_all = jnp.sum(summed[:, :, 2 * wide :], 0)
    full = jnp.concatenate(
        [summed[m, :, :wide] for m in range(chips)]
        + [summed[m, :, wide : 2 * wide] for m in range(chips)]
        + [inner_all],
        1,
    ).astype(bf16)
    expanded = dot(pick, full, ((0,), (0,))).astype(bf16)
    expanded = jnp.pad(expanded, ((0, 0), (0, 7 * LANES))).reshape(nodes, -1, LANES)
    home = lax.all_to_all(expanded, "node", split_axis=0, concat_axis=0, tiled=True)

    mixed, grad_tokens, grad_gates = call(
        home_kernel,
        [tokens.shape, tokens.shape, choices.shape],
        (),
        home,
        groups,
        choices,
        hbm=2,
        scratch=[*tables, wide_rows, pltpu.SemaphoreType.DMA((2,))],
    )
    return mixed, grad_tokens, grad_gates.transpose(2, 0, 1)


def solution(mesh):
    nodes, members = mesh.devices.shape
    axes = ("node", "expert", "chip", "core")
    fine = Mesh(
        mesh.devices.reshape(nodes, EXPERTS, members // (EXPERTS * CORES), CORES), axes
    )
    placed = (
        P(axes, None),
        P(axes, None),
        P(axes, None),
        P(axes, None, None),
        P(axes, None, None),
        P(None, axes),
        P(axes, None),
    )
    return jax.shard_map(
        per_device,
        mesh=fine,
        in_specs=placed,
        out_specs=(P(axes, None), P(axes, None), P(axes, None, None)),
        check_vma=False,
    )
```
